32 devices in a mesh: dp: 4 (over y, core), blk: 8 (over z, x).
Axes of the slice: x: 2, y: 2, z: 4, core: 2. Of those that a mesh axis runs over, the one named last changes fastest.
Arguments:
- features: float32 [4, 16384, 128], P('dp', 'blk'), may hold values from -14 to 14
- func_points: float32 [4, 3, 4096, 128], P('dp', None, 'blk'), may hold values from -14 to 14
- coords: float32 [4, 2, 16384], P('dp', None, 'blk'), may hold values from -1 to 1
- presence: int32 [4, 3], P('dp'), may hold values from 0 to 1, as said below
- valid_rows: int32 [4, 3, 8], P('dp'), may hold values from 1 to 512, as said below
- norm_gain: float32 [2, 3, 128], replicated, may hold values from 0.25 to 1.75
- in_proj: float32 [2, 2, 3, 128, 128], replicated, may hold values from -1 to 1
- out_proj: float32 [2, 2, 128, 128], replicated, may hold values from -1.5 to 1.5
- router: float32 [2, 2, 4], replicated, may hold values from -4 to 4
- expert_up: float32 [2, 4, 128, 256], replicated, may hold values from -0.5 to 0.5
- expert_down: float32 [2, 4, 256, 128], replicated, may hold values from -0.375 to 0.375
- cotangent: float32 [4, 16384, 128], P('dp', 'blk'), may hold values from -6 to 6
Outputs:
- layer_output: float32 [4, 16384, 128], P('dp', 'blk')
- features_grad: float32 [4, 16384, 128], P('dp', 'blk')
- gain_grad: float32 [2, 3, 128], replicated
- in_proj_grad: float32 [2, 2, 3, 128, 128], replicated
- out_proj_grad: float32 [2, 2, 128, 128], replicated
- router_grad: float32 [2, 2, 4], replicated
- up_grad: float32 [2, 4, 128, 256], replicated
- down_grad: float32 [2, 4, 256, 128], replicated
The draws below stay inside these ranges and needn't reach their ends.
Inputs may be any that keep to these rules, and one draw needn't show every extreme that they name: `presence`: every mesh has one function or more. `valid_rows`: the valid points of a block are its first slots; every block has one or more; each function of each mesh has a block of 512 valid points.
All inputs are finite; a program needn't handle non-finite values.
Results may differ from the reference program's by a relative error of at most 0.0003.
Values sent between devices are 32-bit elements; how exact they have to be, the bound alone decides.
A program may use at most 192 MiB of HBM per device.

```python
import jax
import jax.numpy as jnp
from jax import lax

D = 128
HEADS = 8
HID = 256
EXPERTS = 4
FUNCS = 3
LAYERS = 2
QPTS_DEV = 2048
FPTS_DEV = 512
MESHES = 4
NPTS = 16384
FPTS = 4096


def draw_features(key, part):
    key = jax.random.fold_in(key, 11)
    first, second = jax.random.split(key)
    blocks = NPTS // QPTS_DEV
    noise = jax.random.normal(first, (MESHES, blocks, QPTS_DEV, D), jnp.float32)
    spread = 1.5
    offsets = spread * jax.random.normal(second, (MESHES, blocks, 1, D), jnp.float32)
    return jnp.clip(noise + offsets, -14.0, 14.0).reshape(MESHES, NPTS, D)


def draw_func_points(key, part):
    key = jax.random.fold_in(key, 23)
    first, second = jax.random.split(key)
    blocks = FPTS // FPTS_DEV
    noise = jax.random.normal(first, (MESHES, FUNCS, blocks, FPTS_DEV, D), jnp.float32)
    spread = 1.5
    offsets = spread * jax.random.normal(second, (MESHES, FUNCS, blocks, 1, D), jnp.float32)
    return jnp.clip(noise + offsets, -14.0, 14.0).reshape(MESHES, FUNCS, FPTS, D)


def draw_presence(key, part):
    key = jax.random.fold_in(key, 37)
    first, second = jax.random.split(key)
    coins = jax.random.randint(first, (MESHES, FUNCS), 0, 2, jnp.int32)
    chosen = jax.random.randint(second, (MESHES,), 0, FUNCS, jnp.int32)
    forced = (jnp.arange(FUNCS, dtype=jnp.int32)[None, :] == chosen[:, None]).astype(jnp.int32)
    return jnp.maximum(coins, forced)


def draw_valid_rows(key, part):
    key = jax.random.fold_in(key, 41)
    first, second = jax.random.split(key)
    blocks = FPTS // FPTS_DEV
    lowest = max(FPTS_DEV // 4, 1)
    counts = jax.random.randint(first, (MESHES, FUNCS, blocks), lowest, FPTS_DEV + 1, jnp.int32)
    full_at = jax.random.randint(second, (MESHES, FUNCS), 0, blocks, jnp.int32)
    is_full = jnp.arange(blocks, dtype=jnp.int32)[None, None, :] == full_at[:, :, None]
    return jnp.where(is_full, FPTS_DEV, counts).astype(jnp.int32)


def shard_levels(key, shape, pieces, least, high):
    def one(axis_at, shards_of):
        draws = jax.random.uniform(jax.random.fold_in(jax.random.fold_in(key, 6), axis_at), (shards_of,), jnp.float32, least / len(pieces), high / len(pieces))
        return jnp.repeat(jnp.exp(draws), shape[axis_at] // shards_of).reshape((-1,) + (1,) * (len(shape) - axis_at - 1))

    factor_of = one(*pieces[0])
    for cut in pieces[1:]:
        factor_of = factor_of * one(*cut)
    return factor_of


def scatter_about(key, shape, scale, bound, pieces=(), kind=jnp.bfloat16):
    gain = shard_levels(key, shape, pieces, -0.22, 0.18) if pieces else 1.0
    drawn = jax.random.normal(key, shape, jnp.float32) * scale * gain
    return jnp.minimum(jnp.maximum(drawn, -bound), bound).astype(kind)


def setup_inputs(seed: int = 0) -> dict:
    key_of = jax.random.split(jax.random.key(seed), 13)
    return {
        "features": draw_features(jax.random.fold_in(key_of[12], 71), 0),
        "func_points": draw_func_points(jax.random.fold_in(key_of[12], 71), 0),
        "coords": jnp.clip(jax.random.uniform(key_of[2], (MESHES, 2, NPTS), jnp.float32, -1.0, 1.0) * shard_levels(key_of[2], (MESHES, 2, NPTS), ((0, 4), (2, 8)), -0.4, 0.0), -1.0, 1.0),
        "presence": draw_presence(jax.random.fold_in(key_of[12], 71), 0),
        "valid_rows": draw_valid_rows(jax.random.fold_in(key_of[12], 71), 0),
        "norm_gain": jnp.clip(1.0 + 0.15 * jax.random.normal(key_of[5], (LAYERS, 3, D), jnp.float32), 0.25, 1.75),
        "in_proj": scatter_about(key_of[6], (LAYERS, 2, 3, D, D), (D // 4) ** -0.5, 1.0, (), jnp.float32),
        "out_proj": scatter_about(key_of[7], (LAYERS, 2, D, D), (D // 8) ** -0.5, 1.5, (), jnp.float32),
        "router": scatter_about(key_of[8], (LAYERS, 2, EXPERTS), 1.2, 4.0, (), jnp.float32),
        "expert_up": scatter_about(key_of[9], (LAYERS, EXPERTS, D, HID), D ** -0.5, 0.5, (), jnp.float32),
        "expert_down": scatter_about(key_of[10], (LAYERS, EXPERTS, HID, D), HID ** -0.5, 0.375, (), jnp.float32),
        "cotangent": scatter_about(key_of[11], (MESHES, NPTS, D), 1.0, 6.0, ((0, 4), (1, 8)), jnp.float32),
    }


@jax.custom_vjp
def low(v):
    return lax.optimization_barrier(v.astype(jnp.bfloat16)).astype(jnp.float32)

@jax.custom_vjp
def low_back(v):
    return v

def low_keep(v):
    return (low(v), None)

def low_pass(kept, grad):
    return (grad,)

def back_keep(v):
    return (v, None)

def back_low(kept, grad):
    return (low(grad),)
low.defvjp(low_keep, low_pass)
low_back.defvjp(back_keep, back_low)
PRECISE = lax.Precision.HIGHEST
eps = 1e-05

def layer_norm(stream, gain_row):
    row_mean = lax.optimization_barrier(jnp.mean(stream, axis=-1, keepdims=True))
    centred = stream - row_mean
    row_var = lax.optimization_barrier(jnp.mean(centred * centred, axis=-1, keepdims=True))
    return centred * lax.rsqrt(row_var + eps) * gain_row

def split_heads(matrix):
    return matrix.reshape(matrix.shape[:-1] + (HEADS, D // HEADS))

def head_softmax(matrix):
    return jax.nn.softmax(split_heads(matrix), axis=-1)

def linear(matrix, weight):
    return jnp.dot(matrix, weight, precision=PRECISE)

def forward(stream, func_points, coords, presence_w, keep, norm_gain, in_proj, out_proj, router, expert_up, expert_down):
    for layer_at in range(LAYERS):
        normed = layer_norm(stream, norm_gain[layer_at, 0])
        queries = head_softmax(linear(normed, in_proj[layer_at, 0, 0]))
        key_soft = head_softmax(linear(func_points, in_proj[layer_at, 0, 1])) * keep[..., None, None]
        values = split_heads(linear(func_points, in_proj[layer_at, 0, 2]))
        summary = jnp.einsum('mfpha,mfphc->mfhac', key_soft, values, precision=PRECISE)
        normalizer = lax.optimization_barrier(jnp.sum(key_soft, axis=2))
        numerator = jnp.einsum('mnha,mfhac->mfnhc', queries, summary, precision=PRECISE)
        denominator = jnp.einsum('mnha,mfha->mfnh', queries, normalizer, precision=PRECISE)
        mixed = jnp.einsum('mf,mfnhc->mnhc', presence_w, numerator / denominator[..., None], precision=PRECISE) + queries
        stream = stream + linear(mixed.reshape(stream.shape), out_proj[layer_at, 0])
        normed = layer_norm(stream, norm_gain[layer_at, 1])
        queries = head_softmax(linear(normed, in_proj[layer_at, 1, 0]))
        key_soft = head_softmax(linear(normed, in_proj[layer_at, 1, 1]))
        values = split_heads(linear(normed, in_proj[layer_at, 1, 2]))
        summary = jnp.einsum('mnha,mnhc->mhac', key_soft, values, precision=PRECISE)
        normalizer = lax.optimization_barrier(jnp.sum(key_soft, axis=1))
        numerator = jnp.einsum('mnha,mhac->mnhc', queries, summary, precision=PRECISE)
        denominator = jnp.einsum('mnha,mha->mnh', queries, normalizer, precision=PRECISE)
        mixed = numerator / denominator[..., None] + queries
        stream = stream + linear(mixed.reshape(stream.shape), out_proj[layer_at, 1])
        normed = layer_norm(stream, norm_gain[layer_at, 2])
        gate_probs = jax.nn.softmax(jnp.einsum('mcn,ce->mne', coords, router[layer_at], precision=PRECISE), axis=-1)
        hidden = jax.nn.gelu(jnp.einsum('mnd,edh->mneh', normed, expert_up[layer_at], precision=PRECISE), approximate=True)
        stream = stream + jnp.einsum('mneh,ehd->mnd', hidden * gate_probs[..., None], expert_down[layer_at], precision=PRECISE)
    return stream

def reference(features, func_points, coords, presence, valid_rows, norm_gain, in_proj, out_proj, router, expert_up, expert_down, cotangent):
    presence_f = presence.astype(jnp.float32)
    presence_w = presence_f / lax.optimization_barrier(jnp.sum(presence_f, axis=1, keepdims=True))
    within = jnp.arange(FPTS, dtype=jnp.int32) % FPTS_DEV
    keep = (within[None, None, :] < jnp.repeat(valid_rows, FPTS_DEV, axis=2)).astype(jnp.float32)

    def closed(stream_in, gain_all, proj_in, proj_out, route_all, up_all, down_all):
        return forward(stream_in, func_points, coords, presence_w, keep, gain_all, proj_in, proj_out, route_all, up_all, down_all)
    output, pullback = jax.vjp(closed, features, norm_gain, in_proj, out_proj, router, expert_up, expert_down)
    grads = pullback(cotangent)
    return (output, grads[0], grads[1], grads[2], grads[3], grads[4], grads[5], grads[6])
```

```python
import functools
import math

import jax
import jax.numpy as jnp
from jax import lax
from jax.experimental import pallas as pl
from jax.experimental.pallas import tpu as pltpu
from jax.sharding import PartitionSpec as P

MESH = pl.DeviceIdType.MESH
F32 = jnp.float32
BF16 = jnp.bfloat16
HEADS = 8
HEAD_DIM = 16
EPS = 1e-05
C1 = math.sqrt(2.0 / math.pi)
C2 = C1 * 0.044715
TILE = 512
MSG = 24


def nn(a, b):
    return jnp.dot(a, b, preferred_element_type=F32)


def nt(a, b):
    return lax.dot_general(a, b, (((1,), (1,)), ((), ())), preferred_element_type=F32)


def tn(a, b):
    return lax.dot_general(a, b, (((0,), (0,)), ((), ())), preferred_element_type=F32)


def split(x):
    high = x.astype(BF16)
    return high, (x - high.astype(F32)).astype(BF16)


def rows(*parts):
    return jnp.concatenate(parts, axis=0)


def cols(*parts):
    return jnp.concatenate(parts, axis=1)


def triple(w):
    high, low = split(w)
    return cols(high, low, high)


def k3(w3, x):
    high, low = x
    return nn(w3, rows(high, high, low))


def d3(w_high, w_low, x):
    high, low = x
    return nn(w_high, high) + (nn(w_low, high) + nn(w_high, low))


def outer(a, b):
    m, n = a[0].shape[0], b[0].shape[0]
    r = nt(rows(*a), rows(*b))
    return r[:m, :n] + (r[:m, n:] + r[m:, :n])


def wide(column, t):
    return cols(*([column] * (t // 128)))


def lanes(x):
    total = x[:, :128]
    for at in range(128, x.shape[1], 128):
        total = total + x[:, at : at + 128]
    return total


def by_head(x):
    return x.reshape(HEAD_DIM, HEADS, x.shape[-1])


def head_sum(x):
    return jnp.sum(by_head(x), axis=0)


def spread(r):
    return jnp.broadcast_to(r[None], (HEAD_DIM,) + r.shape).reshape(HEAD_DIM * HEADS, r.shape[-1])


def head_softmax(z):
    z = by_head(z)
    e = jnp.exp(z - jnp.max(z, axis=0)[None])
    p = e * (1.0 / jnp.sum(e, axis=0))[None]
    return p.reshape(HEAD_DIM * HEADS, p.shape[-1])


def softmax_back(p, dp):
    return p * (dp - spread(head_sum(p * dp)))


def mean(x):
    return jnp.sum(x, axis=0, keepdims=True) * (1.0 / x.shape[0])


def layer_norm(s, gain):
    centred = s - mean(s)
    r = lax.rsqrt(mean(centred * centred) + EPS)
    return centred * r * gain, r


def norm_back(dy, y, r, gain, inv_gain):
    xhat = y * inv_gain
    v = gain * dy
    return r * (v - mean(v) - xhat * mean(v * xhat)), dy * xhat


def put(ref, at, sl, x):
    d = x[0].shape[0]
    ref[at, 0:d, sl] = x[0]
    ref[at, d : 2 * d, sl] = x[1]


def get(ref, at, sl):
    both = ref[at, :, sl]
    d = both.shape[0] // 2
    return both[:d], both[d:]


def whole(x):
    return x[0].astype(F32) + x[1].astype(F32)


def gelu_parts(v):
    v2 = v * v
    g = 0.5 + 0.5 * jnp.tanh(v * (C1 + C2 * v2))
    return v2, g


def device_kernel(
    n_blk,
    features,
    func_points,
    coords,
    presence,
    valid,
    gain,
    in_proj,
    out_proj,
    router,
    up,
    down,
    cot,
    out,
    fgrad,
    g_gain,
    g_in,
    g_out,
    g_router,
    g_up,
    g_down,
    w_in,
    w_qc,
    w_self,
    w_out,
    w_outb,
    up_t,
    up_n,
    down_t,
    down_n,
    gcol,
    rgcol,
    fp,
    kc,
    vc,
    stream,
    y_ref,
    r_ref,
    qc,
    mixc,
    qs,
    ks,
    vs,
    mixs,
    dzq,
    inv_ref,
    rden_ref,
    gates,
    kv_t,
    kv_n,
    z_col,
    dkv_t,
    dkv_n,
    dz_col,
    acc_kv,
    acc_dkvc,
    acc_wi,
    acc_wo,
    acc_g,
    src_c,
    got_c,
    src_s,
    got_s,
    send_c,
    recv_c,
    send_s,
    recv_s,
):
    layers, experts, hid = up.shape[0], up.shape[1], up.shape[3]
    funcs, points = func_points.shape[1], func_points.shape[2]
    d = features.shape[2]
    count = features.shape[1]
    t = TILE
    tiles = count // t
    me = lax.axis_index("blk")

    barrier = pltpu.get_barrier_semaphore()
    for j in range(1, n_blk):
        pl.semaphore_signal(
            barrier, inc=1, device_id={"blk": lax.rem(me + j, n_blk)}, device_id_type=MESH
        )

    def copies(src, got, send, recv, at):
        return [
            pltpu.make_async_remote_copy(
                src_ref=src.at[at],
                dst_ref=got.at[at, j - 1],
                send_sem=send.at[at, j - 1],
                recv_sem=recv.at[at, j - 1],
                device_id={"blk": lax.rem(me + j, n_blk)},
                device_id_type=MESH,
            )
            for j in range(1, n_blk)
        ]

    def send_off(refs, at):
        for copy in copies(*refs, at):
            copy.start()

    def collect(refs, at):
        for copy in copies(*refs, at):
            copy.wait()
        src, got = refs[0], refs[1]
        total = src[at]
        for j in range(n_blk - 1):
            total = total + got[at, j]
        return total

    cross = (src_c, got_c, send_c, recv_c)
    own = (src_s, got_s, send_s, recv_s)

    head_mask = (
        lax.broadcasted_iota(jnp.int32, (HEADS, d), 0)
        == lax.broadcasted_iota(jnp.int32, (HEADS, d), 1) % HEADS
    ).astype(F32)
    spot = lax.broadcasted_iota(jnp.int32, (d, d), 0)
    perm = (
        lax.broadcasted_iota(jnp.int32, (d, d), 1) == (spot % HEADS) * HEAD_DIM + spot // HEADS
    ).astype(F32)
    perm16 = perm.astype(BF16)

    def compact(full):
        return jnp.sum(full.reshape(HEAD_DIM, HEADS, d) * head_mask[None], axis=1)

    def expand(compacted):
        full = jnp.broadcast_to(compacted[:, None, :], (HEAD_DIM, HEADS, d)) * head_mask[None]
        return full.reshape(d, d)

    def unpack(total, t_ref, n_ref, c_ref, at):
        full = expand(total[:HEAD_DIM])
        t_ref[at] = triple(full)
        n_ref[at] = triple(full.T)
        c_ref[at] = rows(*([total[HEAD_DIM:MSG]] * HEAD_DIM)).T

    for l in range(layers):
        for a in range(2):
            for j in range(3):
                w_high, w_low = split(in_proj[l, a, j])
                at = a * 3 + j
                high = nt(perm16, w_high).astype(BF16)
                low = nt(perm16, w_low).astype(BF16)
                w_in[l, at * d : (at + 1) * d, :] = cols(high, low, high)
                if (a, j) == (0, 0) or a == 1:
                    high = nt(w_high, perm16).astype(BF16)
                    low = nt(w_low, perm16).astype(BF16)
                    if a == 0:
                        w_qc[l] = cols(high, low, high)
                    else:
                        w_self[l, :, j * d : (j + 1) * d] = high
                        w_self[l, :, (3 + j) * d : (4 + j) * d] = low
            w_high, w_low = split(out_proj[l, a])
            contract = (((0,), (1,)), ((), ()))
            high = lax.dot_general(w_high, perm16, contract, preferred_element_type=F32).astype(BF16)
            low = lax.dot_general(w_low, perm16, contract, preferred_element_type=F32).astype(BF16)
            w_out[l, a] = cols(high, low, high)
            high = nn(perm16, w_high).astype(BF16)
            low = nn(perm16, w_low).astype(BF16)
            w_outb[l, a] = cols(high, low, high)
        for e in range(experts):
            lo, hi = e * hid, (e + 1) * hid
            w = up[l, e]
            high, low = split(w)
            up_n[l, :, lo:hi] = high
            up_n[l, :, experts * hid + lo : experts * hid + hi] = low
            up_t[l, lo:hi, :] = triple(w.T)
            w = down[l, e]
            down_n[l, lo:hi, :] = triple(w)
            high, low = split(w.T)
            down_t[l, :, lo:hi] = high
            down_t[l, :, experts * hid + lo : experts * hid + hi] = low
        for j in range(3):
            column = jnp.broadcast_to(gain[l, j : j + 1, :], (d, d)).T
            gcol[l * 3 + j] = column
            rgcol[l * 3 + j] = 1.0 / column

    present = [presence[0, f].astype(F32) for f in range(funcs)]
    all_present = present[0]
    for f in range(1, funcs):
        all_present = all_present + present[f]
    weight = [
        jnp.full((1, 1), present[f], F32) / jnp.full((1, 1), all_present, F32) for f in range(funcs)
    ]

    for f in range(funcs):
        high, low = split(func_points[0, f].T)
        fp[f, :d, :] = high
        fp[f, d:, :] = low

    ones = jnp.ones((16, points), BF16)
    ones_t = jnp.ones((16, t), BF16)

    def cross_summary(l):
        for f in range(funcs):
            both = fp[f]
            z = k3(w_in[l, d : 3 * d, :], (both[:d], both[d:]))
            kept = (
                lax.broadcasted_iota(jnp.int32, (1, points), 1) < valid[0, f, me]
            ).astype(F32)
            k = split(head_softmax(z[:d]) * kept)
            v = split(z[d:])
            put(kc, l * funcs + f, slice(None), k)
            put(vc, l * funcs + f, slice(None), v)
            r = nt(rows(*v, ones), rows(*k))
            src_c[l, f * MSG : f * MSG + HEAD_DIM, :] = compact(
                r[:d, :d] + (r[:d, d:] + r[d : 2 * d, :d])
            )
            src_c[l, f * MSG + HEAD_DIM : (f + 1) * MSG, :] = (
                r[2 * d : 2 * d + 8, :d] + r[2 * d : 2 * d + 8, d:]
            )
        send_off(cross, l)

    def cross_total(l):
        total = collect(cross, l)
        for f in range(funcs):
            unpack(
                total[f * MSG : (f + 1) * MSG],
                kv_t.at[l],
                kv_n.at[l],
                z_col.at[l],
                f,
            )

    def self_total(l):
        unpack(collect(own, l), kv_t.at[l], kv_n.at[l], z_col.at[l], funcs)

    def norm_in(l, at, s, sl):
        y, r = layer_norm(s, wide(gcol[l * 3 + at], t))
        y = split(y)
        put(y_ref, l * 3 + at, sl, y)
        r_ref[l * 3 + at, 0:1, sl] = r
        return y

    def norm_out(l, at, dy, sl):
        y = whole(get(y_ref, l * 3 + at, sl))
        ds, dg = norm_back(
            dy,
            y,
            r_ref[l * 3 + at, 0:1, sl],
            wide(gcol[l * 3 + at], t),
            wide(rgcol[l * 3 + at], t),
        )
        acc_g[l * 3 + at] += lanes(dg)
        return ds

    def cross_query(l, s, sl):
        y = norm_in(l, 0, s, sl)
        put(qc, l, sl, split(head_softmax(k3(w_in[l, :d, :], y))))

    def cross_read(l, s, sl):
        q2 = get(qc, l, sl)
        q = whole(q2)
        num = k3(kv_t[l, :funcs].reshape(funcs * d, 3 * d), q2)
        mix = q
        for f in range(funcs):
            rden = 1.0 / head_sum(q * wide(z_col[l, f], t))
            inv = rden * weight[f]
            inv_ref[l, f * 8 : (f + 1) * 8, sl] = inv
            inv_ref[l, (funcs + f) * 8 : (funcs + f + 1) * 8, sl] = rden
            mix = mix + num[f * d : (f + 1) * d] * spread(inv)
        mix = split(mix)
        put(mixc, l, sl, mix)
        s = s + k3(w_out[l, 0], mix)
        y = norm_in(l, 1, s, sl)
        z = k3(w_in[l, 3 * d :, :], y)
        q = split(head_softmax(z[:d]))
        k = split(head_softmax(z[d : 2 * d]))
        v = split(z[2 * d :])
        put(qs, l, sl, q)
        put(ks, l, sl, k)
        put(vs, l, sl, v)
        r = nt(rows(*v, ones_t), rows(*k))
        acc_kv[:d, :] += r[:d, :d] + (r[:d, d:] + r[d : 2 * d, :d])
        acc_kv[d:, :] += r[2 * d : 2 * d + 8, :d] + r[2 * d : 2 * d + 8, d:]
        stream[:, sl] = s

    def send_self(l):
        src_s[l, :HEAD_DIM, :] = compact(acc_kv[:d, :])
        src_s[l, HEAD_DIM:, :] = acc_kv[d:, :]
        send_off(own, l)

    def self_read(l, s, sl):
        q2 = get(qs, l, sl)
        q = whole(q2)
        num = k3(kv_t[l, funcs], q2)
        rden = 1.0 / head_sum(q * wide(z_col[l, funcs], t))
        rden_ref[l, :, sl] = rden
        mix = split(num * spread(rden) + q)
        put(mixs, l, sl, mix)
        s = s + k3(w_out[l, 1], mix)
        return s, norm_in(l, 2, s, sl)

    def hidden_in(l, e, y):
        return k3(up_t[l, e * hid : (e + 1) * hid, :], y)

    def down_of(l, e, x):
        at = experts * hid
        return d3(
            down_t[l, :, e * hid : (e + 1) * hid],
            down_t[l, :, at + e * hid : at + (e + 1) * hid],
            x,
        )

    def run_experts(l, y, sl):
        total = None
        for e in range(experts):
            v = hidden_in(l, e, y)
            _, g = gelu_parts(v)
            part = down_of(l, e, split(v * g * gates[l, e : e + 1, sl]))
            total = part if total is None else total + part
        return total

    def experts_back(l, ds, y, sl, forward):
        ds2 = split(ds)
        total, dy, dgate = None, None, []
        at = experts * hid
        for e in range(experts):
            gate = gates[l, e : e + 1, sl]
            v = hidden_in(l, e, y)
            back = k3(down_n[l, e * hid : (e + 1) * hid, :], ds2)
            v2, g = gelu_parts(v)
            act = v * g
            slope = g * (1.0 + (1.0 - g) * v * (2.0 * C1 + 6.0 * C2 * v2))
            dgate.append(jnp.sum(act * back, axis=0, keepdims=True))
            gated = split(act * gate)
            dpre = split(slope * back * gate)
            g_down[l, e] += outer(gated, ds2)
            g_up[l, e] += outer(y, dpre)
            if forward:
                part = down_of(l, e, gated)
                total = part if total is None else total + part
            part = d3(
                up_n[l, :, e * hid : (e + 1) * hid],
                up_n[l, :, at + e * hid : at + (e + 1) * hid],
                dpre,
            )
            dy = part if dy is None else dy + part
        probs = [gates[l, e : e + 1, sl] for e in range(experts)]
        centre = probs[0] * dgate[0]
        for e in range(1, experts):
            centre = centre + probs[e] * dgate[e]
        dlogit = rows(*[probs[e] * (dgate[e] - centre) for e in range(experts)])
        place = coords[0, :, sl]
        g_router[l] += lanes(rows(dlogit * place[0:1], dlogit * place[1:2]))
        return total, ds + norm_out(l, 2, dy, sl)

    def self_read_back(l, ds, sl):
        ds2 = split(ds)
        dmix = k3(w_outb[l, 1], ds2)
        acc_wo[l, 1] += outer(get(mixs, l, sl), ds2)
        back = k3(kv_n[l, funcs], split(dmix))
        q2 = get(qs, l, sl)
        q = whole(q2)
        rden = rden_ref[l, :, sl]
        u = rden * rden * head_sum(q * back)
        dq = dmix + spread(rden) * back - wide(z_col[l, funcs], t) * spread(u)
        put(dzq, 0, sl, split(softmax_back(q, dq)))
        da = split(dmix * spread(rden))
        u2 = split(u)
        r = nt(rows(*da, *u2), rows(*q2))
        acc_kv[:d, :] += r[:d, :d] + (r[:d, d:] + r[d : 2 * d, :d])
        low = r[2 * d :, :d] + r[2 * d :, d:]
        acc_kv[d:, :] += low[:8] + low[8:]

    def back_row(x):
        return jnp.broadcast_to(-jnp.sum(x * head_mask, axis=0, keepdims=True), (HEADS, d))

    def send_self_back(l):
        at = layers + l
        src_s[at, :HEAD_DIM, :] = compact(acc_kv[:d, :])
        src_s[at, HEAD_DIM:, :] = back_row(acc_kv[d:, :])
        send_off(own, at)

    def self_total_back(l):
        unpack(collect(own, layers + l), dkv_t, dkv_n, dz_col, 0)

    def attention_back(l, ds, sl):
        k2, v2 = get(ks, l, sl), get(vs, l, sl)
        dk = k3(dkv_n[0], v2) + wide(dz_col[0], t)
        dv = split(k3(dkv_t[0], k2))
        dzk = split(softmax_back(whole(k2), dk))
        q2 = get(dzq, 0, sl)
        dz = (rows(q2[0], dzk[0], dv[0]), rows(q2[1], dzk[1], dv[1]))
        y2 = get(y_ref, l * 3 + 1, sl)
        acc_wi[l, 3 * d :, :] += outer(dz, y2)
        dy = d3(w_self[l, :, : 3 * d], w_self[l, :, 3 * d :], dz)
        ds = ds + norm_out(l, 1, dy, sl)
        ds2 = split(ds)
        dmix = k3(w_outb[l, 0], ds2)
        acc_wo[l, 0] += outer(get(mixc, l, sl), ds2)
        back = k3(kv_n[l, :funcs].reshape(funcs * d, 3 * d), split(dmix))
        q2 = get(qc, l, sl)
        q = whole(q2)
        dq = dmix
        da, us = [], []
        for f in range(funcs):
            inv = inv_ref[l, f * 8 : (f + 1) * 8, sl]
            rden = inv_ref[l, (funcs + f) * 8 : (funcs + f + 1) * 8, sl]
            back_f = back[f * d : (f + 1) * d]
            u = inv * rden * head_sum(q * back_f)
            dq = dq + spread(inv) * back_f - wide(z_col[l, f], t) * spread(u)
            da.append(dmix * spread(inv))
            us.append(u)
        us.append(jnp.zeros_like(us[0]))
        side = rows(*us[:4])
        m = funcs * d
        r = nt(rows(*split(rows(*da)), *split(side)), rows(*q2))
        acc_dkvc[:m, :] += r[:m, :d] + (r[:m, d:] + r[m : 2 * m, :d])
        low = r[2 * m :, :d] + r[2 * m :, d:]
        acc_dkvc[m:, :] += (low[: 8 * (funcs + 1)] + low[8 * (funcs + 1) :])[: 8 * funcs]
        dz2 = split(softmax_back(q, dq))
        acc_wi[l, :d, :] += outer(dz2, get(y_ref, l * 3, sl))
        return ds + norm_out(l, 0, k3(w_qc[l], dz2), sl)

    def send_cross_back(l):
        at = layers + l
        for f in range(funcs):
            src_c[at, f * MSG : f * MSG + HEAD_DIM, :] = compact(acc_dkvc[f * d : (f + 1) * d, :])
            src_c[at, f * MSG + HEAD_DIM : (f + 1) * MSG, :] = back_row(
                acc_dkvc[funcs * d + f * 8 : funcs * d + (f + 1) * 8, :]
            )
        send_off(cross, at)

    def cross_keys_back(l):
        total = collect(cross, layers + l)
        for f in range(funcs):
            unpack(total[f * MSG : (f + 1) * MSG], dkv_t, dkv_n, dz_col, f)
        for f in range(funcs):
            k2 = get(kc, l * funcs + f, slice(None))
            v2 = get(vc, l * funcs + f, slice(None))
            dk = k3(dkv_n[f], v2) + wide(dz_col[f], points)
            dv = split(k3(dkv_t[f], k2))
            dzk = split(softmax_back(whole(k2), dk))
            both = fp[f]
            part = outer(
                (rows(dzk[0], dv[0]), rows(dzk[1], dv[1])), (both[:d], both[d:])
            )
            if f == 0:
                acc_wi[l, d : 3 * d, :] = part
            else:
                acc_wi[l, d : 3 * d, :] += part

    def each_tile(body):
        def step(i, carry):
            body(pl.ds(pl.multiple_of(i * t, t), t))
            return carry

        lax.fori_loop(0, tiles, step, 0)

    for ref in (acc_wi, acc_wo, acc_g, g_router, g_up, g_down):
        ref[...] = jnp.zeros_like(ref)
    acc_kv[...] = jnp.zeros_like(acc_kv)
    acc_dkvc[...] = jnp.zeros_like(acc_dkvc)
    pl.semaphore_wait(barrier, n_blk - 1)
    cross_summary(0)

    def first(sl):
        s = features[0, sl, :].T
        stream[:, sl] = s
        cross_query(0, s, sl)
        place = coords[0, :, sl]
        for l in range(layers):
            logit = [
                place[0:1] * router[l, 0, e] + place[1:2] * router[l, 1, e] for e in range(experts)
            ]
            top = functools.reduce(jnp.maximum, logit)
            grown = [jnp.exp(x - top) for x in logit]
            total = functools.reduce(jnp.add, grown)
            for e in range(experts):
                gates[l, e : e + 1, sl] = grown[e] / total

    each_tile(first)
    cross_summary(1)
    cross_total(0)
    each_tile(lambda sl: cross_read(0, stream[:, sl], sl))
    send_self(0)
    cross_total(1)
    acc_kv[...] = jnp.zeros_like(acc_kv)
    self_total(0)

    def second(sl):
        s, y = self_read(0, stream[:, sl], sl)
        s = s + run_experts(0, y, sl)
        cross_query(1, s, sl)
        cross_read(1, s, sl)

    each_tile(second)
    send_self(1)
    acc_kv[...] = jnp.zeros_like(acc_kv)
    self_total(1)

    def third(sl):
        s, y = self_read(1, stream[:, sl], sl)
        ds = cot[0, sl, :].T
        more, ds = experts_back(1, ds, y, sl, True)
        out[0, sl, :] = (s + more).T
        self_read_back(1, ds, sl)
        stream[:, sl] = ds

    each_tile(third)
    send_self_back(1)
    acc_kv[...] = jnp.zeros_like(acc_kv)
    self_total_back(1)

    def fourth(sl):
        ds = attention_back(1, stream[:, sl], sl)
        _, ds = experts_back(0, ds, get(y_ref, 2, sl), sl, False)
        self_read_back(0, ds, sl)
        stream[:, sl] = ds

    each_tile(fourth)
    send_self_back(0)
    send_cross_back(1)
    acc_dkvc[...] = jnp.zeros_like(acc_dkvc)
    self_total_back(0)

    def fifth(sl):
        fgrad[0, sl, :] = attention_back(0, stream[:, sl], sl).T

    each_tile(fifth)
    send_cross_back(0)
    cross_keys_back(1)
    cross_keys_back(0)

    exact = functools.partial(
        lax.dot_general, precision=lax.Precision.HIGHEST, preferred_element_type=F32
    )
    for l in range(layers):
        for a in range(2):
            for j in range(3):
                at = a * 3 + j
                g_in[l, a, j] = exact(
                    acc_wi[l, at * d : (at + 1) * d, :], perm, (((0,), (0,)), ((), ()))
                )
            g_out[l, a] = exact(perm, acc_wo[l, a], (((0,), (0,)), ((), ())))
        for j in range(3):
            g_gain[l, j : j + 1, :] = jnp.sum(acc_g[l * 3 + j].T, axis=0, keepdims=True)


def on_device(
    n_blk,
    features,
    func_points,
    coords,
    presence,
    valid_rows,
    norm_gain,
    in_proj,
    out_proj,
    router,
    expert_up,
    expert_down,
    cotangent,
):
    layers, experts, d, hid = expert_up.shape
    count = features.shape[1]
    funcs, points = func_points.shape[1], func_points.shape[2]
    wide_hid = experts * hid
    shape = jax.ShapeDtypeStruct
    vmem = pl.BlockSpec(memory_space=pltpu.VMEM)
    smem = pl.BlockSpec(memory_space=pltpu.SMEM)
    pair = pltpu.VMEM((layers, 2 * d, count), BF16)
    scratch = [
        pltpu.VMEM((layers, 6 * d, 3 * d), BF16),
        pltpu.VMEM((layers, d, 3 * d), BF16),
        pltpu.VMEM((layers, d, 6 * d), BF16),
        pltpu.VMEM((layers, 2, d, 3 * d), BF16),
        pltpu.VMEM((layers, 2, d, 3 * d), BF16),
        pltpu.VMEM((layers, wide_hid, 3 * d), BF16),
        pltpu.VMEM((layers, d, 2 * wide_hid), BF16),
        pltpu.VMEM((layers, d, 2 * wide_hid), BF16),
        pltpu.VMEM((layers, wide_hid, 3 * d), BF16),
        pltpu.VMEM((layers * 3, d, 128), F32),
        pltpu.VMEM((layers * 3, d, 128), F32),
        pltpu.VMEM((funcs, 2 * d, points), BF16),
        pltpu.VMEM((layers * funcs, 2 * d, points), BF16),
        pltpu.VMEM((layers * funcs, 2 * d, points), BF16),
        pltpu.VMEM((d, count), F32),
        pltpu.VMEM((layers * 3, 2 * d, count), BF16),
        pltpu.VMEM((layers * 3, 8, count), F32),
        pair,
        pair,
        pair,
        pair,
        pair,
        pair,
        pltpu.VMEM((1, 2 * d, count), BF16),
        pltpu.VMEM((layers, 2 * funcs * HEADS, count), F32),
        pltpu.VMEM((layers, HEADS, count), F32),
        pltpu.VMEM((layers, experts, count), F32),
        pltpu.VMEM((layers, funcs + 1, d, 3 * d), BF16),
        pltpu.VMEM((layers, funcs + 1, d, 3 * d), BF16),
        pltpu.VMEM((layers, funcs + 1, d, 128), F32),
        pltpu.VMEM((funcs, d, 3 * d), BF16),
        pltpu.VMEM((funcs, d, 3 * d), BF16),
        pltpu.VMEM((funcs, d, 128), F32),
        pltpu.VMEM((d + HEADS, d), F32),
        pltpu.VMEM((funcs * (d + HEADS), d), F32),
        pltpu.VMEM((layers, 6 * d, d), F32),
        pltpu.VMEM((layers, 2, d, d), F32),
        pltpu.VMEM((layers * 3, d, 128), F32),
        pltpu.VMEM((2 * layers, funcs * MSG, d), F32),
        pltpu.VMEM((2 * layers, n_blk - 1, funcs * MSG, d), F32),
        pltpu.VMEM((2 * layers, MSG, d), F32),
        pltpu.VMEM((2 * layers, n_blk - 1, MSG, d), F32),
    ] + [pltpu.SemaphoreType.DMA((2 * layers, n_blk - 1))] * 4
    results = pl.pallas_call(
        functools.partial(device_kernel, n_blk),
        out_shape=[
            shape(features.shape, F32),
            shape(features.shape, F32),
            shape(norm_gain.shape, F32),
            shape(in_proj.shape, F32),
            shape(out_proj.shape, F32),
            shape((layers, 2 * experts, 128), F32),
            shape(expert_up.shape, F32),
            shape(expert_down.shape, F32),
        ],
        in_specs=[vmem, vmem, vmem, smem, smem, vmem, vmem, vmem, smem, vmem, vmem, vmem],
        out_specs=[vmem] * 8,
        scratch_shapes=scratch,
        compiler_params=pltpu.CompilerParams(
            collective_id=0, has_side_effects=True, vmem_limit_bytes=62 * 2**20
        ),
        name="gnot",
    )(
        features,
        func_points,
        coords,
        presence,
        valid_rows,
        norm_gain,
        in_proj,
        out_proj,
        router,
        expert_up,
        expert_down,
        cotangent,
    )
    y, dx, gain_g, in_g, out_g, route_g, up_g, down_g = results
    route_g = jnp.sum(route_g, axis=-1).reshape(router.shape)
    return (y, dx) + lax.psum((gain_g, in_g, out_g, route_g, up_g, down_g), ("dp", "blk"))


def solution(mesh):
    placed = (
        P("dp", "blk", None),
        P("dp", None, "blk", None),
        P("dp", None, "blk"),
        P("dp", None),
        P("dp", None, None),
        P(),
        P(),
        P(),
        P(),
        P(),
        P(),
        P("dp", "blk", None),
    )
    return jax.shard_map(
        functools.partial(on_device, mesh.shape["blk"]),
        mesh=mesh,
        in_specs=placed,
        out_specs=(P("dp", "blk", None), P("dp", "blk", None), P(), P(), P(), P(), P(), P()),
        check_vma=False,
    )
```

```python
import functools
import math

import jax
import jax.numpy as jnp
from jax import lax
from jax.experimental import pallas as pl
from jax.experimental.pallas import tpu as pltpu
from jax.sharding import PartitionSpec as P

MESH = pl.DeviceIdType.MESH
F32 = jnp.float32
BF16 = jnp.bfloat16
HEADS = 8
HEAD_DIM = 16
EPS = 1e-05
C1 = math.sqrt(2.0 / math.pi)
C2 = C1 * 0.044715
TILE = 1024
MSG = 24


def nn(a, b):
    return jnp.dot(a, b, preferred_element_type=F32)


def nt(a, b):
    return lax.dot_general(a, b, (((1,), (1,)), ((), ())), preferred_element_type=F32)


def tn(a, b):
    return lax.dot_general(a, b, (((0,), (0,)), ((), ())), preferred_element_type=F32)


def split(x):
    high = x.astype(BF16)
    return high, (x - high.astype(F32)).astype(BF16)


def rows(*parts):
    return jnp.concatenate(parts, axis=0)


def cols(*parts):
    return jnp.concatenate(parts, axis=1)


def triple(w):
    high, low = split(w)
    return cols(high, low, high)


def k3(w3, x):
    high, low = x
    return nn(w3, rows(high, high, low))


def d3(w_high, w_low, x):
    high, low = x
    return nn(w_high, high) + (nn(w_low, high) + nn(w_high, low))


def outer(a, b):
    m, n = a[0].shape[0], b[0].shape[0]
    r = nt(rows(*a), rows(*b))
    return r[:m, :n] + (r[:m, n:] + r[m:, :n])


def wide(column, t):
    return cols(*([column] * (t // 128)))


def lanes(x):
    total = x[:, :128]
    for at in range(128, x.shape[1], 128):
        total = total + x[:, at : at + 128]
    return total


def by_head(x):
    return x.reshape(HEAD_DIM, HEADS, x.shape[-1])


def head_sum(x):
    return jnp.sum(by_head(x), axis=0)


def spread(r):
    return jnp.broadcast_to(r[None], (HEAD_DIM,) + r.shape).reshape(HEAD_DIM * HEADS, r.shape[-1])


def head_softmax(z):
    z = by_head(z)
    e = jnp.exp(z - jnp.max(z, axis=0)[None])
    p = e * (1.0 / jnp.sum(e, axis=0))[None]
    return p.reshape(HEAD_DIM * HEADS, p.shape[-1])


def softmax_back(p, dp):
    return p * (dp - spread(head_sum(p * dp)))


def mean(x):
    return jnp.sum(x, axis=0, keepdims=True) * (1.0 / x.shape[0])


def layer_norm(s, gain):
    centred = s - mean(s)
    r = lax.rsqrt(mean(centred * centred) + EPS)
    return centred * r * gain, r


def norm_back(dy, y, r, gain, inv_gain):
    xhat = y * inv_gain
    v = gain * dy
    return r * (v - mean(v) - xhat * mean(v * xhat)), dy * xhat


def put(ref, at, sl, x):
    d = x[0].shape[0]
    ref[at, 0:d, sl] = x[0]
    ref[at, d : 2 * d, sl] = x[1]


def get(ref, at, sl):
    both = ref[at, :, sl]
    d = both.shape[0] // 2
    return both[:d], both[d:]


def whole(x):
    return x[0].astype(F32) + x[1].astype(F32)


def gelu_parts(v):
    v2 = v * v
    g = 0.5 + 0.5 * jnp.tanh(v * (C1 + C2 * v2))
    return v2, g


def device_kernel(
    n_dp,
    n_blk,
    summed,
    features_hbm,
    points_hbm,
    coords,
    presence,
    valid,
    gain,
    in_hbm,
    out_hbm,
    router,
    up_hbm,
    down_hbm,
    cot_hbm,
    out,
    fgrad,
    f_att,
    f_up,
    f_down,
    f_small,
    points_ref,
    load_sem,
    g_att,
    g_up,
    g_down,
    g_small,
    w_in,
    w_qc,
    w_self,
    w_out,
    w_outb,
    up_t,
    up_n,
    down_t,
    down_n,
    gcol,
    rgcol,
    fp,
    kc,
    vc,
    stream,
    y_ref,
    r_ref,
    qc,
    mixc,
    qs,
    ks,
    vs,
    mixs,
    dzq,
    inv_ref,
    rden_ref,
    gates,
    kv_t,
    kv_n,
    z_col,
    dkv_t,
    dkv_n,
    dz_col,
    acc_kv,
    acc_dkvc,
    acc_wi,
    acc_wo,
    acc_g,
    acc_r,
    dy_ref,
    dgate_ref,
    src_c,
    got_c,
    src_s,
    got_s,
    send_c,
    recv_c,
    send_s,
    recv_s,
    *ring,
):
    if not summed:
        g_att, g_up, g_down, g_small = f_att, f_up, f_down, f_small
    layers, experts, hid = router.shape[0], router.shape[2], up_hbm.shape[2]
    funcs, points = points_hbm.shape[1], points_hbm.shape[2]
    count, d = features_hbm.shape[1:]

    def load(src, dst, at):
        copy = pltpu.make_async_copy(src, dst, load_sem.at[at])
        copy.start()
        return copy

    att_loads = []
    for at in range(layers * 2):
        att_loads.append(load(in_hbm.at[at], f_att.at[at, pl.ds(0, 3 * d)], 2 * at))
        att_loads.append(load(out_hbm.at[at], f_att.at[at, pl.ds(3 * d, d)], 2 * at + 1))
    at = 4 * layers
    points_load = load(points_hbm, points_ref, at)
    features_load = load(features_hbm, out, at + 1)
    up_load = load(up_hbm, f_up, at + 2)
    down_load = load(down_hbm, f_down, at + 3)
    cot_load = load(cot_hbm, fgrad, at + 4)
    me = lax.axis_index("blk")
    own_dp = lax.axis_index("dp")
    n_flat, n_line = n_dp, n_blk // 2
    core, line = own_dp % 2, me // 2
    flat = (own_dp // 2) * 2 + me % 2

    sibling = {"dp": own_dp - core + (1 - core), "blk": me}

    def flat_at(j):
        at = lax.rem(flat + j, n_flat)
        return {"dp": (at // 2) * 2 + core, "blk": line * 2 + at % 2}

    def line_at(j):
        return {"dp": own_dp, "blk": lax.rem(line + j, n_line) * 2 + me % 2}

    partners = [{"dp": own_dp, "blk": lax.rem(me + j, n_blk)} for j in range(1, n_blk)]
    if summed:
        partners += [sibling] + [flat_at(j) for j in range(1, n_flat)]
    barrier = pltpu.get_barrier_semaphore()
    for partner in partners:
        pl.semaphore_signal(barrier, inc=1, device_id=partner, device_id_type=MESH)

    running = []

    def take():
        now = [steps.pop(0) for steps in running]
        running[:] = [steps for steps in running if steps]

        def run():
            for step in now:
                step()

        return run

    def tick():
        take()()

    def made(jobs, send, recv):
        return [
            pltpu.make_async_remote_copy(
                src_ref=src,
                dst_ref=dst,
                send_sem=send.at[k],
                recv_sem=recv.at[k],
                device_id=device,
                device_id_type=MESH,
            )
            for k, src, dst, device in jobs()
        ]

    def go(jobs, send, recv):
        for copy in made(jobs, send, recv):
            copy.start()

    def settle(jobs, send, recv):
        for copy in made(jobs, send, recv):
            copy.wait()

    def reduction(local, final, halves, parts, pieces, send, recv):
        half = local.shape[0] // 2
        part = half // n_flat
        piece = part // n_line

        def at(start, size):
            return pl.ds(pl.multiple_of(start, 8), size)

        def of_core(other=0):
            return at((core if not other else 1 - core) * half, half)

        def of_flat(j=0):
            return at(core * half + lax.rem(flat + j, n_flat) * part, part)

        def of_line(j=0):
            return at(core * half + flat * part + lax.rem(line + j, n_line) * piece, piece)

        k1 = 1
        k2 = k1 + n_flat - 1
        k3_ = k2 + n_line - 1
        k4 = k3_ + n_line - 1
        k5 = k4 + n_flat - 1

        def core_out():
            return [(0, local.at[of_core(1)], halves, sibling)]

        def flat_out():
            return [
                (k1 + j - 1, local.at[of_flat(j)], parts.at[j - 1], flat_at(j))
                for j in range(1, n_flat)
            ]

        def line_out():
            return [
                (k2 + j - 1, local.at[of_line(j)], pieces.at[j - 1], line_at(j))
                for j in range(1, n_line)
            ]

        def line_back():
            mine = final.at[of_line()]
            return [(k3_ + j - 1, mine, mine, line_at(j)) for j in range(1, n_line)]

        def flat_back():
            mine = final.at[of_flat()]
            return [(k4 + j - 1, mine, mine, flat_at(j)) for j in range(1, n_flat)]

        def core_back():
            mine = final.at[of_core()]
            return [(k5, mine, mine, sibling)]

        def one():
            go(core_out, send, recv)

        def two():
            settle(core_out, send, recv)
            spot = of_core()
            local[spot] = local[spot] + halves[...]
            go(flat_out, send, recv)

        def three():
            settle(flat_out, send, recv)
            spot = of_flat()
            total = local[spot]
            for j in range(n_flat - 1):
                total = total + parts[j]
            local[spot] = total
            go(line_out, send, recv)

        def four():
            settle(line_out, send, recv)
            spot = of_line()
            total = local[spot]
            for j in range(n_line - 1):
                total = total + pieces[j]
            final[spot] = total
            go(line_back, send, recv)

        def five():
            settle(line_back, send, recv)
            go(flat_back, send, recv)

        def six():
            settle(flat_back, send, recv)
            go(core_back, send, recv)

        def seven():
            settle(core_back, send, recv)

        return [one, two, three, four, five, six, seven]

    def exchange_small(local, final, held, send, recv):
        levels = (
            (0, 2, core, lambda: [sibling], 0),
            (2, n_flat, flat, lambda: [flat_at(j) for j in range(1, n_flat)], 1),
            (2 + n_flat, n_line, line, lambda: [line_at(j) for j in range(1, n_line)], n_flat),
        )

        def jobs_of(level):
            at, _, place, devices, k = levels[level]

            def jobs():
                mine = held.at[at + place]
                return [(k + j, mine, mine, device) for j, device in enumerate(devices())]

            return jobs

        def start(level, value):
            at, _, place, _, _ = levels[level]
            held[at + place] = value
            go(jobs_of(level), send, recv)

        def finish(level):
            settle(jobs_of(level), send, recv)
            at, size = levels[level][:2]
            value = held[at]
            for j in range(1, size):
                value = value + held[at + j]
            return value

        def last():
            final[...] = finish(2)

        return [
            lambda: start(0, local[...]),
            lambda: start(1, finish(0)),
            lambda: start(2, finish(1)),
            last,
        ]

    def reduce_up(l, pair):
        seg = l * 2 + pair
        running.append(
            reduction(g_up.at[seg], f_up.at[seg], *[ref.at[seg] for ref in ring[:5]])
        )

    def reduce_rows(seg, local, final):
        running.append(reduction(local, final, *[ref.at[seg] for ref in ring[5:10]]))

    def reduce_pair(l, pair):
        if summed:
            reduce_up(l, pair)
            reduce_rows(l * 2 + pair, g_down.at[l * 2 + pair], f_down.at[l * 2 + pair])

    def reduce_att(l, a):
        if summed:
            reduce_rows(layers * 2 + l * 2 + a, g_att.at[l * 2 + a], f_att.at[l * 2 + a])

    def copies(src, got, send, recv, at):
        return [
            pltpu.make_async_remote_copy(
                src_ref=src.at[at],
                dst_ref=got.at[at, j - 1],
                send_sem=send.at[at, j - 1],
                recv_sem=recv.at[at, j - 1],
                device_id={"blk": lax.rem(me + j, n_blk)},
                device_id_type=MESH,
            )
            for j in range(1, n_blk)
        ]

    def send_off(refs, at):
        for copy in copies(*refs, at):
            copy.start()

    def collect(refs, at):
        for copy in copies(*refs, at):
            copy.wait()
        src, got = refs[0], refs[1]
        total = src[at]
        for j in range(n_blk - 1):
            total = total + got[at, j]
        return total

    cross = (src_c, got_c, send_c, recv_c)
    own = (src_s, got_s, send_s, recv_s)

    head_mask = (
        lax.broadcasted_iota(jnp.int32, (HEADS, d), 0)
        == lax.broadcasted_iota(jnp.int32, (HEADS, d), 1) % HEADS
    ).astype(F32)
    spot = lax.broadcasted_iota(jnp.int32, (d, d), 0)
    perm = (
        lax.broadcasted_iota(jnp.int32, (d, d), 1) == (spot % HEADS) * HEAD_DIM + spot // HEADS
    ).astype(F32)
    perm16 = perm.astype(BF16)

    def compact(full):
        return jnp.sum(full.reshape(HEAD_DIM, HEADS, d) * head_mask[None], axis=1)

    def expand(compacted):
        full = jnp.broadcast_to(compacted[:, None, :], (HEAD_DIM, HEADS, d)) * head_mask[None]
        return full.reshape(d, d)

    def unpack(total, t_ref, n_ref, c_ref, at):
        full = expand(total[:HEAD_DIM])
        t_ref[at] = triple(full)
        n_ref[at] = triple(full.T)
        c_ref[at] = rows(*([total[HEAD_DIM:MSG]] * HEAD_DIM)).T

    def cut_attention():
        for copy in att_loads:
            copy.wait()
        for l in range(layers):
            for a in range(2):
                for j in range(3):
                    w_high, w_low = split(f_att[l * 2 + a, j * d : (j + 1) * d, :])
                    at = a * 3 + j
                    high = nt(perm16, w_high).astype(BF16)
                    low = nt(perm16, w_low).astype(BF16)
                    w_in[l, at * d : (at + 1) * d, :] = cols(high, low, high)
                    if (a, j) == (0, 0) or a == 1:
                        high = nt(w_high, perm16).astype(BF16)
                        low = nt(w_low, perm16).astype(BF16)
                        if a == 0:
                            w_qc[l] = cols(high, low, high)
                        else:
                            w_self[l, :, j * d : (j + 1) * d] = high
                            w_self[l, :, (3 + j) * d : (4 + j) * d] = low
                w_high, w_low = split(f_att[l * 2 + a, 3 * d :, :])
                contract = (((0,), (1,)), ((), ()))
                high, low = [
                    lax.dot_general(w, perm16, contract, preferred_element_type=F32).astype(BF16)
                    for w in (w_high, w_low)
                ]
                w_out[l, a] = cols(high, low, high)
                high = nn(perm16, w_high).astype(BF16)
                low = nn(perm16, w_low).astype(BF16)
                w_outb[l, a] = cols(high, low, high)

    def cut_experts():
        up_load.wait()
        down_load.wait()
        for l in range(layers):
            for e in range(experts):
                lo, hi = e * hid, (e + 1) * hid
                seg, spot = l * 2 + e // 2, e % 2
                w = f_up[seg, spot * d : (spot + 1) * d, :]
                high, low = split(w)
                up_n[l, :, lo:hi] = high
                up_n[l, :, experts * hid + lo : experts * hid + hi] = low
                up_t[l, lo:hi, :] = triple(w.T)
                w = f_down[seg, spot * hid : (spot + 1) * hid, :]
                down_n[l, lo:hi, :] = triple(w)
                high, low = split(w.T)
                down_t[l, :, lo:hi] = high
                down_t[l, :, experts * hid + lo : experts * hid + hi] = low

    cut_attention()
    for l in range(layers):
        for j in range(3):
            column = jnp.broadcast_to(gain[l, j : j + 1, :], (d, d)).T
            gcol[l * 3 + j] = column
            rgcol[l * 3 + j] = 1.0 / column

    present = [presence[0, f].astype(F32) for f in range(funcs)]
    all_present = present[0]
    for f in range(1, funcs):
        all_present = all_present + present[f]
    weight = [
        jnp.full((1, 1), present[f], F32) / jnp.full((1, 1), all_present, F32) for f in range(funcs)
    ]

    points_load.wait()
    for f in range(funcs):
        high, low = split(points_ref[0, f].T)
        fp[f, :d, :] = high
        fp[f, d:, :] = low

    ones = jnp.ones((16, points), BF16)

    def cross_summary(l):
        for f in range(funcs):
            both = fp[f]
            z = k3(w_in[l, d : 3 * d, :], (both[:d], both[d:]))
            kept = (
                lax.broadcasted_iota(jnp.int32, (1, points), 1) < valid[0, f, me]
            ).astype(F32)
            k = split(head_softmax(z[:d]) * kept)
            v = split(z[d:])
            put(kc, l * funcs + f, slice(None), k)
            put(vc, l * funcs + f, slice(None), v)
            r = nt(rows(*v, ones), rows(*k))
            src_c[l, f * MSG : f * MSG + HEAD_DIM, :] = compact(
                r[:d, :d] + (r[:d, d:] + r[d : 2 * d, :d])
            )
            src_c[l, f * MSG + HEAD_DIM : (f + 1) * MSG, :] = (
                r[2 * d : 2 * d + 8, :d] + r[2 * d : 2 * d + 8, d:]
            )
        send_off(cross, l)

    def cross_total(l):
        total = collect(cross, l)
        for f in range(funcs):
            unpack(
                total[f * MSG : (f + 1) * MSG],
                kv_t.at[l],
                kv_n.at[l],
                z_col.at[l],
                f,
            )

    def self_total(l):
        unpack(collect(own, l), kv_t.at[l], kv_n.at[l], z_col.at[l], funcs)

    def norm_in(l, at, s, sl):
        y, r = layer_norm(s, wide(gcol[l * 3 + at], sl.size))
        y = split(y)
        put(y_ref, l * 3 + at, sl, y)
        r_ref[l * 3 + at, 0:1, sl] = r
        return y

    def norm_out(l, at, dy, sl):
        y = whole(get(y_ref, l * 3 + at, sl))
        ds, dg = norm_back(
            dy,
            y,
            r_ref[l * 3 + at, 0:1, sl],
            wide(gcol[l * 3 + at], sl.size),
            wide(rgcol[l * 3 + at], sl.size),
        )
        acc_g[l * 3 + at] += lanes(dg)
        return ds

    def cross_query(l, s, sl):
        y = norm_in(l, 0, s, sl)
        put(qc, l, sl, split(head_softmax(k3(w_in[l, :d, :], y))))

    def cross_read(l, s, sl):
        q2 = get(qc, l, sl)
        q = whole(q2)
        num = k3(kv_t[l, :funcs].reshape(funcs * d, 3 * d), q2)
        mix = q
        for f in range(funcs):
            rden = 1.0 / head_sum(q * wide(z_col[l, f], sl.size))
            inv = rden * weight[f]
            inv_ref[l, f * 8 : (f + 1) * 8, sl] = inv
            inv_ref[l, (funcs + f) * 8 : (funcs + f + 1) * 8, sl] = rden
            mix = mix + num[f * d : (f + 1) * d] * spread(inv)
        mix = split(mix)
        put(mixc, l, sl, mix)
        s = s + k3(w_out[l, 0], mix)
        y = norm_in(l, 1, s, sl)
        z = k3(w_in[l, 3 * d :, :], y)
        q = split(head_softmax(z[:d]))
        k = split(head_softmax(z[d : 2 * d]))
        v = split(z[2 * d :])
        put(qs, l, sl, q)
        put(ks, l, sl, k)
        put(vs, l, sl, v)
        r = nt(rows(*v, jnp.ones((16, sl.size), BF16)), rows(*k))
        acc_kv[:d, :] += r[:d, :d] + (r[:d, d:] + r[d : 2 * d, :d])
        acc_kv[d:, :] += r[2 * d : 2 * d + 8, :d] + r[2 * d : 2 * d + 8, d:]
        stream[:, sl] = s

    def send_self(l):
        src_s[l, :HEAD_DIM, :] = compact(acc_kv[:d, :])
        src_s[l, HEAD_DIM:, :] = acc_kv[d:, :]
        send_off(own, l)

    def self_read(l, s, sl):
        q2 = get(qs, l, sl)
        q = whole(q2)
        num = k3(kv_t[l, funcs], q2)
        rden = 1.0 / head_sum(q * wide(z_col[l, funcs], sl.size))
        rden_ref[l, :, sl] = rden
        mix = split(num * spread(rden) + q)
        put(mixs, l, sl, mix)
        s = s + k3(w_out[l, 1], mix)
        return s, norm_in(l, 2, s, sl)

    def hidden_in(l, e, y):
        return k3(up_t[l, e * hid : (e + 1) * hid, :], y)

    def down_of(l, e, x):
        at = experts * hid
        return d3(
            down_t[l, :, e * hid : (e + 1) * hid],
            down_t[l, :, at + e * hid : at + (e + 1) * hid],
            x,
        )

    def run_experts(l, y, sl):
        total = None
        for e in range(experts):
            v = hidden_in(l, e, y)
            _, g = gelu_parts(v)
            part = down_of(l, e, split(v * g * gates[l, e : e + 1, sl]))
            total = part if total is None else total + part
        return total

    def expert_back(l, e, y, ds2, sl):
        at = experts * hid
        gate = gates[l, e : e + 1, sl]
        v = hidden_in(l, e, y)
        back = k3(down_n[l, e * hid : (e + 1) * hid, :], ds2)
        v2, g = gelu_parts(v)
        act = v * g
        slope = g * (1.0 + (1.0 - g) * v * (2.0 * C1 + 6.0 * C2 * v2))
        dgate_ref[e : e + 1, sl] = jnp.sum(act * back, axis=0, keepdims=True)
        gated = split(act * gate)
        dpre = split(slope * back * gate)
        seg, spot = l * 2 + e // 2, e % 2
        g_down[seg, spot * hid : (spot + 1) * hid, :] += outer(gated, ds2)
        g_up[seg, spot * d : (spot + 1) * d, :] += outer(y, dpre)
        dy = d3(
            up_n[l, :, e * hid : (e + 1) * hid],
            up_n[l, :, at + e * hid : at + (e + 1) * hid],
            dpre,
        )
        return gated, dy

    def gates_back(l, ds, dy, sl):
        probs = [gates[l, e : e + 1, sl] for e in range(experts)]
        dgate = [dgate_ref[e : e + 1, sl] for e in range(experts)]
        centre = probs[0] * dgate[0]
        for e in range(1, experts):
            centre = centre + probs[e] * dgate[e]
        dlogit = rows(*[probs[e] * (dgate[e] - centre) for e in range(experts)])
        place = coords[0, :, sl]
        acc_r[l] += lanes(rows(dlogit * place[0:1], dlogit * place[1:2]))
        return ds + norm_out(l, 2, dy, sl)

    def experts_both(l, ds, y, sl):
        ds2 = split(ds)
        total, dy = None, None
        for e in range(experts):
            gated, part = expert_back(l, e, y, ds2, sl)
            dy = part if dy is None else dy + part
            part = down_of(l, e, gated)
            total = part if total is None else total + part
        return total, gates_back(l, ds, dy, sl)

    def self_read_back(l, ds, sl):
        ds2 = split(ds)
        dmix = k3(w_outb[l, 1], ds2)
        acc_wo[l, 1] += outer(get(mixs, l, sl), ds2)
        back = k3(kv_n[l, funcs], split(dmix))
        q2 = get(qs, l, sl)
        q = whole(q2)
        rden = rden_ref[l, :, sl]
        u = rden * rden * head_sum(q * back)
        dq = dmix + spread(rden) * back - wide(z_col[l, funcs], sl.size) * spread(u)
        put(dzq, 0, sl, split(softmax_back(q, dq)))
        da = split(dmix * spread(rden))
        u2 = split(u)
        r = nt(rows(*da, *u2), rows(*q2))
        acc_kv[:d, :] += r[:d, :d] + (r[:d, d:] + r[d : 2 * d, :d])
        low = r[2 * d :, :d] + r[2 * d :, d:]
        acc_kv[d:, :] += low[:8] + low[8:]

    def back_row(x):
        return jnp.broadcast_to(-jnp.sum(x * head_mask, axis=0, keepdims=True), (HEADS, d))

    def send_self_back(l):
        at = layers + l
        src_s[at, :HEAD_DIM, :] = compact(acc_kv[:d, :])
        src_s[at, HEAD_DIM:, :] = back_row(acc_kv[d:, :])
        send_off(own, at)

    def self_total_back(l):
        unpack(collect(own, layers + l), dkv_t, dkv_n, dz_col, 0)

    def attention_back(l, ds, sl):
        k2, v2 = get(ks, l, sl), get(vs, l, sl)
        dk = k3(dkv_n[0], v2) + wide(dz_col[0], sl.size)
        dv = split(k3(dkv_t[0], k2))
        dzk = split(softmax_back(whole(k2), dk))
        q2 = get(dzq, 0, sl)
        dz = (rows(q2[0], dzk[0], dv[0]), rows(q2[1], dzk[1], dv[1]))
        y2 = get(y_ref, l * 3 + 1, sl)
        acc_wi[l, 3 * d :, :] += outer(dz, y2)
        dy = d3(w_self[l, :, : 3 * d], w_self[l, :, 3 * d :], dz)
        return ds + norm_out(l, 1, dy, sl)

    def cross_read_back(l, ds, sl):
        ds2 = split(ds)
        dmix = k3(w_outb[l, 0], ds2)
        acc_wo[l, 0] += outer(get(mixc, l, sl), ds2)
        back = k3(kv_n[l, :funcs].reshape(funcs * d, 3 * d), split(dmix))
        q2 = get(qc, l, sl)
        q = whole(q2)
        dq = dmix
        da, us = [], []
        for f in range(funcs):
            inv = inv_ref[l, f * 8 : (f + 1) * 8, sl]
            rden = inv_ref[l, (funcs + f) * 8 : (funcs + f + 1) * 8, sl]
            back_f = back[f * d : (f + 1) * d]
            u = inv * rden * head_sum(q * back_f)
            dq = dq + spread(inv) * back_f - wide(z_col[l, f], sl.size) * spread(u)
            da.append(dmix * spread(inv))
            us.append(u)
        if funcs % 2:
            us.append(jnp.zeros_like(us[0]))
        side = rows(*us)
        m = funcs * d
        r = nt(rows(*split(rows(*da)), *split(side)), rows(*q2))
        acc_dkvc[:m, :] += r[:m, :d] + (r[:m, d:] + r[m : 2 * m, :d])
        low = r[2 * m :, :d] + r[2 * m :, d:]
        high = side.shape[0]
        acc_dkvc[m:, :] += (low[:high] + low[high:])[: 8 * funcs]
        return softmax_back(q, dq)

    def cross_query_back(l, ds, dz, sl):
        dz2 = split(dz)
        acc_wi[l, :d, :] += outer(dz2, get(y_ref, l * 3, sl))
        return ds + norm_out(l, 0, k3(w_qc[l], dz2), sl)

    def send_cross_back(l):
        at = layers + l
        for f in range(funcs):
            src_c[at, f * MSG : f * MSG + HEAD_DIM, :] = compact(acc_dkvc[f * d : (f + 1) * d, :])
            src_c[at, f * MSG + HEAD_DIM : (f + 1) * MSG, :] = back_row(
                acc_dkvc[funcs * d + f * 8 : funcs * d + (f + 1) * 8, :]
            )
        send_off(cross, at)

    def cross_keys_back(l):
        total = collect(cross, layers + l)
        for f in range(funcs):
            unpack(total[f * MSG : (f + 1) * MSG], dkv_t, dkv_n, dz_col, f)
        for f in range(funcs):
            k2 = get(kc, l * funcs + f, slice(None))
            v2 = get(vc, l * funcs + f, slice(None))
            dk = k3(dkv_n[f], v2) + wide(dz_col[f], points)
            dv = split(k3(dkv_t[f], k2))
            dzk = split(softmax_back(whole(k2), dk))
            both = fp[f]
            part = outer(
                (rows(dzk[0], dv[0]), rows(dzk[1], dv[1])), (both[:d], both[d:])
            )
            if f == 0:
                acc_wi[l, d : 3 * d, :] = part
            else:
                acc_wi[l, d : 3 * d, :] += part

    def each_tile(body, tile=TILE, ticks=()):
        tile = min(tile, count)
        if tile == count:
            body(pl.ds(0, count))
            return

        moves = [(at, take()) for at in ticks]

        def step(i, carry):
            for at, move in moves:
                pl.when(i == at)(move)
            body(pl.ds(pl.multiple_of(i * tile, tile), tile))
            return carry

        lax.fori_loop(0, count // tile, step, 0)

    exact = functools.partial(
        lax.dot_general, precision=lax.Precision.HIGHEST, preferred_element_type=F32
    )

    def finish_in(l, a, j):
        at = a * 3 + j
        g_att[l * 2 + a, j * d : (j + 1) * d, :] = exact(
            acc_wi[l, at * d : (at + 1) * d, :], perm, (((0,), (0,)), ((), ()))
        )

    def finish_out(l, a):
        g_att[l * 2 + a, 3 * d :, :] = exact(perm, acc_wo[l, a], (((0,), (0,)), ((), ())))

    for ref in (acc_wi, acc_wo, acc_g, acc_r):
        ref[...] = jnp.zeros_like(ref)
    acc_kv[...] = jnp.zeros_like(acc_kv)
    acc_dkvc[...] = jnp.zeros_like(acc_dkvc)
    pl.semaphore_wait(barrier, len(partners))
    cross_summary(0)

    features_load.wait()

    def first(sl):
        s = out[0, sl, :].T
        stream[:, sl] = s
        cross_query(0, s, sl)
        place = coords[0, :, sl]
        for l in range(layers):
            logit = [
                place[0:1] * router[l, 0, e] + place[1:2] * router[l, 1, e] for e in range(experts)
            ]
            top = functools.reduce(jnp.maximum, logit)
            grown = [jnp.exp(x - top) for x in logit]
            total = functools.reduce(jnp.add, grown)
            for e in range(experts):
                gates[l, e : e + 1, sl] = grown[e] / total

    each_tile(first)
    cut_experts()
    for ref in (g_up, g_down):
        ref[...] = jnp.zeros_like(ref)
    cross_summary(1)
    cross_total(0)
    each_tile(lambda sl: cross_read(0, stream[:, sl], sl))
    send_self(0)
    cross_total(1)
    acc_kv[...] = jnp.zeros_like(acc_kv)
    self_total(0)

    def second(sl):
        s, y = self_read(0, stream[:, sl], sl)
        s = s + run_experts(0, y, sl)
        cross_query(1, s, sl)
        cross_read(1, s, sl)

    each_tile(second)
    send_self(1)
    acc_kv[...] = jnp.zeros_like(acc_kv)
    self_total(1)

    cot_load.wait()

    def third(sl):
        s, y = self_read(1, stream[:, sl], sl)
        ds = fgrad[0, sl, :].T
        more, ds = experts_both(1, ds, y, sl)
        out[0, sl, :] = (s + more).T
        self_read_back(1, ds, sl)
        stream[:, sl] = ds

    each_tile(third)
    send_self_back(1)
    reduce_pair(1, 0)
    reduce_pair(1, 1)
    tick()
    acc_kv[...] = jnp.zeros_like(acc_kv)
    self_total_back(1)
    tick()

    def fourth(sl):
        ds = attention_back(1, stream[:, sl], sl)
        dz = cross_read_back(1, ds, sl)
        stream[:, sl] = cross_query_back(1, ds, dz, sl)

    each_tile(fourth, ticks=(1,))
    tick()

    for pair in range(experts // 2):

        def experts_of(sl, pair=pair):
            ds2 = split(stream[:, sl])
            y = get(y_ref, 2, sl)
            dy = None
            for e in (2 * pair, 2 * pair + 1):
                _, part = expert_back(0, e, y, ds2, sl)
                dy = part if dy is None else dy + part
            dy_ref[:, sl] = dy if pair == 0 else dy_ref[:, sl] + dy

        each_tile(experts_of, ticks=(1,))
        reduce_pair(0, pair)
        tick()

    def fifth(sl):
        ds = gates_back(0, stream[:, sl], dy_ref[:, sl], sl)
        self_read_back(0, ds, sl)
        stream[:, sl] = ds

    each_tile(fifth)
    send_self_back(0)
    send_cross_back(1)
    tick()
    acc_dkvc[...] = jnp.zeros_like(acc_dkvc)
    for j in range(3):
        finish_in(1, 1, j)
    finish_out(1, 1)
    finish_out(1, 0)
    reduce_att(1, 1)
    finish_in(1, 0, 0)
    tick()
    cross_keys_back(1)
    finish_in(1, 0, 1)
    finish_in(1, 0, 2)
    reduce_att(1, 0)
    self_total_back(0)
    tick()

    def sixth(sl):
        ds = attention_back(0, stream[:, sl], sl)
        stream[:, sl] = ds
        dy_ref[:, sl] = cross_read_back(0, ds, sl)

    each_tile(sixth, ticks=(1,))
    send_cross_back(0)
    tick()
    for j in range(3):
        finish_in(0, 1, j)
    finish_out(0, 1)
    reduce_att(0, 1)
    tick()

    def seventh(sl):
        fgrad[0, sl, :] = cross_query_back(0, stream[:, sl], dy_ref[:, sl], sl).T

    each_tile(seventh)
    tick()
    finish_out(0, 0)
    finish_in(0, 0, 0)
    cross_keys_back(0)
    finish_in(0, 0, 1)
    finish_in(0, 0, 2)
    reduce_att(0, 0)
    g_small[...] = jnp.zeros_like(g_small)
    for at in range(layers * 3):
        g_small[at : at + 1, :] = jnp.sum(acc_g[at].T, axis=0, keepdims=True)
    for l in range(layers):
        at = 8 * (l + 1)
        g_small[at : at + 8, :] = acc_r[l]
    if summed:
        running.append(exchange_small(g_small, f_small, *ring[10:13]))
    while running:
        tick()


def on_device(
    n_dp,
    n_blk,
    features,
    func_points,
    coords,
    presence,
    valid_rows,
    norm_gain,
    in_proj,
    out_proj,
    router,
    expert_up,
    expert_down,
    cotangent,
):
    layers, experts, d, hid = expert_up.shape
    pairs = layers * 2
    summed = n_dp % 2 == 0 and n_blk % 2 == 0 and (2 * d) % (8 * n_dp * n_blk) == 0
    count = features.shape[1]
    funcs, points = func_points.shape[1], func_points.shape[2]
    wide_hid = experts * hid
    shape = jax.ShapeDtypeStruct
    vmem = pl.BlockSpec(memory_space=pltpu.VMEM)
    smem = pl.BlockSpec(memory_space=pltpu.SMEM)
    far = pl.BlockSpec(memory_space=pl.ANY)
    pair = pltpu.VMEM((layers, 2 * d, count), BF16)
    up_shape, row_shape = (2 * d, hid), (4 * d, d)
    scratch = [
        pltpu.VMEM(func_points.shape, F32),
        pltpu.SemaphoreType.DMA((4 * layers + 5,)),
        pltpu.VMEM(((pairs,) + row_shape) if summed else (8, 128), F32),
        pltpu.VMEM(((pairs,) + up_shape) if summed else (8, 128), F32),
        pltpu.VMEM(((pairs,) + row_shape) if summed else (8, 128), F32),
        pltpu.VMEM((32, 128), F32),
        pltpu.VMEM((layers, 6 * d, 3 * d), BF16),
        pltpu.VMEM((layers, d, 3 * d), BF16),
        pltpu.VMEM((layers, d, 6 * d), BF16),
        pltpu.VMEM((layers, 2, d, 3 * d), BF16),
        pltpu.VMEM((layers, 2, d, 3 * d), BF16),
        pltpu.VMEM((layers, wide_hid, 3 * d), BF16),
        pltpu.VMEM((layers, d, 2 * wide_hid), BF16),
        pltpu.VMEM((layers, d, 2 * wide_hid), BF16),
        pltpu.VMEM((layers, wide_hid, 3 * d), BF16),
        pltpu.VMEM((layers * 3, d, 128), F32),
        pltpu.VMEM((layers * 3, d, 128), F32),
        pltpu.VMEM((funcs, 2 * d, points), BF16),
        pltpu.VMEM((layers * funcs, 2 * d, points), BF16),
        pltpu.VMEM((layers * funcs, 2 * d, points), BF16),
        pltpu.VMEM((d, count), F32),
        pltpu.VMEM((layers * 3, 2 * d, count), BF16),
        pltpu.VMEM((layers * 3, 8, count), F32),
        pair,
        pair,
        pair,
        pair,
        pair,
        pair,
        pltpu.VMEM((1, 2 * d, count), BF16),
        pltpu.VMEM((layers, 2 * funcs * HEADS, count), F32),
        pltpu.VMEM((layers, HEADS, count), F32),
        pltpu.VMEM((layers, experts, count), F32),
        pltpu.VMEM((layers, funcs + 1, d, 3 * d), BF16),
        pltpu.VMEM((layers, funcs + 1, d, 3 * d), BF16),
        pltpu.VMEM((layers, funcs + 1, d, 128), F32),
        pltpu.VMEM((funcs, d, 3 * d), BF16),
        pltpu.VMEM((funcs, d, 3 * d), BF16),
        pltpu.VMEM((funcs, d, 128), F32),
        pltpu.VMEM((d + HEADS, d), F32),
        pltpu.VMEM((funcs * (d + HEADS), d), F32),
        pltpu.VMEM((layers, 6 * d, d), F32),
        pltpu.VMEM((layers, 2, d, d), F32),
        pltpu.VMEM((layers * 3, d, 128), F32),
        pltpu.VMEM((layers, 2 * experts, 128), F32),
        pltpu.VMEM((d, count), F32),
        pltpu.VMEM((experts, count), F32),
        pltpu.VMEM((2 * layers, funcs * MSG, d), F32),
        pltpu.VMEM((2 * layers, n_blk - 1, funcs * MSG, d), F32),
        pltpu.VMEM((2 * layers, MSG, d), F32),
        pltpu.VMEM((2 * layers, n_blk - 1, MSG, d), F32),
    ] + [pltpu.SemaphoreType.DMA((2 * layers, n_blk - 1))] * 4
    if summed:
        n_flat, n_line = n_dp, n_blk // 2
        moves = 2 + 2 * (n_flat - 1) + 2 * (n_line - 1)
        for segs, (high, width) in ((pairs, up_shape), (2 * pairs, row_shape)):
            scratch += [
                pltpu.VMEM((segs, high // 2, width), F32),
                pltpu.VMEM((segs, n_flat - 1, high // 2 // n_flat, width), F32),
                pltpu.VMEM((segs, n_line - 1, high // 2 // n_flat // n_line, width), F32),
                pltpu.SemaphoreType.DMA((segs, moves)),
                pltpu.SemaphoreType.DMA((segs, moves)),
            ]
        few = n_flat + n_line - 1
        scratch += [
            pltpu.VMEM((2 + n_flat + n_line, 32, 128), F32),
            pltpu.SemaphoreType.DMA((few,)),
            pltpu.SemaphoreType.DMA((few,)),
        ]
    results = pl.pallas_call(
        functools.partial(device_kernel, n_dp, n_blk, summed),
        out_shape=[
            shape(features.shape, F32),
            shape(features.shape, F32),
            shape((pairs,) + row_shape, F32),
            shape((pairs,) + up_shape, F32),
            shape((pairs,) + row_shape, F32),
            shape((32, 128), F32),
        ],
        in_specs=[far, far, vmem, smem, smem, vmem, far, far, smem, far, far, far],
        out_specs=[vmem] * 6,
        scratch_shapes=scratch,
        compiler_params=pltpu.CompilerParams(
            collective_id=0, has_side_effects=True, vmem_limit_bytes=62 * 2**20
        ),
        name="gnot",
    )(
        features,
        func_points,
        coords,
        presence,
        valid_rows,
        norm_gain,
        in_proj.reshape(pairs, 3 * d, d),
        out_proj.reshape(pairs, d, d),
        router,
        expert_up.reshape((pairs,) + up_shape),
        expert_down.reshape((pairs,) + row_shape),
        cotangent,
    )
    y, dx, *grads = results
    if not summed:
        grads = lax.psum(grads, ("dp", "blk"))
    att_g, up_g, down_g, small = grads
    att_g = att_g.reshape(layers, 2, 4, d, d)
    return (
        y,
        dx,
        small[: layers * 3].reshape(norm_gain.shape),
        att_g[:, :, :3],
        att_g[:, :, 3],
        jnp.sum(small[8 : 8 * (layers + 1)], axis=-1).reshape(router.shape),
        up_g.reshape(expert_up.shape),
        down_g.reshape(expert_down.shape),
    )


def solution(mesh):
    placed = (
        P("dp", "blk", None),
        P("dp", None, "blk", None),
        P("dp", None, "blk"),
        P("dp", None),
        P("dp", None, None),
        P(),
        P(),
        P(),
        P(),
        P(),
        P(),
        P("dp", "blk", None),
    )
    return jax.shard_map(
        functools.partial(on_device, mesh.shape["dp"], mesh.shape["blk"]),
        mesh=mesh,
        in_specs=placed,
        out_specs=(P("dp", "blk", None), P("dp", "blk", None), P(), P(), P(), P(), P(), P()),
        check_vma=False,
    )
```

```python
import functools
import math

import jax
import jax.numpy as jnp
from jax import lax
from jax.experimental import pallas as pl
from jax.experimental.pallas import tpu as pltpu
from jax.sharding import PartitionSpec as P

MESH = pl.DeviceIdType.MESH
F32 = jnp.float32
BF16 = jnp.bfloat16
HEADS = 8
HEAD_DIM = 16
EPS = 1e-05
C1 = math.sqrt(2.0 / math.pi)
C2 = C1 * 0.044715
TILE = 1024
MSG = 24


def nn(a, b):
    return jnp.dot(a, b, preferred_element_type=F32)


def nt(a, b):
    return lax.dot_general(a, b, (((1,), (1,)), ((), ())), preferred_element_type=F32)


def tn(a, b):
    return lax.dot_general(a, b, (((0,), (0,)), ((), ())), preferred_element_type=F32)


def split(x):
    high = x.astype(BF16)
    return high, (x - high.astype(F32)).astype(BF16)


def rows(*parts):
    return jnp.concatenate(parts, axis=0)


def cols(*parts):
    return jnp.concatenate(parts, axis=1)


def triple(w):
    high, low = split(w)
    return cols(high, low, high)


def k3(w3, x):
    high, low = x
    return nn(w3, rows(high, high, low))


def d3(w_high, w_low, x):
    high, low = x
    return nn(w_high, high) + (nn(w_low, high) + nn(w_high, low))


def outer(a, b):
    m, n = a[0].shape[0], b[0].shape[0]
    r = nt(rows(*a), rows(*b))
    return r[:m, :n] + (r[:m, n:] + r[m:, :n])


def wide(column, t):
    return cols(*([column] * (t // 128)))


def lanes(x):
    total = x[:, :128]
    for at in range(128, x.shape[1], 128):
        total = total + x[:, at : at + 128]
    return total


def by_head(x):
    return x.reshape(HEAD_DIM, HEADS, x.shape[-1])


def head_sum(x):
    return jnp.sum(by_head(x), axis=0)


def spread(r):
    return jnp.broadcast_to(r[None], (HEAD_DIM,) + r.shape).reshape(HEAD_DIM * HEADS, r.shape[-1])


def head_softmax(z):
    z = by_head(z)
    e = jnp.exp(z - jnp.max(z, axis=0)[None])
    p = e * (1.0 / jnp.sum(e, axis=0))[None]
    return p.reshape(HEAD_DIM * HEADS, p.shape[-1])


def softmax_back(p, dp):
    return p * (dp - spread(head_sum(p * dp)))


def mean(x):
    return jnp.sum(x, axis=0, keepdims=True) * (1.0 / x.shape[0])


def layer_norm(s, gain):
    centred = s - mean(s)
    r = lax.rsqrt(mean(centred * centred) + EPS)
    return centred * r * gain, r


def norm_back(dy, y, r, gain, inv_gain):
    xhat = y * inv_gain
    v = gain * dy
    return r * (v - mean(v) - xhat * mean(v * xhat)), dy * xhat


def put(ref, at, sl, x):
    d = x[0].shape[0]
    ref[at, 0:d, sl] = x[0]
    ref[at, d : 2 * d, sl] = x[1]


def get(ref, at, sl):
    both = ref[at, :, sl]
    d = both.shape[0] // 2
    return both[:d], both[d:]


def whole(x):
    return x[0].astype(F32) + x[1].astype(F32)


def gelu_parts(v):
    v2 = v * v
    g = 0.5 + 0.5 * jnp.tanh(v * (C1 + C2 * v2))
    return v2, g


def device_kernel(
    n_dp,
    n_blk,
    summed,
    features_hbm,
    points_hbm,
    coords,
    presence,
    valid,
    gain,
    in_hbm,
    out_hbm,
    router,
    up_hbm,
    down_hbm,
    cot_hbm,
    out,
    fgrad,
    f_in,
    f_out,
    f_up,
    f_down,
    f_gain,
    f_router,
    points_ref,
    load_sem,
    g_in,
    g_out,
    g_up,
    g_down,
    g_early,
    f_early,
    g_small,
    f_small,
    w_in,
    w_qc,
    w_self,
    w_out,
    w_outb,
    up_t,
    up_n,
    down_t,
    down_n,
    gcol,
    rgcol,
    fp,
    kc,
    vc,
    stream,
    y_ref,
    r_ref,
    qc,
    mixc,
    qs,
    ks,
    vs,
    mixs,
    hold,
    inv_ref,
    rden_ref,
    gates,
    kv_t,
    kv_n,
    z_col,
    dkv_t,
    dkv_n,
    dz_col,
    acc_kv,
    acc_dkvc,
    acc_wi,
    acc_wo,
    acc_g,
    acc_r,
    dy_ref,
    dgate_ref,
    src_c,
    got_c,
    src_s,
    got_s,
    send_c,
    recv_c,
    send_s,
    recv_s,
    *ring,
):
    if not summed:
        g_in, g_out, g_up, g_down = f_in, f_out, f_up, f_down
    layers, experts, hid = router.shape[0], router.shape[2], up_hbm.shape[2]
    funcs, points = points_hbm.shape[1], points_hbm.shape[2]
    count, d = features_hbm.shape[1:]

    def load(src, dst, at):
        copy = pltpu.make_async_copy(src, dst, load_sem.at[at])
        copy.start()
        return copy

    in_load = load(in_hbm, f_in, 0)
    out_load = load(out_hbm, f_out, 1)
    at = 2
    points_load = load(points_hbm, points_ref, at)
    features_load = load(features_hbm, out, at + 1)
    up_load = load(up_hbm, f_up, at + 2)
    down_load = load(down_hbm, f_down, at + 3)
    cot_load = load(cot_hbm, fgrad, at + 4)
    me = lax.axis_index("blk")
    own_dp = lax.axis_index("dp")
    n_flat, n_line = n_dp, n_blk // 2
    core, line = own_dp % 2, me // 2
    flat = (own_dp // 2) * 2 + me % 2

    sibling = {"dp": own_dp - core + (1 - core), "blk": me}

    def flat_at(j):
        at = lax.rem(flat + j, n_flat)
        return {"dp": (at // 2) * 2 + core, "blk": line * 2 + at % 2}

    def line_at(j):
        return {"dp": own_dp, "blk": lax.rem(line + j, n_line) * 2 + me % 2}

    def group_at(j):
        at = lax.rem(flat * 2 + core + j, 2 * n_flat)
        spot = at // 2
        return {"dp": (spot // 2) * 2 + at % 2, "blk": line * 2 + spot % 2}

    partners = [{"dp": own_dp, "blk": lax.rem(me + j, n_blk)} for j in range(1, n_blk)]
    if summed:
        partners += [group_at(j) for j in range(1, 2 * n_flat)]
    barrier = pltpu.get_barrier_semaphore()
    for partner in partners:
        pl.semaphore_signal(barrier, inc=1, device_id=partner, device_id_type=MESH)

    sums = {}

    def take(names):
        now = [steps.pop(0) for name in names.split() for steps in sums.get(name, ()) if steps]

        def run():
            for step in now:
                step()

        return run

    def advance(names):
        take(names)()

    def made(jobs, send, recv):
        return [
            pltpu.make_async_remote_copy(
                src_ref=src,
                dst_ref=dst,
                send_sem=send.at[k],
                recv_sem=recv.at[k],
                device_id=device,
                device_id_type=MESH,
            )
            for k, src, dst, device in jobs()
        ]

    def go(jobs, send, recv):
        for copy in made(jobs, send, recv):
            copy.start()

    def settle(jobs, send, recv):
        for copy in made(jobs, send, recv):
            copy.wait()

    def reduction(local, final, halves, parts, pieces, send, recv):
        half = local.shape[0] // 2
        part = half // n_flat
        piece = part // n_line

        def at(start, size):
            return pl.ds(pl.multiple_of(start, 8), size)

        def of_core(other=0):
            return at((core if not other else 1 - core) * half, half)

        def of_flat(j=0):
            return at(core * half + lax.rem(flat + j, n_flat) * part, part)

        def of_line(j=0):
            return at(core * half + flat * part + lax.rem(line + j, n_line) * piece, piece)

        k1 = 1
        k2 = k1 + n_flat - 1
        k3_ = k2 + n_line - 1
        k4 = k3_ + n_line - 1
        k5 = k4 + n_flat - 1

        def core_out():
            return [(0, local.at[of_core(1)], halves, sibling)]

        def flat_out():
            return [
                (k1 + j - 1, local.at[of_flat(j)], parts.at[j - 1], flat_at(j))
                for j in range(1, n_flat)
            ]

        def line_out():
            return [
                (k2 + j - 1, local.at[of_line(j)], pieces.at[j - 1], line_at(j))
                for j in range(1, n_line)
            ]

        def line_back():
            mine = final.at[of_line()]
            return [(k3_ + j - 1, mine, mine, line_at(j)) for j in range(1, n_line)]

        def flat_back():
            mine = final.at[of_flat()]
            return [(k4 + j - 1, mine, mine, flat_at(j)) for j in range(1, n_flat)]

        def core_back():
            mine = final.at[of_core()]
            return [(k5, mine, mine, sibling)]

        def one():
            go(core_out, send, recv)

        def two():
            settle(core_out, send, recv)
            spot = of_core()
            local[spot] = local[spot] + halves[...]
            go(flat_out, send, recv)

        def three():
            settle(flat_out, send, recv)
            spot = of_flat()
            total = local[spot]
            for j in range(n_flat - 1):
                total = total + parts[j]
            local[spot] = total
            go(line_out, send, recv)

        def four():
            settle(line_out, send, recv)
            spot = of_line()
            total = local[spot]
            for j in range(n_line - 1):
                total = total + pieces[j]
            final[spot] = total
            go(line_back, send, recv)

        def five():
            settle(line_back, send, recv)
            go(flat_back, send, recv)

        def six():
            settle(flat_back, send, recv)
            go(core_back, send, recv)

        def seven():
            settle(core_back, send, recv)

        return [one, two, three, four, five, six, seven]

    def quick(local, final, parts, held, send, recv):
        group = 2 * n_flat
        size = local.shape[0] // group
        place = flat * 2 + core

        def piece(j):
            return pl.ds(pl.multiple_of(lax.rem(place + j, group) * size, 8), size)

        def out_jobs():
            return [
                (j - 1, local.at[piece(j)], parts.at[j - 1], group_at(j)) for j in range(1, group)
            ]

        def line_jobs():
            mine = held.at[line]
            return [(group + j - 2, mine, mine, line_at(j)) for j in range(1, n_line)]

        def back_jobs():
            mine = final.at[piece(0)]
            return [(group + n_line + j - 3, mine, mine, group_at(j)) for j in range(1, group)]

        def one():
            go(out_jobs, send, recv)

        def two():
            settle(out_jobs, send, recv)
            total = local[piece(0)]
            for j in range(group - 1):
                total = total + parts[j]
            held[line] = total
            go(line_jobs, send, recv)

        def three():
            settle(line_jobs, send, recv)
            total = held[0]
            for j in range(1, n_line):
                total = total + held[j]
            final[piece(0)] = total
            go(back_jobs, send, recv)

        def four():
            settle(back_jobs, send, recv)

        return [one, two, three, four]

    def exchange_small(local, final, held, send, recv):
        levels = (
            (0, 2, core, lambda: [sibling], 0),
            (2, n_flat, flat, lambda: [flat_at(j) for j in range(1, n_flat)], 1),
            (2 + n_flat, n_line, line, lambda: [line_at(j) for j in range(1, n_line)], n_flat),
        )

        def jobs_of(level):
            at, _, place, devices, k = levels[level]

            def jobs():
                mine = held.at[at + place]
                return [(k + j, mine, mine, device) for j, device in enumerate(devices())]

            return jobs

        def start(level, value):
            at, _, place, _, _ = levels[level]
            held[at + place] = value
            go(jobs_of(level), send, recv)

        def finish(level):
            settle(jobs_of(level), send, recv)
            at, size = levels[level][:2]
            value = held[at]
            for j in range(1, size):
                value = value + held[at + j]
            return value

        def last():
            final[...] = finish(2)

        return [
            lambda: start(0, local[...]),
            lambda: start(1, finish(0)),
            lambda: start(2, finish(1)),
            last,
        ]

    def begin(name, steps):
        if summed:
            sums.setdefault(name, []).append(steps)

    def reduce(name, seg, local, final):
        if summed:
            begin(name, reduction(local, final, *ring[5 * seg : 5 * seg + 5]))

    def reduce_quick(name, at, local, final):
        if summed:
            start = 5 * (4 * layers + 2) + 4 * at
            begin(name, quick(local, final, *ring[start : start + 4]))

    def reduce_pair(name, l, pair):
        seg = l * 2 + pair
        reduce(name, 2 * seg, g_up.at[seg], f_up.at[seg])
        reduce(name, 2 * seg + 1, g_down.at[seg], f_down.at[seg])

    def copies(src, got, send, recv, at):
        return [
            pltpu.make_async_remote_copy(
                src_ref=src.at[at],
                dst_ref=got.at[at, j - 1],
                send_sem=send.at[at, j - 1],
                recv_sem=recv.at[at, j - 1],
                device_id={"blk": lax.rem(me + j, n_blk)},
                device_id_type=MESH,
            )
            for j in range(1, n_blk)
        ]

    def send_off(refs, at):
        for copy in copies(*refs, at):
            copy.start()

    def collect(refs, at):
        for copy in copies(*refs, at):
            copy.wait()
        src, got = refs[0], refs[1]
        total = src[at]
        for j in range(n_blk - 1):
            total = total + got[at, j]
        return total

    cross = (src_c, got_c, send_c, recv_c)
    own = (src_s, got_s, send_s, recv_s)

    head_mask = (
        lax.broadcasted_iota(jnp.int32, (HEADS, d), 0)
        == lax.broadcasted_iota(jnp.int32, (HEADS, d), 1) % HEADS
    ).astype(F32)
    spot = lax.broadcasted_iota(jnp.int32, (d, d), 0)
    perm = (
        lax.broadcasted_iota(jnp.int32, (d, d), 1) == (spot % HEADS) * HEAD_DIM + spot // HEADS
    ).astype(F32)
    perm16 = perm.astype(BF16)

    def compact(full):
        return jnp.sum(full.reshape(HEAD_DIM, HEADS, d) * head_mask[None], axis=1)

    def expand(compacted):
        full = jnp.broadcast_to(compacted[:, None, :], (HEAD_DIM, HEADS, d)) * head_mask[None]
        return full.reshape(d, d)

    def unpack(total, t_ref, n_ref, c_ref, at):
        full = expand(total[:HEAD_DIM])
        t_ref[at] = triple(full)
        n_ref[at] = triple(full.T)
        c_ref[at] = rows(*([total[HEAD_DIM:MSG]] * HEAD_DIM)).T

    def cut_attention(l, a):
        for j in range(3):
            at = a * 3 + j
            w_high, w_low = split(f_in[l, at * d : (at + 1) * d, :])
            high = nt(perm16, w_high).astype(BF16)
            low = nt(perm16, w_low).astype(BF16)
            w_in[l, at * d : (at + 1) * d, :] = cols(high, low, high)
            if (a, j) == (0, 0) or a == 1:
                high = nt(w_high, perm16).astype(BF16)
                low = nt(w_low, perm16).astype(BF16)
                if a == 0:
                    w_qc[l] = cols(high, low, high)
                else:
                    w_self[l, :, j * d : (j + 1) * d] = high
                    w_self[l, :, (3 + j) * d : (4 + j) * d] = low

    def cut_out(l, a):
        w_high, w_low = split(f_out[l, a * d : (a + 1) * d, :])
        contract = (((0,), (1,)), ((), ()))
        high, low = [
            lax.dot_general(w, perm16, contract, preferred_element_type=F32).astype(BF16)
            for w in (w_high, w_low)
        ]
        w_out[l, a] = cols(high, low, high)
        high = nn(perm16, w_high).astype(BF16)
        low = nn(perm16, w_low).astype(BF16)
        w_outb[l, a] = cols(high, low, high)

    def cut_experts(l):
        for e in range(experts):
            lo, hi = e * hid, (e + 1) * hid
            seg, spot = l * 2 + e // 2, e % 2
            w = f_up[seg, spot * d : (spot + 1) * d, :]
            high, low = split(w)
            up_n[l, :, lo:hi] = high
            up_n[l, :, experts * hid + lo : experts * hid + hi] = low
            up_t[l, lo:hi, :] = triple(w.T)
            w = f_down[seg, spot * hid : (spot + 1) * hid, :]
            down_n[l, lo:hi, :] = triple(w)
            high, low = split(w.T)
            down_t[l, :, lo:hi] = high
            down_t[l, :, experts * hid + lo : experts * hid + hi] = low

    def cut_gains(l):
        for j in range(3):
            column = jnp.broadcast_to(gain[j, l : l + 1, :], (d, d)).T
            gcol[l * 3 + j] = column
            rgcol[l * 3 + j] = 1.0 / column

    present = [presence[0, f].astype(F32) for f in range(funcs)]
    all_present = present[0]
    for f in range(1, funcs):
        all_present = all_present + present[f]
    weight = [
        jnp.full((1, 1), present[f], F32) / jnp.full((1, 1), all_present, F32) for f in range(funcs)
    ]

    ones = jnp.ones((16, points), BF16)

    def cross_summary(l):
        for f in range(funcs):
            both = fp[f]
            z = k3(w_in[l, d : 3 * d, :], (both[:d], both[d:]))
            kept = (
                lax.broadcasted_iota(jnp.int32, (1, points), 1) < valid[f, 0, me]
            ).astype(F32)
            k = split(head_softmax(z[:d]) * kept)
            v = split(z[d:])
            put(kc, l * funcs + f, slice(None), k)
            put(vc, l * funcs + f, slice(None), v)
            r = nt(rows(*v, ones), rows(*k))
            src_c[l, f * MSG : f * MSG + HEAD_DIM, :] = compact(
                r[:d, :d] + (r[:d, d:] + r[d : 2 * d, :d])
            )
            src_c[l, f * MSG + HEAD_DIM : (f + 1) * MSG, :] = (
                r[2 * d : 2 * d + 8, :d] + r[2 * d : 2 * d + 8, d:]
            )
        send_off(cross, l)

    def cross_total(l):
        total = collect(cross, l)
        for f in range(funcs):
            unpack(
                total[f * MSG : (f + 1) * MSG],
                kv_t.at[l],
                kv_n.at[l],
                z_col.at[l],
                f,
            )

    def self_total(l):
        unpack(collect(own, l), kv_t.at[l], kv_n.at[l], z_col.at[l], funcs)

    def norm_in(l, at, s, sl):
        y, r = layer_norm(s, wide(gcol[l * 3 + at], sl.size))
        y = split(y)
        put(y_ref, l * 3 + at, sl, y)
        r_ref[l * 3 + at, 0:1, sl] = r
        return y

    def norm_out(l, at, dy, sl):
        y = whole(get(y_ref, l * 3 + at, sl))
        ds, dg = norm_back(
            dy,
            y,
            r_ref[l * 3 + at, 0:1, sl],
            wide(gcol[l * 3 + at], sl.size),
            wide(rgcol[l * 3 + at], sl.size),
        )
        acc_g[l * 3 + at] += lanes(dg)
        return ds

    def cross_query(l, s, sl):
        y = norm_in(l, 0, s, sl)
        put(qc, l, sl, split(head_softmax(k3(w_in[l, :d, :], y))))

    def cross_read(l, s, sl):
        q2 = get(qc, l, sl)
        q = whole(q2)
        num = k3(kv_t[l, :funcs].reshape(funcs * d, 3 * d), q2)
        mix = q
        for f in range(funcs):
            rden = 1.0 / head_sum(q * wide(z_col[l, f], sl.size))
            inv = rden * weight[f]
            inv_ref[l, f * 8 : (f + 1) * 8, sl] = inv
            inv_ref[l, (funcs + f) * 8 : (funcs + f + 1) * 8, sl] = rden
            mix = mix + num[f * d : (f + 1) * d] * spread(inv)
        mix = split(mix)
        put(mixc, l, sl, mix)
        s = s + k3(w_out[l, 0], mix)
        y = norm_in(l, 1, s, sl)
        z = k3(w_in[l, 3 * d :, :], y)
        q = split(head_softmax(z[:d]))
        k = split(head_softmax(z[d : 2 * d]))
        v = split(z[2 * d :])
        put(qs, l, sl, q)
        put(ks, l, sl, k)
        put(vs, l, sl, v)
        r = nt(rows(*v, jnp.ones((16, sl.size), BF16)), rows(*k))
        acc_kv[:d, :] += r[:d, :d] + (r[:d, d:] + r[d : 2 * d, :d])
        acc_kv[d:, :] += r[2 * d : 2 * d + 8, :d] + r[2 * d : 2 * d + 8, d:]
        stream[:, sl] = s

    def send_self(l):
        src_s[l, :HEAD_DIM, :] = compact(acc_kv[:d, :])
        src_s[l, HEAD_DIM:, :] = acc_kv[d:, :]
        send_off(own, l)

    def self_read(l, s, sl):
        q2 = get(qs, l, sl)
        q = whole(q2)
        num = k3(kv_t[l, funcs], q2)
        rden = 1.0 / head_sum(q * wide(z_col[l, funcs], sl.size))
        rden_ref[l, :, sl] = rden
        mix = split(num * spread(rden) + q)
        put(mixs, l, sl, mix)
        s = s + k3(w_out[l, 1], mix)
        return s, norm_in(l, 2, s, sl)

    def hidden_in(l, e, y):
        return k3(up_t[l, e * hid : (e + 1) * hid, :], y)

    def down_of(l, e, x):
        at = experts * hid
        return d3(
            down_t[l, :, e * hid : (e + 1) * hid],
            down_t[l, :, at + e * hid : at + (e + 1) * hid],
            x,
        )

    def run_experts(l, y, sl):
        total = None
        for e in range(experts):
            v = hidden_in(l, e, y)
            _, g = gelu_parts(v)
            part = down_of(l, e, split(v * g * gates[l, e : e + 1, sl]))
            total = part if total is None else total + part
        return total

    def expert_back(l, e, y, ds2, sl):
        at = experts * hid
        gate = gates[l, e : e + 1, sl]
        v = hidden_in(l, e, y)
        back = k3(down_n[l, e * hid : (e + 1) * hid, :], ds2)
        v2, g = gelu_parts(v)
        act = v * g
        slope = g * (1.0 + (1.0 - g) * v * (2.0 * C1 + 6.0 * C2 * v2))
        dgate_ref[e : e + 1, sl] = jnp.sum(act * back, axis=0, keepdims=True)
        gated = split(act * gate)
        dpre = split(slope * back * gate)
        seg, spot = l * 2 + e // 2, e % 2
        g_down[seg, spot * hid : (spot + 1) * hid, :] += outer(gated, ds2)
        g_up[seg, spot * d : (spot + 1) * d, :] += outer(y, dpre)
        dy = d3(
            up_n[l, :, e * hid : (e + 1) * hid],
            up_n[l, :, at + e * hid : at + (e + 1) * hid],
            dpre,
        )
        return gated, dy

    def gates_back(l, ds, dy, sl):
        probs = [gates[l, e : e + 1, sl] for e in range(experts)]
        dgate = [dgate_ref[e : e + 1, sl] for e in range(experts)]
        centre = probs[0] * dgate[0]
        for e in range(1, experts):
            centre = centre + probs[e] * dgate[e]
        dlogit = rows(*[probs[e] * (dgate[e] - centre) for e in range(experts)])
        place = coords[0, :, sl]
        acc_r[l] += lanes(rows(dlogit * place[0:1], dlogit * place[1:2]))
        return ds + norm_out(l, 2, dy, sl)

    def experts_back(l, pair, sl, forward):
        ds2 = get(hold, 0, sl)
        y = get(y_ref, l * 3 + 2, sl)
        total, dy = None, None
        for e in (2 * pair, 2 * pair + 1):
            gated, part = expert_back(l, e, y, ds2, sl)
            dy = part if dy is None else dy + part
            if forward:
                part = down_of(l, e, gated)
                total = part if total is None else total + part
        dy_ref[:, sl] = dy if pair == 0 else dy_ref[:, sl] + dy
        if forward:
            stream[:, sl] += total

    def self_read_back(l, ds, sl):
        ds2 = split(ds)
        dmix = k3(w_outb[l, 1], ds2)
        acc_wo[l, 1] += outer(get(mixs, l, sl), ds2)
        back = k3(kv_n[l, funcs], split(dmix))
        q2 = get(qs, l, sl)
        q = whole(q2)
        rden = rden_ref[l, :, sl]
        u = rden * rden * head_sum(q * back)
        dq = dmix + spread(rden) * back - wide(z_col[l, funcs], sl.size) * spread(u)
        put(hold, 0, sl, split(softmax_back(q, dq)))
        da = split(dmix * spread(rden))
        u2 = split(u)
        r = nt(rows(*da, *u2), rows(*q2))
        acc_kv[:d, :] += r[:d, :d] + (r[:d, d:] + r[d : 2 * d, :d])
        low = r[2 * d :, :d] + r[2 * d :, d:]
        acc_kv[d:, :] += low[:8] + low[8:]

    def back_row(x):
        return jnp.broadcast_to(-jnp.sum(x * head_mask, axis=0, keepdims=True), (HEADS, d))

    def send_self_back(l):
        at = layers + l
        src_s[at, :HEAD_DIM, :] = compact(acc_kv[:d, :])
        src_s[at, HEAD_DIM:, :] = back_row(acc_kv[d:, :])
        send_off(own, at)

    def self_total_back(l):
        unpack(collect(own, layers + l), dkv_t, dkv_n, dz_col, 0)

    def attention_back(l, ds, sl, later=False):
        k2, v2 = get(ks, l, sl), get(vs, l, sl)
        dk = k3(dkv_n[0], v2) + wide(dz_col[0], sl.size)
        dv = split(k3(dkv_t[0], k2))
        dzk = split(softmax_back(whole(k2), dk))
        q2 = get(hold, 0, sl)
        dz = (rows(q2[0], dzk[0], dv[0]), rows(q2[1], dzk[1], dv[1]))
        if later:
            put(qs, 1, sl, dzk)
            put(ks, 1, sl, dv)
        else:
            acc_wi[l, 3 * d :, :] += outer(dz, get(y_ref, l * 3 + 1, sl))
        dy = d3(w_self[l, :, : 3 * d], w_self[l, :, 3 * d :], dz)
        return ds + norm_out(l, 1, dy, sl)

    def weights_later():
        every = pl.ds(0, count)
        parts = (get(hold, 0, every), get(qs, 1, every), get(ks, 1, every))
        dz = (rows(*[part[0] for part in parts]), rows(*[part[1] for part in parts]))
        acc_wi[0, 3 * d :, :] = outer(dz, get(y_ref, 1, every))
        acc_wo[0, 0] = outer(get(mixc, 0, every), get(vs, 1, every))

    def cross_read_back(l, ds, sl, later=False):
        ds2 = split(ds)
        dmix = k3(w_outb[l, 0], ds2)
        if later:
            put(vs, 1, sl, ds2)
        else:
            acc_wo[l, 0] += outer(get(mixc, l, sl), ds2)
        back = k3(kv_n[l, :funcs].reshape(funcs * d, 3 * d), split(dmix))
        q2 = get(qc, l, sl)
        q = whole(q2)
        dq = dmix
        da, us = [], []
        for f in range(funcs):
            inv = inv_ref[l, f * 8 : (f + 1) * 8, sl]
            rden = inv_ref[l, (funcs + f) * 8 : (funcs + f + 1) * 8, sl]
            back_f = back[f * d : (f + 1) * d]
            u = inv * rden * head_sum(q * back_f)
            dq = dq + spread(inv) * back_f - wide(z_col[l, f], sl.size) * spread(u)
            da.append(dmix * spread(inv))
            us.append(u)
        if funcs % 2:
            us.append(jnp.zeros_like(us[0]))
        side = rows(*us)
        m = funcs * d
        r = nt(rows(*split(rows(*da)), *split(side)), rows(*q2))
        acc_dkvc[:m, :] += r[:m, :d] + (r[:m, d:] + r[m : 2 * m, :d])
        low = r[2 * m :, :d] + r[2 * m :, d:]
        high = side.shape[0]
        acc_dkvc[m:, :] += (low[:high] + low[high:])[: 8 * funcs]
        return softmax_back(q, dq)

    def cross_query_back(l, ds, dz, sl):
        dz2 = split(dz)
        acc_wi[l, :d, :] += outer(dz2, get(y_ref, l * 3, sl))
        return ds + norm_out(l, 0, k3(w_qc[l], dz2), sl)

    def send_cross_back(l):
        at = layers + l
        for f in range(funcs):
            src_c[at, f * MSG : f * MSG + HEAD_DIM, :] = compact(acc_dkvc[f * d : (f + 1) * d, :])
            src_c[at, f * MSG + HEAD_DIM : (f + 1) * MSG, :] = back_row(
                acc_dkvc[funcs * d + f * 8 : funcs * d + (f + 1) * 8, :]
            )
        send_off(cross, at)

    def cross_keys_back(l):
        total = collect(cross, layers + l)
        for f in range(funcs):
            unpack(total[f * MSG : (f + 1) * MSG], dkv_t, dkv_n, dz_col, f)
        for f in range(funcs):
            k2 = get(kc, l * funcs + f, slice(None))
            v2 = get(vc, l * funcs + f, slice(None))
            dk = k3(dkv_n[f], v2) + wide(dz_col[f], points)
            dv = split(k3(dkv_t[f], k2))
            dzk = split(softmax_back(whole(k2), dk))
            both = fp[f]
            part = outer(
                (rows(dzk[0], dv[0]), rows(dzk[1], dv[1])), (both[:d], both[d:])
            )
            if f == 0:
                acc_wi[l, d : 3 * d, :] = part
            else:
                acc_wi[l, d : 3 * d, :] += part

    def each_tile(body, tile=TILE, then=()):
        tile = min(tile, count)
        if tile == count:
            body(pl.ds(0, count))
            return

        moves = [(at, take(names)) for at, names in then]

        def step(i, carry):
            for at, move in moves:
                pl.when(i == at)(move)
            body(pl.ds(pl.multiple_of(i * tile, tile), tile))
            return carry

        lax.fori_loop(0, count // tile, step, 0)

    exact = functools.partial(
        lax.dot_general, precision=lax.Precision.HIGHEST, preferred_element_type=F32
    )

    def finish_in(l, at, ref, spot):
        ref[spot : spot + d, :] = exact(
            acc_wi[l, at * d : (at + 1) * d, :], perm, (((0,), (0,)), ((), ()))
        )

    def finish_out(l, a):
        g_out[l, a * d : (a + 1) * d, :] = exact(perm, acc_wo[l, a], (((0,), (0,)), ((), ())))

    in_load.wait()
    points_load.wait()
    for f in range(funcs):
        high, low = split(points_ref[0, f].T)
        fp[f, :d, :] = high
        fp[f, d:, :] = low
    cut_attention(0, 0)
    pl.semaphore_wait(barrier, len(partners))
    cross_summary(0)

    out_load.wait()
    features_load.wait()
    cut_gains(0)

    def first(sl):
        s = out[0, sl, :].T
        stream[:, sl] = s
        cross_query(0, s, sl)

    each_tile(first)
    cut_attention(0, 1)
    cut_out(0, 0)
    cut_out(0, 1)
    acc_kv[...] = jnp.zeros_like(acc_kv)
    cross_total(0)
    each_tile(lambda sl: cross_read(0, stream[:, sl], sl))
    send_self(0)

    cut_attention(1, 0)
    cross_summary(1)
    up_load.wait()
    down_load.wait()
    cut_experts(0)

    def route(sl):
        place = coords[0, :, sl]
        for l in range(layers):
            logit = [
                place[0:1] * router[l, 0, e] + place[1:2] * router[l, 1, e] for e in range(experts)
            ]
            top = functools.reduce(jnp.maximum, logit)
            grown = [jnp.exp(x - top) for x in logit]
            total = functools.reduce(jnp.add, grown)
            for e in range(experts):
                gates[l, e : e + 1, sl] = grown[e] / total

    route(pl.ds(0, count))
    acc_kv[...] = jnp.zeros_like(acc_kv)
    self_total(0)

    def second(sl):
        s, y = self_read(0, stream[:, sl], sl)
        stream[:, sl] = s + run_experts(0, y, sl)

    each_tile(second)
    cut_gains(1)
    cut_attention(1, 1)
    cut_out(1, 0)
    cross_total(1)

    def second_cross(sl):
        s = stream[:, sl]
        cross_query(1, s, sl)
        cross_read(1, s, sl)

    each_tile(second_cross)
    send_self(1)

    cut_out(1, 1)
    cut_experts(1)
    cot_load.wait()

    def turn(sl):
        put(hold, 0, sl, split(fgrad[0, sl, :].T))

    each_tile(turn)
    for ref in (acc_wi, acc_wo, acc_g, acc_r, g_up, g_down, acc_kv, acc_dkvc):
        ref[...] = jnp.zeros_like(ref)
    self_total(1)

    def third(sl):
        stream[:, sl] = self_read(1, stream[:, sl], sl)[0]

    each_tile(third)

    def pair_loop(l, pair, then):
        each_tile(lambda sl: experts_back(l, pair, sl, l == layers - 1), then=then)

    pair_loop(1, 0, ())
    reduce_pair("a0", 1, 0)
    advance("a0")
    pair_loop(1, 1, ((1, "a0"),))
    reduce_pair("a1", 1, 1)
    advance("a1")

    def third_back(sl):
        ds = gates_back(1, whole(get(hold, 0, sl)), dy_ref[:, sl], sl)
        self_read_back(1, ds, sl)
        out[0, sl, :] = stream[:, sl].T
        stream[:, sl] = ds

    each_tile(third_back)
    send_self_back(1)
    advance("a0")
    acc_kv[...] = jnp.zeros_like(acc_kv)
    self_total_back(1)
    advance("a1")

    def fourth(sl):
        ds = attention_back(1, stream[:, sl], sl)
        dz = cross_read_back(1, ds, sl)
        ds = cross_query_back(1, ds, dz, sl)
        stream[:, sl] = ds
        put(hold, 0, sl, split(ds))

    each_tile(fourth, then=((1, "a0"),))
    send_cross_back(1)
    advance("a1")
    acc_dkvc[...] = jnp.zeros_like(acc_dkvc)
    pair_loop(0, 0, ((1, "a0"),))
    reduce_pair("b0", 0, 0)
    advance("b0 a1")
    for at in range(3, 6):
        finish_in(1, at, g_in.at[1], at * d)
    finish_out(1, 0)
    finish_out(1, 1)
    finish_in(1, 0, g_in.at[1], 0)
    cross_keys_back(1)
    finish_in(1, 1, g_in.at[1], d)
    finish_in(1, 2, g_in.at[1], 2 * d)
    reduce("c", 4 * layers, g_in.at[1], f_in.at[1])
    reduce("c", 4 * layers + 1, g_out.at[1], f_out.at[1])
    advance("c")
    pair_loop(0, 1, ((1, "a0 b0"),))
    reduce_pair("b1", 0, 1)
    advance("b1 a0 c")

    def fifth(sl):
        ds = gates_back(0, stream[:, sl], dy_ref[:, sl], sl)
        self_read_back(0, ds, sl)
        stream[:, sl] = ds

    each_tile(fifth)
    send_self_back(0)
    advance("b0")
    self_total_back(0)
    advance("a1 b1 c")

    def sixth(sl):
        ds = attention_back(0, stream[:, sl], sl, True)
        stream[:, sl] = ds
        dy_ref[:, sl] = cross_read_back(0, ds, sl, True)

    each_tile(sixth, then=((1, "b0"),))
    send_cross_back(0)

    weights_later()
    for at in range(3, 6):
        finish_in(0, at, g_early, (at - 2) * d)
    finish_out(0, 0)
    finish_out(0, 1)
    advance("b1 c a1")

    def seventh(sl):
        fgrad[0, sl, :] = cross_query_back(0, stream[:, sl], dy_ref[:, sl], sl).T

    each_tile(seventh, then=((1, "b0"),))
    finish_in(0, 0, g_early, 0)
    g_small[...] = jnp.zeros_like(g_small)
    for at in range(layers * 3):
        g_small[at : at + 1, :] = jnp.sum(acc_g[at].T, axis=0, keepdims=True)
    for l in range(layers):
        at = 8 * (l + 1)
        g_small[at : at + 8, :] = acc_r[l]
    reduce_quick("d", 1, g_early, f_early)
    reduce_quick("d", 2, g_out.at[0], f_out.at[0])
    if summed:
        begin("s", exchange_small(g_small, f_small, *ring[-3:]))
    advance("d s")
    cross_keys_back(0)
    keys = pl.ds(d, 2 * d)
    finish_in(0, 1, g_in.at[0, keys], 0)
    finish_in(0, 2, g_in.at[0, keys], d)
    reduce_quick("e", 0, g_in.at[0, keys], f_in.at[0, keys])
    while any(steps for group in sums.values() for steps in group):
        advance("e d s b1 c b0 a1 a0")
    early, small = (f_early, f_small) if summed else (g_early, g_small)
    f_in[0, :d, :] = early[:d, :]
    f_in[0, 3 * d :, :] = early[d:, :]
    for l in range(layers):
        for j in range(3):
            f_gain[j, l : l + 1, :] = small[l * 3 + j : l * 3 + j + 1, :]
    routed = jnp.sum(small[...].T, axis=0, keepdims=True)
    for l in range(layers):
        for c in range(2):
            at = 8 * (l + 1) + c * experts
            f_router[l, c : c + 1, :] = routed[:, at : at + experts]


def finish_kernel(n, *refs):
    sources, targets, held, sems = refs[:n], refs[n : 2 * n], refs[2 * n : 3 * n], refs[3 * n]
    inward = [pltpu.make_async_copy(sources[at], held[at], sems.at[0, at]) for at in range(n)]
    outward = [pltpu.make_async_copy(held[at], targets[at], sems.at[1, at]) for at in range(n)]
    for move in inward:
        move.start()
    for at in range(n):
        inward[at].wait()
        outward[at].start()
    for move in outward:
        move.wait()


def on_device(
    n_dp,
    n_blk,
    features,
    func_points,
    coords,
    presence,
    valid_rows,
    norm_gain,
    in_proj,
    out_proj,
    router,
    expert_up,
    expert_down,
    cotangent,
):
    layers, experts, d, hid = expert_up.shape
    pairs = layers * 2
    summed = n_dp % 2 == 0 and n_blk % 2 == 0 and (2 * d) % (8 * n_dp * n_blk) == 0
    count = features.shape[1]
    funcs, points = func_points.shape[1], func_points.shape[2]
    wide_hid = experts * hid
    shape = jax.ShapeDtypeStruct
    vmem = pl.BlockSpec(memory_space=pltpu.VMEM)
    smem = pl.BlockSpec(memory_space=pltpu.SMEM)
    far = pl.BlockSpec(memory_space=pl.ANY)
    pair = pltpu.VMEM((layers, 2 * d, count), BF16)
    up_shape, row_shape = (2 * d, hid), (4 * d, d)

    def local(dims):
        return pltpu.VMEM(dims if summed else (8, 128), F32)

    scratch = [
        pltpu.VMEM(func_points.shape, F32),
        pltpu.SemaphoreType.DMA((8,)),
        local((layers, 6 * d, d)),
        local((layers, 2 * d, d)),
        local((pairs,) + up_shape),
        local((pairs,) + row_shape),
        pltpu.VMEM((4 * d, d), F32),
        local((4 * d, d)),
        pltpu.VMEM((32, 128), F32),
        local((32, 128)),
        pltpu.VMEM((layers, 6 * d, 3 * d), BF16),
        pltpu.VMEM((layers, d, 3 * d), BF16),
        pltpu.VMEM((layers, d, 6 * d), BF16),
        pltpu.VMEM((layers, 2, d, 3 * d), BF16),
        pltpu.VMEM((layers, 2, d, 3 * d), BF16),
        pltpu.VMEM((layers, wide_hid, 3 * d), BF16),
        pltpu.VMEM((layers, d, 2 * wide_hid), BF16),
        pltpu.VMEM((layers, d, 2 * wide_hid), BF16),
        pltpu.VMEM((layers, wide_hid, 3 * d), BF16),
        pltpu.VMEM((layers * 3, d, 128), F32),
        pltpu.VMEM((layers * 3, d, 128), F32),
        pltpu.VMEM((funcs, 2 * d, points), BF16),
        pltpu.VMEM((layers * funcs, 2 * d, points), BF16),
        pltpu.VMEM((layers * funcs, 2 * d, points), BF16),
        pltpu.VMEM((d, count), F32),
        pltpu.VMEM((layers * 3, 2 * d, count), BF16),
        pltpu.VMEM((layers * 3, 8, count), F32),
        pair,
        pair,
        pair,
        pair,
        pair,
        pair,
        pltpu.VMEM((1, 2 * d, count), BF16),
        pltpu.VMEM((layers, 2 * funcs * HEADS, count), F32),
        pltpu.VMEM((layers, HEADS, count), F32),
        pltpu.VMEM((layers, experts, count), F32),
        pltpu.VMEM((layers, funcs + 1, d, 3 * d), BF16),
        pltpu.VMEM((layers, funcs + 1, d, 3 * d), BF16),
        pltpu.VMEM((layers, funcs + 1, d, 128), F32),
        pltpu.VMEM((funcs, d, 3 * d), BF16),
        pltpu.VMEM((funcs, d, 3 * d), BF16),
        pltpu.VMEM((funcs, d, 128), F32),
        pltpu.VMEM((d + HEADS, d), F32),
        pltpu.VMEM((funcs * (d + HEADS), d), F32),
        pltpu.VMEM((layers, 6 * d, d), F32),
        pltpu.VMEM((layers, 2, d, d), F32),
        pltpu.VMEM((layers * 3, d, 128), F32),
        pltpu.VMEM((layers, 2 * experts, 128), F32),
        pltpu.VMEM((d, count), F32),
        pltpu.VMEM((experts, count), F32),
        pltpu.VMEM((2 * layers, funcs * MSG, d), F32),
        pltpu.VMEM((2 * layers, n_blk - 1, funcs * MSG, d), F32),
        pltpu.VMEM((2 * layers, MSG, d), F32),
        pltpu.VMEM((2 * layers, n_blk - 1, MSG, d), F32),
    ] + [pltpu.SemaphoreType.DMA((2 * layers, n_blk - 1))] * 4
    if summed:
        n_flat, n_line = n_dp, n_blk // 2
        moves = 2 + 2 * (n_flat - 1) + 2 * (n_line - 1)
        blocks = [up_shape, row_shape] * pairs + [(6 * d, d), (2 * d, d)]
        for high, width in blocks:
            scratch += [
                pltpu.VMEM((high // 2, width), F32),
                pltpu.VMEM((n_flat - 1, high // 2 // n_flat, width), F32),
                pltpu.VMEM((n_line - 1, high // 2 // n_flat // n_line, width), F32),
                pltpu.SemaphoreType.DMA((moves,)),
                pltpu.SemaphoreType.DMA((moves,)),
            ]
        group = 2 * n_flat
        some = 2 * (group - 1) + n_line - 1
        for high in (2 * d, 4 * d, 2 * d):
            scratch += [
                pltpu.VMEM((group - 1, high // group, d), F32),
                pltpu.VMEM((n_line, high // group, d), F32),
                pltpu.SemaphoreType.DMA((some,)),
                pltpu.SemaphoreType.DMA((some,)),
            ]
        few = n_flat + n_line - 1
        scratch += [
            pltpu.VMEM((2 + n_flat + n_line, 32, 128), F32),
            pltpu.SemaphoreType.DMA((few,)),
            pltpu.SemaphoreType.DMA((few,)),
        ]
    results = pl.pallas_call(
        functools.partial(device_kernel, n_dp, n_blk, summed),
        out_shape=[
            shape(features.shape, F32),
            shape(features.shape, F32),
            shape((layers, 6 * d, d), F32),
            shape((layers, 2 * d, d), F32),
            shape((pairs,) + up_shape, F32),
            shape((pairs,) + row_shape, F32),
            shape((3, layers, d), F32),
            shape(router.shape, F32),
        ],
        in_specs=[far, far, vmem, smem, smem, vmem, far, far, smem, far, far, far],
        out_specs=[vmem] * 8,
        scratch_shapes=scratch,
        compiler_params=pltpu.CompilerParams(
            collective_id=0, has_side_effects=True, vmem_limit_bytes=62 * 2**20
        ),
        name="gnot",
    )(
        features,
        func_points,
        coords,
        presence,
        valid_rows.transpose(1, 0, 2),
        norm_gain.transpose(1, 0, 2),
        in_proj.reshape(layers, 6 * d, d),
        out_proj.reshape(layers, 2 * d, d),
        router,
        expert_up.reshape((pairs,) + up_shape),
        expert_down.reshape((pairs,) + row_shape),
        cotangent,
    )
    if not summed:
        results = list(results[:2]) + list(lax.psum(list(results[2:]), ("dp", "blk")))
    results = pl.pallas_call(
        functools.partial(finish_kernel, len(results)),
        out_shape=[shape(x.shape, F32) for x in results],
        in_specs=[far] * len(results),
        out_specs=[far] * len(results),
        scratch_shapes=[pltpu.VMEM(x.shape, F32) for x in results]
        + [pltpu.SemaphoreType.DMA((2, len(results)))],
        compiler_params=pltpu.CompilerParams(vmem_limit_bytes=62 * 2**20),
        name="finish",
    )(*results)
    y, dx, in_g, out_g, up_g, down_g, gain_g, route_g = results
    return (
        y,
        dx,
        gain_g.transpose(1, 0, 2),
        in_g.reshape(in_proj.shape),
        out_g.reshape(out_proj.shape),
        route_g,
        up_g.reshape(expert_up.shape),
        down_g.reshape(expert_down.shape),
    )


def solution(mesh):
    placed = (
        P("dp", "blk", None),
        P("dp", None, "blk", None),
        P("dp", None, "blk"),
        P("dp", None),
        P("dp", None, None),
        P(),
        P(),
        P(),
        P(),
        P(),
        P(),
        P("dp", "blk", None),
    )
    return jax.shard_map(
        functools.partial(on_device, mesh.shape["dp"], mesh.shape["blk"]),
        mesh=mesh,
        in_specs=placed,
        out_specs=(P("dp", "blk", None), P("dp", "blk", None), P(), P(), P(), P(), P(), P()),
        check_vma=False,
    )
```

```python
import functools
import math

import jax
import jax.numpy as jnp
from jax import lax
from jax.experimental import pallas as pl
from jax.experimental.pallas import tpu as pltpu
from jax.sharding import PartitionSpec as P

MESH = pl.DeviceIdType.MESH
F32 = jnp.float32
BF16 = jnp.bfloat16
HEADS = 8
HEAD_DIM = 16
EPS = 1e-05
C1 = math.sqrt(2.0 / math.pi)
C2 = C1 * 0.044715
TILE = 2048
WIDE_TILE = 1024
VMEM_BYTES = 66500000
SPAN = 512
MSG = 24


def nn(a, b):
    return jnp.dot(a, b, preferred_element_type=F32)


def nt(a, b):
    return lax.dot_general(a, b, (((1,), (1,)), ((), ())), preferred_element_type=F32)


def tn(a, b):
    return lax.dot_general(a, b, (((0,), (0,)), ((), ())), preferred_element_type=F32)


def split(x):
    high = x.astype(BF16)
    return high, (x - high.astype(F32)).astype(BF16)


def rows(*parts):
    return jnp.concatenate(parts, axis=0)


def cols(*parts):
    return jnp.concatenate(parts, axis=1)


def triple(w):
    high, low = split(w)
    return cols(high, low, high)


def k3(w3, x):
    high, low = x
    return nn(w3, rows(high, high, low))


def d3(w_high, w_low, x):
    high, low = x
    return nn(w_high, high) + (nn(w_low, high) + nn(w_high, low))


def outer(a, b):
    m, n = a[0].shape[0], b[0].shape[0]
    r = nt(rows(*a), rows(*b))
    return r[:m, :n] + (r[:m, n:] + r[m:, :n])


def wide(column, t):
    return cols(*([column] * (t // 128)))


def lanes(x):
    total = x[:, :128]
    for at in range(128, x.shape[1], 128):
        total = total + x[:, at : at + 128]
    return total


def by_head(x):
    return x.reshape(HEAD_DIM, HEADS, x.shape[-1])


def head_sum(x):
    return jnp.sum(by_head(x), axis=0)


def spread(r):
    return jnp.broadcast_to(r[None], (HEAD_DIM,) + r.shape).reshape(HEAD_DIM * HEADS, r.shape[-1])


def head_softmax(z):
    z = by_head(z)
    e = jnp.exp(z - jnp.max(z, axis=0)[None])
    p = e * (1.0 / jnp.sum(e, axis=0))[None]
    return p.reshape(HEAD_DIM * HEADS, p.shape[-1])


def softmax_back(p, dp):
    return p * (dp - spread(head_sum(p * dp)))


def mean(x):
    return jnp.sum(x, axis=0, keepdims=True) * (1.0 / x.shape[0])


def layer_norm(s, gain):
    centred = s - mean(s)
    r = lax.rsqrt(mean(centred * centred) + EPS)
    return centred * r * gain, r


def norm_back(dy, y, r, gain, inv_gain):
    xhat = y * inv_gain
    v = gain * dy
    return r * (v - mean(v) - xhat * mean(v * xhat)), dy * xhat


def put(ref, at, sl, x):
    d = x[0].shape[0]
    ref[at, 0:d, sl] = x[0]
    ref[at, d : 2 * d, sl] = x[1]


def get(ref, at, sl):
    both = ref[at, :, sl]
    d = both.shape[0] // 2
    return both[:d], both[d:]


def whole(x):
    return x[0].astype(F32) + x[1].astype(F32)


def gelu_parts(v):
    v2 = v * v
    g = 0.5 + 0.5 * jnp.tanh(v * (C1 + C2 * v2))
    return v2, g


def device_kernel(
    n_dp,
    n_blk,
    summed,
    features_hbm,
    points_hbm,
    coords,
    presence,
    valid,
    gain,
    in_hbm,
    out_hbm,
    router,
    up_hbm,
    down_hbm,
    cot_hbm,
    out_to,
    fgrad_to,
    in_to,
    out_proj_to,
    up_to,
    down_to,
    gain_to,
    router_to,
    load_sem,
    store_sem,
    out,
    fgrad,
    f_att,
    f_pair,
    f_gain,
    f_router,
    g_att,
    g_pair,
    g_early,
    f_early,
    g_keys,
    g_small,
    f_small,
    w_in,
    w_qc,
    w_self,
    w_out,
    w_outb,
    up_t,
    up_n,
    down_t,
    down_n,
    gcol,
    fp,
    kc,
    vc,
    stream,
    y_ref,
    r_ref,
    qc,
    mixc,
    qs,
    ks,
    vs,
    mixs,
    hold,
    rdens_ref,
    rden_ref,
    gates,
    kv_t,
    kv_n,
    z_col,
    dkv_t,
    dkv_n,
    dz_col,
    acc_kv,
    acc_dkvc,
    acc_wi,
    acc_wo,
    acc_g,
    acc_r,
    dy_ref,
    dgate_ref,
    src_c,
    got_c,
    src_s,
    got_s,
    send_c,
    recv_c,
    send_s,
    recv_s,
    *ring,
):
    if not summed:
        g_att, g_pair, g_keys = f_att.at[1], f_pair, f_att.at[0, pl.ds(128, 256)]
    layers, experts, hid = router.shape[0], router.shape[2], up_hbm.shape[2]
    funcs = presence.shape[1]
    points = points_hbm.shape[0] // funcs
    count, d = features_hbm.shape[1:]

    def load(src, dst, at):
        copy = pltpu.make_async_copy(src, dst, load_sem.at[at])
        copy.start()
        return copy

    stores, sums_stores = [], []

    def storing(src, dst):
        at = len(stores)
        stores.append(lambda: pltpu.make_async_copy(src, dst, store_sem.at[at]))
        return lambda: stores[at]().start()

    def store(src, dst):
        storing(src, dst)()

    in_load = load(in_hbm, f_att.at[:, pl.ds(0, 6 * d)], 0)
    out_load = load(out_hbm, f_att.at[:, pl.ds(6 * d, 2 * d)], 1)
    first_load = 2
    packed = fgrad.at[0, pl.ds(0, funcs * points)]
    points_load = load(points_hbm, packed, first_load)
    features_load = load(features_hbm, out, first_load + 1)
    halves = hid // 128
    up_loads = [
        load(
            up_hbm.at[:, :, pl.ds(h * 128, 128)],
            f_pair.at[:, pl.ds(h * 2 * d, 2 * d)],
            first_load + 5 + h,
        )
        for h in range(halves)
    ]
    down_load = load(down_hbm, f_pair.at[:, pl.ds(2 * hid, 2 * hid)], first_load + 3)
    me = lax.axis_index("blk")
    own_dp = lax.axis_index("dp")
    n_flat, n_line = n_dp, n_blk // 2
    core, line = own_dp % 2, me // 2
    flat = (own_dp // 2) * 2 + me % 2

    sibling = {"dp": own_dp - core + (1 - core), "blk": me}

    def flat_at(j):
        at = lax.rem(flat + j, n_flat)
        return {"dp": (at // 2) * 2 + core, "blk": line * 2 + at % 2}

    def line_at(j):
        return {"dp": own_dp, "blk": lax.rem(line + j, n_line) * 2 + me % 2}

    def group_at(j):
        at = lax.rem(flat * 2 + core + j, 2 * n_flat)
        spot = at // 2
        return {"dp": (spot // 2) * 2 + at % 2, "blk": line * 2 + spot % 2}

    partners = [{"dp": own_dp, "blk": lax.rem(me + j, n_blk)} for j in range(1, n_blk)]
    if summed:
        partners += [group_at(j) for j in range(1, 2 * n_flat)]
    barrier = pltpu.get_barrier_semaphore()
    for partner in partners:
        pl.semaphore_signal(barrier, inc=1, device_id=partner, device_id_type=MESH)

    sums = {}

    def take(names):
        now = [steps.pop(0) for name in names for steps in sums.get(name, ()) if steps]

        def run():
            for step in now:
                step()

        return run

    def advance(names):
        take(names)()

    def made(jobs, send, recv):
        return [
            pltpu.make_async_remote_copy(
                src_ref=src,
                dst_ref=dst,
                send_sem=send.at[k],
                recv_sem=recv.at[k],
                device_id=device,
                device_id_type=MESH,
            )
            for k, src, dst, device in jobs()
        ]

    def go(jobs, send, recv):
        for copy in made(jobs, send, recv):
            copy.start()

    def settle(jobs, send, recv):
        for copy in made(jobs, send, recv):
            copy.wait()

    def reduction(local, final, halves, parts, pieces, send, recv, after):
        half = local.shape[0] // 2
        part = half // n_flat
        piece = part // n_line

        def at(start, size):
            return pl.ds(pl.multiple_of(start, 8), size)

        def of_core(other=0):
            return at((core if not other else 1 - core) * half, half)

        def of_flat(j=0):
            return at(core * half + lax.rem(flat + j, n_flat) * part, part)

        def of_line(j=0):
            return at(core * half + flat * part + lax.rem(line + j, n_line) * piece, piece)

        k1 = 1
        k2 = k1 + n_flat - 1
        k3_ = k2 + n_line - 1
        k4 = k3_ + n_line - 1
        k5 = k4 + n_flat - 1

        def core_out():
            return [(0, local.at[of_core(1)], halves, sibling)]

        def flat_out():
            return [
                (k1 + j - 1, local.at[of_flat(j)], parts.at[j - 1], flat_at(j))
                for j in range(1, n_flat)
            ]

        def line_out():
            return [
                (k2 + j - 1, local.at[of_line(j)], pieces.at[j - 1], line_at(j))
                for j in range(1, n_line)
            ]

        def line_back():
            mine = final.at[of_line()]
            return [(k3_ + j - 1, mine, mine, line_at(j)) for j in range(1, n_line)]

        def flat_back():
            mine = final.at[of_flat()]
            return [(k4 + j - 1, mine, mine, flat_at(j)) for j in range(1, n_flat)]

        def core_back():
            mine = final.at[of_core()]
            return [(k5, mine, mine, sibling)]

        def one():
            go(core_out, send, recv)

        def two():
            settle(core_out, send, recv)
            spot = of_core()
            local[spot] = local[spot] + halves[...]
            go(flat_out, send, recv)

        def three():
            settle(flat_out, send, recv)
            spot = of_flat()
            total = local[spot]
            for j in range(n_flat - 1):
                total = total + parts[j]
            local[spot] = total
            go(line_out, send, recv)

        def four():
            settle(line_out, send, recv)
            spot = of_line()
            total = local[spot]
            for j in range(n_line - 1):
                total = total + pieces[j]
            final[spot] = total
            go(line_back, send, recv)

        def five():
            settle(line_back, send, recv)
            go(flat_back, send, recv)

        def six():
            settle(flat_back, send, recv)
            go(core_back, send, recv)

        def seven():
            settle(core_back, send, recv)
            after()

        return [one, two, three, four, five, six, seven]

    def quick(local, final, parts, held, send, recv, after):
        group = 2 * n_flat
        size = local.shape[0] // group
        place = flat * 2 + core

        def piece(j):
            return pl.ds(pl.multiple_of(lax.rem(place + j, group) * size, 8), size)

        def out_jobs():
            return [
                (j - 1, local.at[piece(j)], parts.at[j - 1], group_at(j)) for j in range(1, group)
            ]

        def line_jobs():
            mine = held.at[line]
            return [(group + j - 2, mine, mine, line_at(j)) for j in range(1, n_line)]

        def back_jobs():
            mine = final.at[piece(0)]
            return [(group + n_line + j - 3, mine, mine, group_at(j)) for j in range(1, group)]

        def one():
            go(out_jobs, send, recv)

        def two():
            settle(out_jobs, send, recv)
            total = local[piece(0)]
            for j in range(group - 1):
                total = total + parts[j]
            held[line] = total
            go(line_jobs, send, recv)

        def three():
            settle(line_jobs, send, recv)
            total = held[0]
            for j in range(1, n_line):
                total = total + held[j]
            final[piece(0)] = total
            go(back_jobs, send, recv)

        def four():
            settle(back_jobs, send, recv)
            after()

        return [one, two, three, four]

    def exchange_small(local, final, held, send, recv):
        levels = (
            (0, 2, core, lambda: [sibling], 0),
            (2, n_flat, flat, lambda: [flat_at(j) for j in range(1, n_flat)], 1),
            (2 + n_flat, n_line, line, lambda: [line_at(j) for j in range(1, n_line)], n_flat),
        )

        def jobs_of(level):
            at, _, place, devices, k = levels[level]

            def jobs():
                mine = held.at[at + place]
                return [(k + j, mine, mine, device) for j, device in enumerate(devices())]

            return jobs

        def start(level, value):
            at, _, place, _, _ = levels[level]
            held[at + place] = value
            go(jobs_of(level), send, recv)

        def finish(level):
            settle(jobs_of(level), send, recv)
            at, size = levels[level][:2]
            value = held[at]
            for j in range(1, size):
                value = value + held[at + j]
            return value

        def last():
            final[...] = finish(2)

        return [
            lambda: start(0, local[...]),
            lambda: start(1, finish(0)),
            lambda: start(2, finish(1)),
            last,
        ]

    def begin(name, steps):
        if summed:
            sums.setdefault(name, []).append(steps)

    def reduce(name, seg, local, final, after):
        sums_stores.append(after)
        if summed:
            begin(name, reduction(local, final, *ring[5 * seg : 5 * seg + 5], after))

    def reduce_quick(name, at, local, final, after):
        sums_stores.append(after)
        if summed:
            start = 5 * (2 * layers + 1) + 4 * at
            begin(name, quick(local, final, *ring[start : start + 4], after))

    def reduce_pair(name, l, pair):
        seg = l * 2 + pair
        moves = [storing(f_pair.at[seg, pl.ds(2 * hid, 2 * hid)], down_to.at[seg])]
        for at in range(2 * halves):
            e, h = at // halves, at % halves
            moves.append(
                storing(
                    g_pair.at[seg, pl.ds(at * 128, 128)],
                    up_to.at[seg, pl.ds(e * d, d), pl.ds(h * 128, 128)],
                )
            )

        def after():
            for at in range(2 * halves):
                spot = slice(at * 128, (at + 1) * 128)
                g_pair[seg, spot, :] = f_pair[seg, spot, :].T
            for move in moves:
                move()

        reduce(name, seg, g_pair.at[seg], f_pair.at[seg], after)

    def copies(src, got, send, recv, at):
        return [
            pltpu.make_async_remote_copy(
                src_ref=src.at[at],
                dst_ref=got.at[at, j - 1],
                send_sem=send.at[at, j - 1],
                recv_sem=recv.at[at, j - 1],
                device_id={"blk": lax.rem(me + j, n_blk)},
                device_id_type=MESH,
            )
            for j in range(1, n_blk)
        ]

    def send_off(refs, at):
        for copy in copies(*refs, at):
            copy.start()

    def collect(refs, at):
        for copy in copies(*refs, at):
            copy.wait()
        src, got = refs[0], refs[1]
        total = src[at]
        for j in range(n_blk - 1):
            total = total + got[at, j]
        return total

    cross = (src_c, got_c, send_c, recv_c)
    own = (src_s, got_s, send_s, recv_s)

    head_mask = (
        lax.broadcasted_iota(jnp.int32, (HEADS, d), 0)
        == lax.broadcasted_iota(jnp.int32, (HEADS, d), 1) % HEADS
    ).astype(F32)
    spot = lax.broadcasted_iota(jnp.int32, (d, d), 0)
    perm = (
        lax.broadcasted_iota(jnp.int32, (d, d), 1) == (spot % HEADS) * HEAD_DIM + spot // HEADS
    ).astype(F32)
    perm16 = perm.astype(BF16)

    def compact(full):
        return jnp.sum(full.reshape(HEAD_DIM, HEADS, d) * head_mask[None], axis=1)

    def expand(compacted):
        full = jnp.broadcast_to(compacted[:, None, :], (HEAD_DIM, HEADS, d)) * head_mask[None]
        return full.reshape(d, d)

    def unpack(total, t_ref, n_ref, c_ref, at):
        full = expand(total[0])
        t_ref[at] = triple(full)
        n_ref[at] = triple(full.T)
        c_ref[at] = jnp.broadcast_to(total[1], (d, d)).T

    def cross_kv(f):
        return slice(f * HEAD_DIM, (f + 1) * HEAD_DIM)

    def cross_key(f):
        return slice(funcs * HEAD_DIM + f, funcs * HEAD_DIM + f + 1)

    def cut_attention(l, a):
        for j in range(3):
            at = a * 3 + j
            w_high, w_low = split(f_att[l, at * d : (at + 1) * d, :])
            high = nt(perm16, w_high).astype(BF16)
            low = nt(perm16, w_low).astype(BF16)
            w_in[l, at * d : (at + 1) * d, :] = cols(high, low, high)
            if (a, j) == (0, 0) or a == 1:
                high = nt(w_high, perm16).astype(BF16)
                low = nt(w_low, perm16).astype(BF16)
                if a == 0:
                    w_qc[l] = cols(high, low, high)
                else:
                    w_self[l, :, j * d : (j + 1) * d] = high
                    w_self[l, :, (3 + j) * d : (4 + j) * d] = low

    def cut_out(l, a):
        w_high, w_low = split(f_att[l, (6 + a) * d : (7 + a) * d, :])
        contract = (((0,), (1,)), ((), ()))
        high, low = [
            lax.dot_general(w, perm16, contract, preferred_element_type=F32).astype(BF16)
            for w in (w_high, w_low)
        ]
        w_out[l, a] = cols(high, low, high)
        high = nn(perm16, w_high).astype(BF16)
        low = nn(perm16, w_low).astype(BF16)
        w_outb[l, a] = cols(high, low, high)

    def cut_experts(l):
        for e in range(experts):
            lo, hi = e * hid, (e + 1) * hid
            seg, spot = l * 2 + e // 2, e % 2
            w = cols(
                *[f_pair[seg, (2 * h + spot) * d : (2 * h + spot + 1) * d, :] for h in range(halves)]
            )
            high, low = split(w)
            up_n[l, :, lo:hi] = high
            up_n[l, :, experts * hid + lo : experts * hid + hi] = low
            up_t[l, lo:hi, :] = triple(w.T)
            w = f_pair[seg, (2 + spot) * hid : (3 + spot) * hid, :]
            down_n[l, lo:hi, :] = triple(w)
            high, low = split(w.T)
            down_t[l, :, lo:hi] = high
            down_t[l, :, experts * hid + lo : experts * hid + hi] = low

    def cut_gains(l):
        for j in range(3):
            column = jnp.broadcast_to(gain[j, l : l + 1, :], (d, d)).T
            gcol[l * 3 + j] = column

    present = [presence[0, f].astype(F32) for f in range(funcs)]
    all_present = present[0]
    for f in range(1, funcs):
        all_present = all_present + present[f]
    weight = [
        jnp.full((1, 1), present[f], F32) / jnp.full((1, 1), all_present, F32) for f in range(funcs)
    ]

    ones = jnp.ones((16, points), BF16)

    def cross_summary(l):
        for f in range(funcs):
            both = fp[f]
            z = k3(w_in[l, d : 3 * d, :], (both[:d], both[d:]))
            kept = (
                lax.broadcasted_iota(jnp.int32, (1, points), 1) < valid[f, 0, me]
            ).astype(F32)
            k = split(head_softmax(z[:d]) * kept)
            v = split(z[d:])
            put(kc, l * funcs + f, slice(None), k)
            put(vc, l * funcs + f, slice(None), v)
            r = nt(rows(*v, ones), rows(*k))
            src_c[l, cross_kv(f), :] = compact(r[:d, :d] + (r[:d, d:] + r[d : 2 * d, :d]))
            src_c[l, cross_key(f), :] = r[2 * d : 2 * d + 1, :d] + r[2 * d : 2 * d + 1, d:]
        send_off(cross, l)

    def cross_total(l):
        total = collect(cross, l)
        for f in range(funcs):
            unpack((total[cross_kv(f)], total[cross_key(f)]), kv_t.at[l], kv_n.at[l], z_col.at[l], f)

    def own_parts(total):
        return total[:HEAD_DIM], total[HEAD_DIM : HEAD_DIM + 1]

    def self_total(l):
        unpack(own_parts(collect(own, l)), kv_t.at[l], kv_n.at[l], z_col.at[l], funcs)

    def norm_in(l, at, s, sl):
        y, r = layer_norm(s, wide(gcol[l * 3 + at], sl.size))
        y = split(y)
        put(y_ref, l * 3 + at, sl, y)
        r_ref[l * 3 + at, 0:1, sl] = r
        return y

    def norm_out(l, at, dy, sl):
        y = whole(get(y_ref, l * 3 + at, sl))
        ds, dg = norm_back(
            dy,
            y,
            r_ref[l * 3 + at, 0:1, sl],
            wide(gcol[l * 3 + at], sl.size),
            wide(1.0 / gcol[l * 3 + at], sl.size),
        )
        acc_g[l * 3 + at] += lanes(dg)
        return ds

    def cross_query(l, s, sl):
        y = norm_in(l, 0, s, sl)
        put(qc, l, sl, split(head_softmax(k3(w_in[l, :d, :], y))))

    def cross_read(l, s, sl):
        q2 = get(qc, l, sl)
        q = whole(q2)
        num = k3(kv_t[l, :funcs].reshape(funcs * d, 3 * d), q2)
        mix = q
        for f in range(funcs):
            rden = 1.0 / head_sum(q * wide(z_col[l, f], sl.size))
            rdens_ref[l, f * 8 : (f + 1) * 8, sl] = rden
            mix = mix + num[f * d : (f + 1) * d] * spread(rden * weight[f])
        mix = split(mix)
        put(mixc, l, sl, mix)
        s = s + k3(w_out[l, 0], mix)
        y = norm_in(l, 1, s, sl)
        z = k3(w_in[l, 3 * d :, :], y)
        q = split(head_softmax(z[:d]))
        k = split(head_softmax(z[d : 2 * d]))
        v = split(z[2 * d :])
        put(qs, l, sl, q)
        put(ks, l, sl, k)
        put(vs, l, sl, v)
        r = nt(rows(*v, jnp.ones((16, sl.size), BF16)), rows(*k))
        acc_kv[:d, :] += r[:d, :d] + (r[:d, d:] + r[d : 2 * d, :d])
        acc_kv[d:, :] += r[2 * d : 2 * d + 8, :d] + r[2 * d : 2 * d + 8, d:]
        stream[:, sl] = s

    def send_self(l):
        src_s[l, :HEAD_DIM, :] = compact(acc_kv[:d, :])
        src_s[l, HEAD_DIM:, :] = acc_kv[d:, :]
        send_off(own, l)

    def self_read(l, s, sl):
        q2 = get(qs, l, sl)
        q = whole(q2)
        num = k3(kv_t[l, funcs], q2)
        rden = 1.0 / head_sum(q * wide(z_col[l, funcs], sl.size))
        rden_ref[l, :, sl] = rden
        mix = split(num * spread(rden) + q)
        put(mixs, l, sl, mix)
        s = s + k3(w_out[l, 1], mix)
        return s, norm_in(l, 2, s, sl)

    def hidden_in(l, e, y):
        return k3(up_t[l, e * hid : (e + 1) * hid, :], y)

    def down_of(l, e, x):
        at = experts * hid
        return d3(
            down_t[l, :, e * hid : (e + 1) * hid],
            down_t[l, :, at + e * hid : at + (e + 1) * hid],
            x,
        )

    def run_experts(l, y, sl):
        total = None
        for e in range(experts):
            v = hidden_in(l, e, y)
            _, g = gelu_parts(v)
            part = down_of(l, e, split(v * g * gates[l, e : e + 1, sl]))
            total = part if total is None else total + part
        return total

    def weights_of(l, e, gated, dpre, y, ds2):
        seg, place = l * 2 + e // 2, e % 2
        g_pair[seg, (2 + place) * hid : (3 + place) * hid, :] += outer(gated, ds2)
        g_pair[seg, place * hid : (place + 1) * hid, :] += outer(dpre, y)

    dzq = [(mixs, 1), (hold, 0)]
    spare = [(y_ref, 3), (y_ref, 4), (y_ref, 5)] + [
        (ref, 1) for ref in (qc, mixc, qs, ks, vs)
    ]

    def expert_later(e, sl):
        gated, dpre = [
            [ref[at, :, sl] for ref, at in spare[4 * (e % 2) + k : 4 * (e % 2) + k + 2]]
            for k in (0, 2)
        ]
        weights_of(0, e, gated, dpre, get(y_ref, 2, sl), get(hold, 0, sl))

    def expert_back(l, pair, y, ds2, sl, later):
        at = experts * hid
        step = min(SPAN, sl.size)
        units = [(e, k) for e in (2 * pair, 2 * pair + 1) for k in range(0, sl.size, step)]

        def products(e, k):
            part = [(x[0][:, k : k + step], x[1][:, k : k + step]) for x in (y, ds2)]
            return hidden_in(l, e, part[0]), k3(down_n[l, e * hid : (e + 1) * hid, :], part[1])

        ready = products(*units[0])
        held = []
        for now, (e, k) in enumerate(units):
            v, back = ready
            if now + 1 < len(units):
                ready = products(*units[now + 1])
            spot = pl.ds(pl.multiple_of(sl.start + k, 128), step)
            gate = 0.5 * gates[l, e : e + 1, spot]
            v2 = v * v
            inner = v * (C1 + C2 * v2)
            twice = 1.0 + jnp.tanh(inner)
            act = v * twice
            slope = twice * (1.0 + (2.0 - twice) * (v * (C1 + 3.0 * C2 * v2)))
            dgate_ref[e : e + 1, spot] = 0.5 * jnp.sum(act * back, axis=0, keepdims=True)
            held.append(split(act * gate) + split(slope * back * gate))
            if k + step < sl.size:
                continue
            joined = [cols(*parts) for parts in zip(*held)]
            gated, dpre = joined[:2], joined[2:]
            held = []
            if later:
                for k, x in enumerate(joined):
                    ref, slot = spare[4 * (e % 2) + k]
                    ref[slot, :, sl] = x
            else:
                weights_of(l, e, gated, dpre, y, ds2)
            dy = d3(
                up_n[l, :, e * hid : (e + 1) * hid],
                up_n[l, :, at + e * hid : at + (e + 1) * hid],
                dpre,
            )
            yield e, gated, dy

    def gates_back(l, ds, dy, sl):
        probs = [gates[l, e : e + 1, sl] for e in range(experts)]
        dgate = [dgate_ref[e : e + 1, sl] for e in range(experts)]
        centre = probs[0] * dgate[0]
        for e in range(1, experts):
            centre = centre + probs[e] * dgate[e]
        dlogit = rows(*[probs[e] * (dgate[e] - centre) for e in range(experts)])
        place = coords[0, :, sl]
        acc_r[l] += lanes(rows(dlogit * place[0:1], dlogit * place[1:2]))
        return ds + norm_out(l, 2, dy, sl)

    def experts_back(l, pair, sl, forward, later):
        ds2 = get(hold, 0, sl)
        y = get(y_ref, l * 3 + 2, sl)
        total, dy = None, None
        for e, gated, part in expert_back(l, pair, y, ds2, sl, later):
            dy = part if dy is None else dy + part
            if forward:
                part = down_of(l, e, gated)
                total = part if total is None else total + part
        dy_ref[:, sl] = dy if pair == 0 else dy_ref[:, sl] + dy
        if forward:
            stream[:, sl] += total

    def self_read_back(l, ds, sl):
        ds2 = split(ds)
        dmix = k3(w_outb[l, 1], ds2)
        back = k3(kv_n[l, funcs], split(dmix))
        q2 = get(qs, l, sl)
        q = whole(q2)
        rden = rden_ref[l, :, sl]
        u = rden * rden * head_sum(q * back)
        dq = dmix + spread(rden) * back - wide(z_col[l, funcs], sl.size) * spread(u)
        put(*dzq[l], sl, split(softmax_back(q, dq)))
        da = split(dmix * spread(rden))
        u2 = split(u)
        r = nt(rows(*da, *u2), rows(*q2))
        acc_kv[:d, :] += r[:d, :d] + (r[:d, d:] + r[d : 2 * d, :d])
        low = r[2 * d :, :d] + r[2 * d :, d:]
        acc_kv[d:, :] += low[:8] + low[8:]

    def self_out_later(l, sl):
        acc_wo[l, 1] += outer(get(mixs, l, sl), split(stream[:, sl]))

    def back_row(x):
        return jnp.broadcast_to(-jnp.sum(x * head_mask, axis=0, keepdims=True), (HEADS, d))

    def send_self_back(l):
        at = layers + l
        src_s[at, :HEAD_DIM, :] = compact(acc_kv[:d, :])
        src_s[at, HEAD_DIM:, :] = back_row(acc_kv[d:, :])
        send_off(own, at)

    def self_total_back(l):
        unpack(own_parts(collect(own, layers + l)), dkv_t, dkv_n, dz_col, 0)

    def attention_back(l, ds, sl, later=False):
        k2, v2 = get(ks, l, sl), get(vs, l, sl)
        dk = k3(dkv_n[0], v2) + wide(dz_col[0], sl.size)
        dv = split(k3(dkv_t[0], k2))
        dzk = split(softmax_back(whole(k2), dk))
        q2 = get(*dzq[l], sl)
        dz = (rows(q2[0], dzk[0], dv[0]), rows(q2[1], dzk[1], dv[1]))
        if later:
            put(qs, 1, sl, dzk)
            put(ks, 1, sl, dv)
        else:
            acc_wi[l, 3 * d :, :] += outer(dz, get(y_ref, l * 3 + 1, sl))
        dy = d3(w_self[l, :, : 3 * d], w_self[l, :, 3 * d :], dz)
        return ds + norm_out(l, 1, dy, sl)

    def weights_later(sl):
        parts = (get(*dzq[0], sl), get(qs, 1, sl), get(ks, 1, sl))
        dz = (rows(*[part[0] for part in parts]), rows(*[part[1] for part in parts]))
        acc_wi[0, 3 * d :, :] += outer(dz, get(y_ref, 1, sl))
        acc_wo[0, 0] += outer(get(mixc, 0, sl), get(vs, 1, sl))

    def cross_read_back(l, ds, sl, later=False):
        ds2 = split(ds)
        dmix = k3(w_outb[l, 0], ds2)
        if later:
            put(vs, 1, sl, ds2)
        else:
            acc_wo[l, 0] += outer(get(mixc, l, sl), ds2)
        back = k3(kv_n[l, :funcs].reshape(funcs * d, 3 * d), split(dmix))
        q2 = get(qc, l, sl)
        q = whole(q2)
        dq = dmix
        da, us = [], []
        for f in range(funcs):
            rden = rdens_ref[l, f * 8 : (f + 1) * 8, sl]
            inv = rden * weight[f]
            back_f = back[f * d : (f + 1) * d]
            u = inv * rden * head_sum(q * back_f)
            dq = dq + spread(inv) * back_f - wide(z_col[l, f], sl.size) * spread(u)
            da.append(dmix * spread(inv))
            us.append(u)
        if funcs % 2:
            us.append(jnp.zeros_like(us[0]))
        side = rows(*us)
        m = funcs * d
        r = nt(rows(*split(rows(*da)), *split(side)), rows(*q2))
        acc_dkvc[:m, :] += r[:m, :d] + (r[:m, d:] + r[m : 2 * m, :d])
        low = r[2 * m :, :d] + r[2 * m :, d:]
        high = side.shape[0]
        acc_dkvc[m:, :] += (low[:high] + low[high:])[: 8 * funcs]
        return softmax_back(q, dq)

    def cross_query_back(l, ds, dz, sl):
        dz2 = split(dz)
        acc_wi[l, :d, :] += outer(dz2, get(y_ref, l * 3, sl))
        return ds + norm_out(l, 0, k3(w_qc[l], dz2), sl)

    def send_cross_back(l):
        at = layers + l
        for f in range(funcs):
            src_c[at, cross_kv(f), :] = compact(acc_dkvc[f * d : (f + 1) * d, :])
            src_c[at, cross_key(f), :] = back_row(
                acc_dkvc[funcs * d + f * 8 : funcs * d + (f + 1) * 8, :]
            )[:1]
        send_off(cross, at)

    def cross_keys_back(l):
        total = collect(cross, layers + l)
        for f in range(funcs):
            unpack((total[cross_kv(f)], total[cross_key(f)]), dkv_t, dkv_n, dz_col, f)
        for f in range(funcs):
            k2 = get(kc, l * funcs + f, slice(None))
            v2 = get(vc, l * funcs + f, slice(None))
            dk = k3(dkv_n[f], v2) + wide(dz_col[f], points)
            dv = split(k3(dkv_t[f], k2))
            dzk = split(softmax_back(whole(k2), dk))
            both = fp[f]
            part = outer(
                (rows(dzk[0], dv[0]), rows(dzk[1], dv[1])), (both[:d], both[d:])
            )
            if f == 0:
                acc_wi[l, d : 3 * d, :] = part
            else:
                acc_wi[l, d : 3 * d, :] += part

    def each_tile(body, tile=TILE, then=()):
        tile = min(tile, count)
        move = take(then)
        if tile == count:
            move()
            body(pl.ds(0, count))
            return

        def step(i, carry):
            if then:
                pl.when(i == count // tile - 1)(move)
            body(pl.ds(pl.multiple_of(i * tile, tile), tile))
            return carry

        lax.fori_loop(0, count // tile, step, 0)

    exact = functools.partial(
        lax.dot_general, precision=lax.Precision.HIGHEST, preferred_element_type=F32
    )

    def finish_in(l, at, ref, spot):
        ref[spot : spot + d, :] = exact(
            acc_wi[l, at * d : (at + 1) * d, :], perm, (((0,), (0,)), ((), ()))
        )

    def finish_out(l, a, ref, spot):
        ref[spot : spot + d, :] = exact(perm, acc_wo[l, a], (((0,), (0,)), ((), ())))

    in_load.wait()
    points_load.wait()
    for f in range(funcs):
        high, low = split(fgrad[0, f * points : (f + 1) * points, :].T)
        fp[f, :d, :] = high
        fp[f, d:, :] = low
    cot_load = load(cot_hbm, fgrad, first_load + 4)
    for ref in (src_c, src_s):
        ref[...] = jnp.zeros_like(ref)
    cut_attention(0, 0)
    pl.semaphore_wait(barrier, len(partners))
    cross_summary(0)

    out_load.wait()
    features_load.wait()
    cut_gains(0)

    def first(sl):
        s = out[0, sl, :].T
        stream[:, sl] = s
        cross_query(0, s, sl)

    each_tile(first)
    cut_attention(0, 1)
    cut_out(0, 0)
    cut_out(0, 1)
    acc_kv[...] = jnp.zeros_like(acc_kv)
    cross_total(0)
    each_tile(lambda sl: cross_read(0, stream[:, sl], sl))
    send_self(0)

    cut_attention(1, 0)
    cross_summary(1)
    for copy in up_loads + [down_load]:
        copy.wait()
    cut_experts(0)

    def route(sl):
        place = coords[0, :, sl]
        for l in range(layers):
            logit = [
                place[0:1] * router[l, 0, e] + place[1:2] * router[l, 1, e] for e in range(experts)
            ]
            top = functools.reduce(jnp.maximum, logit)
            grown = [jnp.exp(x - top) for x in logit]
            total = functools.reduce(jnp.add, grown)
            for e in range(experts):
                gates[l, e : e + 1, sl] = grown[e] / total

    route(pl.ds(0, count))
    acc_kv[...] = jnp.zeros_like(acc_kv)
    self_total(0)

    def second(sl):
        s, y = self_read(0, stream[:, sl], sl)
        stream[:, sl] = s + run_experts(0, y, sl)

    each_tile(second, WIDE_TILE)
    cut_gains(1)
    cut_attention(1, 1)
    cut_out(1, 0)
    cross_total(1)

    def second_cross(sl):
        s = stream[:, sl]
        cross_query(1, s, sl)
        cross_read(1, s, sl)

    each_tile(second_cross)
    send_self(1)

    cut_out(1, 1)
    cut_experts(1)
    cot_load.wait()

    def turn(sl):
        put(hold, 0, sl, split(fgrad[0, sl, :].T))

    each_tile(turn)
    for ref in (acc_wi, acc_wo, acc_g, acc_r, g_pair, acc_kv, acc_dkvc):
        ref[...] = jnp.zeros_like(ref)
    self_total(1)

    def third(sl):
        stream[:, sl] = self_read(1, stream[:, sl], sl)[0]

    each_tile(third)

    def pair_loop(l, pair, between=(), later=False):
        each_tile(
            lambda sl: experts_back(l, pair, sl, l == layers - 1, later), WIDE_TILE, then=between
        )

    pair_loop(1, 0)
    reduce_pair("a0", 1, 0)
    advance(["a0"])
    pair_loop(1, 1, ["a0"])
    reduce_pair("a1", 1, 1)
    advance(["a1"])

    def third_back(sl):
        ds = gates_back(1, whole(get(hold, 0, sl)), dy_ref[:, sl], sl)
        self_read_back(1, ds, sl)
        dy_ref[:, sl] = stream[:, sl]
        stream[:, sl] = ds

    each_tile(third_back)
    send_self_back(1)

    def third_later(sl):
        out[0, sl, :] = dy_ref[:, sl].T
        self_out_later(1, sl)

    each_tile(third_later)
    store(out, out_to)
    advance(["a0"])
    acc_kv[...] = jnp.zeros_like(acc_kv)
    self_total_back(1)
    advance(["a1"])

    def fourth(sl):
        ds = attention_back(1, stream[:, sl], sl)
        dz = cross_read_back(1, ds, sl)
        ds = cross_query_back(1, ds, dz, sl)
        stream[:, sl] = ds
        put(hold, 0, sl, split(ds))

    each_tile(fourth)
    send_cross_back(1)
    advance(["a0", "a1"])
    acc_dkvc[...] = jnp.zeros_like(acc_dkvc)
    pair_loop(0, 0, ["a0", "a1"])
    reduce_pair("b0", 0, 0)
    advance(["b0"])
    for at in range(3, 6):
        finish_in(1, at, g_att, at * d)
    for a in range(2):
        finish_out(1, a, g_att, (6 + a) * d)
    finish_in(1, 0, g_att, 0)
    cross_keys_back(1)
    finish_in(1, 1, g_att, d)
    finish_in(1, 2, g_att, 2 * d)
    att_stores = [
        storing(f_att.at[1, pl.ds(0, 6 * d)], in_to.at[1]),
        storing(f_att.at[1, pl.ds(6 * d, 2 * d)], out_proj_to.at[1]),
    ]
    reduce("c", 2 * layers, g_att, f_att.at[1], lambda: [move() for move in att_stores])
    advance(["c", "a1", "a0"])
    pair_loop(0, 1, ["a0", "b0", "c"], later=True)
    advance(["a1"])

    def fifth(sl):
        ds = gates_back(0, stream[:, sl], dy_ref[:, sl], sl)
        stream[:, sl] = ds
        self_read_back(0, ds, sl)

    each_tile(fifth)
    send_self_back(0)
    advance(["b0"])

    each_tile(lambda sl: self_out_later(0, sl))
    for e in range(2, experts):
        each_tile(lambda sl: expert_later(e, sl), WIDE_TILE)
    reduce_pair("b1", 0, 1)
    advance(["b1", "c"])
    self_total_back(0)
    advance(["b0", "b1", "a1"])

    def sixth(sl):
        stream[:, sl] = attention_back(0, stream[:, sl], sl, True)

    each_tile(sixth)
    advance(["c"])

    def sixth_cross(sl):
        dy_ref[:, sl] = cross_read_back(0, stream[:, sl], sl, True)

    each_tile(sixth_cross)
    send_cross_back(0)
    advance(["b0"])

    each_tile(weights_later, WIDE_TILE)
    for at in range(3, 6):
        finish_in(0, at, g_early, (at - 2) * d)
    for a in range(2):
        finish_out(0, a, g_early, (4 + a) * d)
    advance(["b1", "c"])

    def seventh(sl):
        fgrad[0, sl, :] = cross_query_back(0, stream[:, sl], dy_ref[:, sl], sl).T

    each_tile(seventh)
    store(fgrad, fgrad_to)
    finish_in(0, 0, g_early, 0)
    g_small[...] = jnp.zeros_like(g_small)
    for at in range(layers * 3):
        g_small[at : at + 1, :] = jnp.sum(acc_g[at].T, axis=0, keepdims=True)
    for l in range(layers):
        at = 8 * (l + 1)
        g_small[at : at + 8, :] = acc_r[l]

    early = f_early if summed else g_early
    early_stores = [
        storing(early.at[pl.ds(0, d)], in_to.at[0, pl.ds(0, d)]),
        storing(early.at[pl.ds(d, 3 * d)], in_to.at[0, pl.ds(3 * d, 3 * d)]),
        storing(early.at[pl.ds(4 * d, 2 * d)], out_proj_to.at[0]),
    ]
    reduce_quick("d", 1, g_early, f_early, lambda: [move() for move in early_stores])
    if summed:
        begin("s", exchange_small(g_small, f_small, *ring[-3:]))
    advance(["d", "s", "b0", "b1"])
    cross_keys_back(0)
    finish_in(0, 1, g_keys, 0)
    finish_in(0, 2, g_keys, d)
    keys = pl.ds(d, 2 * d)
    reduce_quick(
        "e", 0, g_keys, f_att.at[0, keys], storing(f_att.at[0, keys], in_to.at[0, keys])
    )
    while any(steps for group in sums.values() for steps in group):
        advance(["e", "s", "d", "b1", "c", "b0", "a1", "a0"])
    small = f_small if summed else g_small
    for l in range(layers):
        for j in range(3):
            f_gain[j, l : l + 1, :] = small[l * 3 + j : l * 3 + j + 1, :]
    routed = jnp.sum(small[...].T, axis=0, keepdims=True)
    for l in range(layers):
        for c in range(2):
            at = 8 * (l + 1) + c * experts
            f_router[l, c : c + 1, :] = routed[:, at : at + experts]
    store(f_gain, gain_to)
    store(f_router, router_to)
    if not summed:
        for store_of_sum in sums_stores:
            store_of_sum()
    for copy in stores:
        copy().wait()


def finish_kernel(n, *refs):
    sources, targets, held, sems = refs[:n], refs[n : 2 * n], refs[2 * n : 3 * n], refs[3 * n]
    inward = [pltpu.make_async_copy(sources[at], held[at], sems.at[0, at]) for at in range(n)]
    outward = [pltpu.make_async_copy(held[at], targets[at], sems.at[1, at]) for at in range(n)]
    for move in inward:
        move.start()
    for at in range(n):
        inward[at].wait()
        outward[at].start()
    for move in outward:
        move.wait()


def on_device(
    n_dp,
    n_blk,
    features,
    func_points,
    coords,
    presence,
    valid_rows,
    norm_gain,
    in_proj,
    out_proj,
    router,
    expert_up,
    expert_down,
    cotangent,
):
    layers, experts, d, hid = expert_up.shape
    pairs = layers * 2
    summed = n_dp % 2 == 0 and n_blk % 2 == 0 and (2 * d) % (8 * n_dp * n_blk) == 0
    count = features.shape[1]
    funcs, points = func_points.shape[1], func_points.shape[2]
    wide_hid = experts * hid
    shape = jax.ShapeDtypeStruct
    vmem = pl.BlockSpec(memory_space=pltpu.VMEM)
    smem = pl.BlockSpec(memory_space=pltpu.SMEM)
    far = pl.BlockSpec(memory_space=pl.ANY)
    pair = pltpu.VMEM((layers, 2 * d, count), BF16)
    up_shape, down_shape, pair_shape = (2 * d, hid), (2 * hid, d), (4 * hid, d)

    def local(dims):
        return pltpu.VMEM(dims if summed else (8, 128), F32)

    cross_rows = -(-funcs * (HEAD_DIM + 1) // 8) * 8
    scratch = [
        pltpu.SemaphoreType.DMA((7 + hid // 128,)),
        pltpu.SemaphoreType.DMA((10 + pairs * (1 + 2 * hid // 128),)),
        pltpu.VMEM(features.shape, F32),
        pltpu.VMEM(features.shape, F32),
        pltpu.VMEM((layers, 8 * d, d), F32),
        pltpu.VMEM((pairs,) + pair_shape, F32),
        pltpu.VMEM((3, layers, d), F32),
        pltpu.VMEM(router.shape, F32),
        local((8 * d, d)),
        local((pairs,) + pair_shape),
        pltpu.VMEM((6 * d, d), F32),
        local((6 * d, d)),
        local((2 * d, d)),
        pltpu.VMEM((32, 128), F32),
        local((32, 128)),
        pltpu.VMEM((layers, 6 * d, 3 * d), BF16),
        pltpu.VMEM((layers, d, 3 * d), BF16),
        pltpu.VMEM((layers, d, 6 * d), BF16),
        pltpu.VMEM((layers, 2, d, 3 * d), BF16),
        pltpu.VMEM((layers, 2, d, 3 * d), BF16),
        pltpu.VMEM((layers, wide_hid, 3 * d), BF16),
        pltpu.VMEM((layers, d, 2 * wide_hid), BF16),
        pltpu.VMEM((layers, d, 2 * wide_hid), BF16),
        pltpu.VMEM((layers, wide_hid, 3 * d), BF16),
        pltpu.VMEM((layers * 3, d, 128), F32),
        pltpu.VMEM((funcs, 2 * d, points), BF16),
        pltpu.VMEM((layers * funcs, 2 * d, points), BF16),
        pltpu.VMEM((layers * funcs, 2 * d, points), BF16),
        pltpu.VMEM((d, count), F32),
        pltpu.VMEM((layers * 3, 2 * d, count), BF16),
        pltpu.VMEM((layers * 3, 8, count), F32),
        pair,
        pair,
        pair,
        pair,
        pair,
        pair,
        pltpu.VMEM((1, 2 * d, count), BF16),
        pltpu.VMEM((layers, funcs * HEADS, count), F32),
        pltpu.VMEM((layers, HEADS, count), F32),
        pltpu.VMEM((layers, experts, count), F32),
        pltpu.VMEM((layers, funcs + 1, d, 3 * d), BF16),
        pltpu.VMEM((layers, funcs + 1, d, 3 * d), BF16),
        pltpu.VMEM((layers, funcs + 1, d, 128), F32),
        pltpu.VMEM((funcs, d, 3 * d), BF16),
        pltpu.VMEM((funcs, d, 3 * d), BF16),
        pltpu.VMEM((funcs, d, 128), F32),
        pltpu.VMEM((d + HEADS, d), F32),
        pltpu.VMEM((funcs * (d + HEADS), d), F32),
        pltpu.VMEM((layers, 6 * d, d), F32),
        pltpu.VMEM((layers, 2, d, d), F32),
        pltpu.VMEM((layers * 3, d, 128), F32),
        pltpu.VMEM((layers, 2 * experts, 128), F32),
        pltpu.VMEM((d, count), F32),
        pltpu.VMEM((experts, count), F32),
        pltpu.VMEM((2 * layers, cross_rows, d), F32),
        pltpu.VMEM((2 * layers, n_blk - 1, cross_rows, d), F32),
        pltpu.VMEM((2 * layers, MSG, d), F32),
        pltpu.VMEM((2 * layers, n_blk - 1, MSG, d), F32),
    ] + [pltpu.SemaphoreType.DMA((2 * layers, n_blk - 1))] * 4
    if summed:
        n_flat, n_line = n_dp, n_blk // 2
        moves = 2 + 2 * (n_flat - 1) + 2 * (n_line - 1)
        blocks = [pair_shape] * pairs + [(8 * d, d)]
        for high, width in blocks:
            scratch += [
                pltpu.VMEM((high // 2, width), F32),
                pltpu.VMEM((n_flat - 1, high // 2 // n_flat, width), F32),
                pltpu.VMEM((n_line - 1, high // 2 // n_flat // n_line, width), F32),
                pltpu.SemaphoreType.DMA((moves,)),
                pltpu.SemaphoreType.DMA((moves,)),
            ]
        group = 2 * n_flat
        some = 2 * (group - 1) + n_line - 1
        for high in (2 * d, 6 * d):
            scratch += [
                pltpu.VMEM((group - 1, high // group, d), F32),
                pltpu.VMEM((n_line, high // group, d), F32),
                pltpu.SemaphoreType.DMA((some,)),
                pltpu.SemaphoreType.DMA((some,)),
            ]
        few = n_flat + n_line - 1
        scratch += [
            pltpu.VMEM((2 + n_flat + n_line, 32, 128), F32),
            pltpu.SemaphoreType.DMA((few,)),
            pltpu.SemaphoreType.DMA((few,)),
        ]
    results = pl.pallas_call(
        functools.partial(device_kernel, n_dp, n_blk, summed),
        out_shape=[
            shape(features.shape, F32),
            shape(features.shape, F32),
            shape((layers, 6 * d, d), F32),
            shape((layers, 2 * d, d), F32),
            shape((pairs,) + up_shape, F32),
            shape((pairs,) + down_shape, F32),
            shape((3, layers, d), F32),
            shape(router.shape, F32),
        ],
        in_specs=[far, far, vmem, smem, smem, vmem, far, far, smem, far, far, far],
        out_specs=[far] * 8,
        scratch_shapes=scratch,
        compiler_params=pltpu.CompilerParams(
            collective_id=0, has_side_effects=True, vmem_limit_bytes=VMEM_BYTES
        ),
        name="gnot",
    )(
        features,
        func_points.reshape(funcs * points, d),
        coords,
        presence,
        valid_rows.transpose(1, 0, 2),
        norm_gain.transpose(1, 0, 2),
        in_proj.reshape(layers, 6 * d, d),
        out_proj.reshape(layers, 2 * d, d),
        router,
        expert_up.reshape((pairs,) + up_shape),
        expert_down.reshape((pairs,) + down_shape),
        cotangent,
    )
    if not summed:
        results = list(results[:2]) + list(lax.psum(list(results[2:]), ("dp", "blk")))
    results = pl.pallas_call(
        functools.partial(finish_kernel, len(results)),
        out_shape=[shape(x.shape, F32) for x in results],
        in_specs=[far] * len(results),
        out_specs=[far] * len(results),
        scratch_shapes=[pltpu.VMEM(x.shape, F32) for x in results]
        + [pltpu.SemaphoreType.DMA((2, len(results)))],
        compiler_params=pltpu.CompilerParams(vmem_limit_bytes=62 * 2**20),
        name="finish",
    )(*results)
    y, dx, in_g, out_g, up_g, down_g, gain_g, route_g = results
    return (
        y,
        dx,
        gain_g.transpose(1, 0, 2),
        in_g.reshape(in_proj.shape),
        out_g.reshape(out_proj.shape),
        route_g,
        up_g.reshape(expert_up.shape),
        down_g.reshape(expert_down.shape),
    )


def solution(mesh):
    placed = (
        P("dp", "blk", None),
        P("dp", None, "blk", None),
        P("dp", None, "blk"),
        P("dp", None),
        P("dp", None, None),
        P(),
        P(),
        P(),
        P(),
        P(),
        P(),
        P("dp", "blk", None),
    )
    return jax.shard_map(
        functools.partial(on_device, mesh.shape["dp"], mesh.shape["blk"]),
        mesh=mesh,
        in_specs=placed,
        out_specs=(P("dp", "blk", None), P("dp", "blk", None), P(), P(), P(), P(), P(), P()),
        check_vma=False,
    )
```

```python
import functools
import math

import jax
import jax.numpy as jnp
from jax import lax
from jax.experimental import pallas as pl
from jax.experimental.pallas import tpu as pltpu
from jax.sharding import PartitionSpec as P

MESH = pl.DeviceIdType.MESH
F32 = jnp.float32
BF16 = jnp.bfloat16
HEADS = 8
HEAD_DIM = 16
EPS = 1e-05
C1 = math.sqrt(2.0 / math.pi)
C2 = C1 * 0.044715
TILE = 2048
WIDE_TILE = 1024
VMEM_BYTES = 66500000
UNROLL = 2
SPAN = 512
MSG = 24


def nn(a, b):
    return jnp.dot(a, b, preferred_element_type=F32)


def nt(a, b):
    return lax.dot_general(a, b, (((1,), (1,)), ((), ())), preferred_element_type=F32)


def tn(a, b):
    return lax.dot_general(a, b, (((0,), (0,)), ((), ())), preferred_element_type=F32)


def split(x):
    high = x.astype(BF16)
    return high, (x - high.astype(F32)).astype(BF16)


def rows(*parts):
    return jnp.concatenate(parts, axis=0)


def cols(*parts):
    return jnp.concatenate(parts, axis=1)


def triple(w):
    high, low = split(w)
    return cols(high, low, high)


def k3(w3, x):
    high, low = x
    return nn(w3, rows(high, high, low))


def d3(w_high, w_low, x):
    high, low = x
    return nn(w_high, high) + (nn(w_low, high) + nn(w_high, low))


def outer(a, b):
    m, n = a[0].shape[0], b[0].shape[0]
    r = nt(rows(*a), rows(*b))
    return r[:m, :n] + (r[:m, n:] + r[m:, :n])


def wide(column, t):
    return cols(*([column] * (t // 128)))


def lanes(x):
    total = x[:, :128]
    for at in range(128, x.shape[1], 128):
        total = total + x[:, at : at + 128]
    return total


def by_head(x):
    return x.reshape(HEAD_DIM, HEADS, x.shape[-1])


def head_sum(x):
    return jnp.sum(by_head(x), axis=0)


def spread(r):
    return jnp.broadcast_to(r[None], (HEAD_DIM,) + r.shape).reshape(HEAD_DIM * HEADS, r.shape[-1])


def head_softmax(z):
    z = by_head(z)
    e = jnp.exp(z - jnp.max(z, axis=0)[None])
    p = e * (1.0 / jnp.sum(e, axis=0))[None]
    return p.reshape(HEAD_DIM * HEADS, p.shape[-1])


def softmax_back(p, dp):
    return p * (dp - spread(head_sum(p * dp)))


def mean(x):
    return jnp.sum(x, axis=0, keepdims=True) * (1.0 / x.shape[0])


def layer_norm(s, gain):
    centred = s - mean(s)
    r = lax.rsqrt(mean(centred * centred) + EPS)
    return centred * r * gain, r


def norm_back(dy, y, r, gain, inv_gain):
    xhat = y * inv_gain
    v = gain * dy
    return r * (v - mean(v) - xhat * mean(v * xhat)), dy * xhat


def put(ref, at, sl, x):
    d = x[0].shape[0]
    ref[at, 0:d, sl] = x[0]
    ref[at, d : 2 * d, sl] = x[1]


def get(ref, at, sl):
    both = ref[at, :, sl]
    d = both.shape[0] // 2
    return both[:d], both[d:]


def whole(x):
    return x[0].astype(F32) + x[1].astype(F32)


def gelu_parts(v):
    v2 = v * v
    g = 0.5 + 0.5 * jnp.tanh(v * (C1 + C2 * v2))
    return v2, g


def device_kernel(
    n_dp,
    n_blk,
    summed,
    features_hbm,
    points_hbm,
    coords,
    presence,
    valid,
    gain,
    in_hbm,
    out_hbm,
    router,
    up_hbm,
    down_hbm,
    cot_hbm,
    out_to,
    fgrad_to,
    in_to,
    out_proj_to,
    up_to,
    down_to,
    gain_to,
    router_to,
    load_sem,
    store_sem,
    out,
    fgrad,
    f_att,
    f_pair,
    f_gain,
    f_router,
    g_att,
    g_pair,
    g_early,
    f_early,
    g_keys,
    g_small,
    f_small,
    w_in,
    w_qc,
    w_self,
    w_out,
    w_outb,
    up_t,
    up_n,
    down_t,
    down_n,
    gcol,
    fp,
    kc,
    vc,
    stream,
    y_ref,
    r_ref,
    qc,
    mixc,
    qs,
    ks,
    vs,
    mixs,
    hold,
    rdens_ref,
    rden_ref,
    gates,
    kv_t,
    kv_n,
    z_col,
    dkv_t,
    dkv_n,
    dz_col,
    acc_kv,
    acc_dkvc,
    acc_wi,
    acc_wo,
    acc_g,
    acc_r,
    dy_ref,
    dgate_ref,
    src_c,
    got_c,
    src_s,
    got_s,
    send_c,
    recv_c,
    send_s,
    recv_s,
    *ring,
):
    if not summed:
        g_att, g_pair, g_keys = f_att.at[1], f_pair, f_att.at[0, pl.ds(128, 256)]
    layers, experts, hid = router.shape[0], router.shape[2], up_hbm.shape[2]
    funcs = presence.shape[1]
    points = points_hbm.shape[0] // funcs
    count, d = features_hbm.shape[1:]

    def load(src, dst, at):
        copy = pltpu.make_async_copy(src, dst, load_sem.at[at])
        copy.start()
        return copy

    stores, sums_stores = [], []

    def storing(src, dst):
        at = len(stores)
        stores.append(lambda: pltpu.make_async_copy(src, dst, store_sem.at[at]))
        return lambda: stores[at]().start()

    def store(src, dst):
        storing(src, dst)()

    in_load = load(in_hbm, f_att.at[:, pl.ds(0, 6 * d)], 0)
    out_load = load(out_hbm, f_att.at[:, pl.ds(6 * d, 2 * d)], 1)
    first_load = 2
    packed = fgrad.at[0, pl.ds(0, funcs * points)]
    points_load = load(points_hbm, packed, first_load)
    features_load = load(features_hbm, out, first_load + 1)
    halves = hid // 128
    up_loads = [
        load(
            up_hbm.at[:, :, pl.ds(h * 128, 128)],
            f_pair.at[:, pl.ds(h * 2 * d, 2 * d)],
            first_load + 5 + h,
        )
        for h in range(halves)
    ]
    down_load = load(down_hbm, f_pair.at[:, pl.ds(2 * hid, 2 * hid)], first_load + 3)
    me = lax.axis_index("blk")
    own_dp = lax.axis_index("dp")
    n_flat, n_line = n_dp, n_blk // 2
    core, line = own_dp % 2, me // 2
    flat = (own_dp // 2) * 2 + me % 2

    sibling = {"dp": own_dp - core + (1 - core), "blk": me}

    def flat_at(j):
        at = lax.rem(flat + j, n_flat)
        return {"dp": (at // 2) * 2 + core, "blk": line * 2 + at % 2}

    def line_at(j):
        return {"dp": own_dp, "blk": lax.rem(line + j, n_line) * 2 + me % 2}

    def group_at(j):
        at = lax.rem(flat * 2 + core + j, 2 * n_flat)
        spot = at // 2
        return {"dp": (spot // 2) * 2 + at % 2, "blk": line * 2 + spot % 2}

    partners = [{"dp": own_dp, "blk": lax.rem(me + j, n_blk)} for j in range(1, n_blk)]
    if summed:
        partners += [group_at(j) for j in range(1, 2 * n_flat)]
    barrier = pltpu.get_barrier_semaphore()
    for partner in partners:
        pl.semaphore_signal(barrier, inc=1, device_id=partner, device_id_type=MESH)

    sums = {}

    def take(names):
        now = [steps.pop(0) for name in names for steps in sums.get(name, ()) if steps]

        def run():
            for step in now:
                step()

        return run

    def advance(names):
        take(names)()

    def made(jobs, send, recv):
        return [
            pltpu.make_async_remote_copy(
                src_ref=src,
                dst_ref=dst,
                send_sem=send.at[k],
                recv_sem=recv.at[k],
                device_id=device,
                device_id_type=MESH,
            )
            for k, src, dst, device in jobs()
        ]

    def go(jobs, send, recv):
        for copy in made(jobs, send, recv):
            copy.start()

    def settle(jobs, send, recv):
        for copy in made(jobs, send, recv):
            copy.wait()

    def reduction(local, final, halves, parts, pieces, send, recv, after):
        half = local.shape[0] // 2
        part = half // n_flat
        piece = part // n_line

        def at(start, size):
            return pl.ds(pl.multiple_of(start, 8), size)

        def of_core(other=0):
            return at((core if not other else 1 - core) * half, half)

        def of_flat(j=0):
            return at(core * half + lax.rem(flat + j, n_flat) * part, part)

        def of_line(j=0):
            return at(core * half + flat * part + lax.rem(line + j, n_line) * piece, piece)

        k1 = 1
        k2 = k1 + n_flat - 1
        k3_ = k2 + n_line - 1
        k4 = k3_ + n_line - 1
        k5 = k4 + n_flat - 1

        def core_out():
            return [(0, local.at[of_core(1)], halves, sibling)]

        def flat_out():
            return [
                (k1 + j - 1, local.at[of_flat(j)], parts.at[j - 1], flat_at(j))
                for j in range(1, n_flat)
            ]

        def line_out():
            return [
                (k2 + j - 1, local.at[of_line(j)], pieces.at[j - 1], line_at(j))
                for j in range(1, n_line)
            ]

        def line_back():
            mine = final.at[of_line()]
            return [(k3_ + j - 1, mine, mine, line_at(j)) for j in range(1, n_line)]

        def flat_back():
            mine = final.at[of_flat()]
            return [(k4 + j - 1, mine, mine, flat_at(j)) for j in range(1, n_flat)]

        def core_back():
            mine = final.at[of_core()]
            return [(k5, mine, mine, sibling)]

        def one():
            go(core_out, send, recv)

        def two():
            settle(core_out, send, recv)
            spot = of_core()
            local[spot] = local[spot] + halves[...]
            go(flat_out, send, recv)

        def three():
            settle(flat_out, send, recv)
            spot = of_flat()
            total = local[spot]
            for j in range(n_flat - 1):
                total = total + parts[j]
            local[spot] = total
            go(line_out, send, recv)

        def four():
            settle(line_out, send, recv)
            spot = of_line()
            total = local[spot]
            for j in range(n_line - 1):
                total = total + pieces[j]
            final[spot] = total
            go(line_back, send, recv)

        def five():
            settle(line_back, send, recv)
            go(flat_back, send, recv)

        def six():
            settle(flat_back, send, recv)
            go(core_back, send, recv)

        def seven():
            settle(core_back, send, recv)
            after()

        return [one, two, three, four, five, six, seven]

    def quick(local, final, parts, held, send, recv, after):
        group = 2 * n_flat
        size = local.shape[0] // group
        place = flat * 2 + core

        def piece(j):
            return pl.ds(pl.multiple_of(lax.rem(place + j, group) * size, 8), size)

        def out_jobs():
            return [
                (j - 1, local.at[piece(j)], parts.at[j - 1], group_at(j)) for j in range(1, group)
            ]

        def line_jobs():
            mine = held.at[line]
            return [(group + j - 2, mine, mine, line_at(j)) for j in range(1, n_line)]

        def back_jobs():
            mine = final.at[piece(0)]
            return [(group + n_line + j - 3, mine, mine, group_at(j)) for j in range(1, group)]

        def one():
            go(out_jobs, send, recv)

        def two():
            settle(out_jobs, send, recv)
            total = local[piece(0)]
            for j in range(group - 1):
                total = total + parts[j]
            held[line] = total
            go(line_jobs, send, recv)

        def three():
            settle(line_jobs, send, recv)
            total = held[0]
            for j in range(1, n_line):
                total = total + held[j]
            final[piece(0)] = total
            go(back_jobs, send, recv)

        def four():
            settle(back_jobs, send, recv)
            after()

        return [one, two, three, four]

    def exchange_small(local, final, held, send, recv):
        levels = (
            (0, 2, core, lambda: [sibling], 0),
            (2, n_flat, flat, lambda: [flat_at(j) for j in range(1, n_flat)], 1),
            (2 + n_flat, n_line, line, lambda: [line_at(j) for j in range(1, n_line)], n_flat),
        )

        def jobs_of(level):
            at, _, place, devices, k = levels[level]

            def jobs():
                mine = held.at[at + place]
                return [(k + j, mine, mine, device) for j, device in enumerate(devices())]

            return jobs

        def start(level, value):
            at, _, place, _, _ = levels[level]
            held[at + place] = value
            go(jobs_of(level), send, recv)

        def finish(level):
            settle(jobs_of(level), send, recv)
            at, size = levels[level][:2]
            value = held[at]
            for j in range(1, size):
                value = value + held[at + j]
            return value

        def last():
            final[...] = finish(2)

        return [
            lambda: start(0, local[...]),
            lambda: start(1, finish(0)),
            lambda: start(2, finish(1)),
            last,
        ]

    def begin(name, steps):
        if summed:
            sums.setdefault(name, []).append(steps)

    def reduce(name, seg, local, final, after):
        sums_stores.append(after)
        if summed:
            begin(name, reduction(local, final, *ring[5 * seg : 5 * seg + 5], after))

    def reduce_quick(name, at, local, final, after):
        sums_stores.append(after)
        if summed:
            start = 5 * (2 * layers + 1) + 4 * at
            begin(name, quick(local, final, *ring[start : start + 4], after))

    def reduce_pair(name, l, pair):
        seg = l * 2 + pair
        moves = [storing(f_pair.at[seg, pl.ds(2 * hid, 2 * hid)], down_to.at[seg])]
        for at in range(2 * halves):
            e, h = at // halves, at % halves
            moves.append(
                storing(
                    g_pair.at[seg, pl.ds(at * 128, 128)],
                    up_to.at[seg, pl.ds(e * d, d), pl.ds(h * 128, 128)],
                )
            )

        def after():
            for at in range(2 * halves):
                spot = slice(at * 128, (at + 1) * 128)
                g_pair[seg, spot, :] = f_pair[seg, spot, :].T
            for move in moves:
                move()

        reduce(name, seg, g_pair.at[seg], f_pair.at[seg], after)

    def copies(src, got, send, recv, at):
        return [
            pltpu.make_async_remote_copy(
                src_ref=src.at[at],
                dst_ref=got.at[at, j - 1],
                send_sem=send.at[at, j - 1],
                recv_sem=recv.at[at, j - 1],
                device_id={"blk": lax.rem(me + j, n_blk)},
                device_id_type=MESH,
            )
            for j in range(1, n_blk)
        ]

    def send_off(refs, at):
        for copy in copies(*refs, at):
            copy.start()

    def collect(refs, at):
        for copy in copies(*refs, at):
            copy.wait()
        src, got = refs[0], refs[1]
        total = src[at]
        for j in range(n_blk - 1):
            total = total + got[at, j]
        return total

    cross = (src_c, got_c, send_c, recv_c)
    own = (src_s, got_s, send_s, recv_s)

    head_mask = (
        lax.broadcasted_iota(jnp.int32, (HEADS, d), 0)
        == lax.broadcasted_iota(jnp.int32, (HEADS, d), 1) % HEADS
    ).astype(F32)
    spot = lax.broadcasted_iota(jnp.int32, (d, d), 0)
    perm = (
        lax.broadcasted_iota(jnp.int32, (d, d), 1) == (spot % HEADS) * HEAD_DIM + spot // HEADS
    ).astype(F32)
    perm16 = perm.astype(BF16)

    def compact(full):
        return jnp.sum(full.reshape(HEAD_DIM, HEADS, d) * head_mask[None], axis=1)

    def expand(compacted):
        full = jnp.broadcast_to(compacted[:, None, :], (HEAD_DIM, HEADS, d)) * head_mask[None]
        return full.reshape(d, d)

    def unpack(total, t_ref, n_ref, c_ref, at):
        full = expand(total[0])
        t_ref[at] = triple(full)
        n_ref[at] = triple(full.T)
        c_ref[at] = jnp.broadcast_to(total[1], (d, d)).T

    def cross_kv(f):
        return slice(f * HEAD_DIM, (f + 1) * HEAD_DIM)

    def cross_key(f):
        return slice(funcs * HEAD_DIM + f, funcs * HEAD_DIM + f + 1)

    def cut_attention(l, a):
        for j in range(3):
            at = a * 3 + j
            w_high, w_low = split(f_att[l, at * d : (at + 1) * d, :])
            high = nt(perm16, w_high).astype(BF16)
            low = nt(perm16, w_low).astype(BF16)
            w_in[l, at * d : (at + 1) * d, :] = cols(high, low, high)
            if (a, j) == (0, 0) or a == 1:
                high = nt(w_high, perm16).astype(BF16)
                low = nt(w_low, perm16).astype(BF16)
                if a == 0:
                    w_qc[l] = cols(high, low, high)
                else:
                    w_self[l, :, j * d : (j + 1) * d] = high
                    w_self[l, :, (3 + j) * d : (4 + j) * d] = low

    def cut_out(l, a):
        w_high, w_low = split(f_att[l, (6 + a) * d : (7 + a) * d, :])
        contract = (((0,), (1,)), ((), ()))
        high, low = [
            lax.dot_general(w, perm16, contract, preferred_element_type=F32).astype(BF16)
            for w in (w_high, w_low)
        ]
        w_out[l, a] = cols(high, low, high)
        high = nn(perm16, w_high).astype(BF16)
        low = nn(perm16, w_low).astype(BF16)
        w_outb[l, a] = cols(high, low, high)

    def cut_experts(l):
        for e in range(experts):
            lo, hi = e * hid, (e + 1) * hid
            seg, spot = l * 2 + e // 2, e % 2
            w = cols(
                *[f_pair[seg, (2 * h + spot) * d : (2 * h + spot + 1) * d, :] for h in range(halves)]
            )
            high, low = split(w)
            up_n[l, :, lo:hi] = high
            up_n[l, :, experts * hid + lo : experts * hid + hi] = low
            up_t[l, lo:hi, :] = triple(w.T)
            w = f_pair[seg, (2 + spot) * hid : (3 + spot) * hid, :]
            down_n[l, lo:hi, :] = triple(w)
            high, low = split(w.T)
            down_t[l, :, lo:hi] = high
            down_t[l, :, experts * hid + lo : experts * hid + hi] = low

    def cut_gains(l):
        for j in range(3):
            column = jnp.broadcast_to(gain[j, l : l + 1, :], (d, d)).T
            gcol[l * 3 + j] = column

    present = [presence[0, f].astype(F32) for f in range(funcs)]
    all_present = present[0]
    for f in range(1, funcs):
        all_present = all_present + present[f]
    weight = [
        jnp.full((1, 1), present[f], F32) / jnp.full((1, 1), all_present, F32) for f in range(funcs)
    ]

    ones = jnp.ones((16, points), BF16)

    def cross_summary(l):
        for f in range(funcs):
            both = fp[f]
            z = k3(w_in[l, d : 3 * d, :], (both[:d], both[d:]))
            kept = (
                lax.broadcasted_iota(jnp.int32, (1, points), 1) < valid[f, 0, me]
            ).astype(F32)
            k = split(head_softmax(z[:d]) * kept)
            v = split(z[d:])
            put(kc, l * funcs + f, slice(None), k)
            put(vc, l * funcs + f, slice(None), v)
            r = nt(rows(*v, ones), rows(*k))
            src_c[l, cross_kv(f), :] = compact(r[:d, :d] + (r[:d, d:] + r[d : 2 * d, :d]))
            src_c[l, cross_key(f), :] = r[2 * d : 2 * d + 1, :d] + r[2 * d : 2 * d + 1, d:]
        send_off(cross, l)

    def cross_total(l):
        total = collect(cross, l)
        for f in range(funcs):
            unpack((total[cross_kv(f)], total[cross_key(f)]), kv_t.at[l], kv_n.at[l], z_col.at[l], f)

    def own_parts(total):
        return total[:HEAD_DIM], total[HEAD_DIM : HEAD_DIM + 1]

    def self_total(l):
        unpack(own_parts(collect(own, l)), kv_t.at[l], kv_n.at[l], z_col.at[l], funcs)

    def norm_in(l, at, s, sl):
        y, r = layer_norm(s, wide(gcol[l * 3 + at], sl.size))
        y = split(y)
        put(y_ref, l * 3 + at, sl, y)
        r_ref[l * 3 + at, 0:1, sl] = r
        return y

    def norm_out(l, at, dy, sl):
        y = whole(get(y_ref, l * 3 + at, sl))
        ds, dg = norm_back(
            dy,
            y,
            r_ref[l * 3 + at, 0:1, sl],
            wide(gcol[l * 3 + at], sl.size),
            wide(1.0 / gcol[l * 3 + at], sl.size),
        )
        acc_g[l * 3 + at] += lanes(dg)
        return ds

    def cross_query(l, s, sl):
        y = norm_in(l, 0, s, sl)
        put(qc, l, sl, split(head_softmax(k3(w_in[l, :d, :], y))))

    def cross_read(l, s, sl):
        q2 = get(qc, l, sl)
        q = whole(q2)
        num = k3(kv_t[l, :funcs].reshape(funcs * d, 3 * d), q2)
        mix = q
        for f in range(funcs):
            rden = 1.0 / head_sum(q * wide(z_col[l, f], sl.size))
            rdens_ref[l, f * 8 : (f + 1) * 8, sl] = rden
            mix = mix + num[f * d : (f + 1) * d] * spread(rden * weight[f])
        mix = split(mix)
        put(mixc, l, sl, mix)
        s = s + k3(w_out[l, 0], mix)
        y = norm_in(l, 1, s, sl)
        z = k3(w_in[l, 3 * d :, :], y)
        q = split(head_softmax(z[:d]))
        k = split(head_softmax(z[d : 2 * d]))
        v = split(z[2 * d :])
        put(qs, l, sl, q)
        put(ks, l, sl, k)
        put(vs, l, sl, v)
        r = nt(rows(*v, jnp.ones((16, sl.size), BF16)), rows(*k))
        acc_kv[:d, :] += r[:d, :d] + (r[:d, d:] + r[d : 2 * d, :d])
        acc_kv[d:, :] += r[2 * d : 2 * d + 8, :d] + r[2 * d : 2 * d + 8, d:]
        stream[:, sl] = s

    def send_self(l):
        src_s[l, :HEAD_DIM, :] = compact(acc_kv[:d, :])
        src_s[l, HEAD_DIM:, :] = acc_kv[d:, :]
        send_off(own, l)

    def self_read(l, s, sl):
        q2 = get(qs, l, sl)
        q = whole(q2)
        num = k3(kv_t[l, funcs], q2)
        rden = 1.0 / head_sum(q * wide(z_col[l, funcs], sl.size))
        rden_ref[l, :, sl] = rden
        mix = split(num * spread(rden) + q)
        put(mixs, l, sl, mix)
        s = s + k3(w_out[l, 1], mix)
        return s, norm_in(l, 2, s, sl)

    def hidden_in(l, e, y):
        return k3(up_t[l, e * hid : (e + 1) * hid, :], y)

    def down_of(l, e, x):
        at = experts * hid
        return d3(
            down_t[l, :, e * hid : (e + 1) * hid],
            down_t[l, :, at + e * hid : at + (e + 1) * hid],
            x,
        )

    def run_experts(l, y, sl):
        total = None
        for e in range(experts):
            v = hidden_in(l, e, y)
            _, g = gelu_parts(v)
            part = down_of(l, e, split(v * g * gates[l, e : e + 1, sl]))
            total = part if total is None else total + part
        return total

    def weights_of(l, e, gated, dpre, y, ds2):
        seg, place = l * 2 + e // 2, e % 2
        g_pair[seg, (2 + place) * hid : (3 + place) * hid, :] += outer(gated, ds2)
        g_pair[seg, place * hid : (place + 1) * hid, :] += outer(dpre, y)

    dzq = [(mixs, 1), (hold, 0)]
    spare = [(y_ref, 3), (y_ref, 4), (y_ref, 5)] + [
        (ref, 1) for ref in (qc, mixc, qs, ks, vs)
    ]

    def expert_later(e, sl):
        gated, dpre = [
            [ref[at, :, sl] for ref, at in spare[4 * (e % 2) + k : 4 * (e % 2) + k + 2]]
            for k in (0, 2)
        ]
        weights_of(0, e, gated, dpre, get(y_ref, 2, sl), get(hold, 0, sl))

    def expert_back(l, pair, y, ds2, sl, later):
        at = experts * hid
        step = min(SPAN, sl.size)
        units = [(e, k) for e in (2 * pair, 2 * pair + 1) for k in range(0, sl.size, step)]

        def products(e, k):
            part = [(x[0][:, k : k + step], x[1][:, k : k + step]) for x in (y, ds2)]
            return hidden_in(l, e, part[0]), k3(down_n[l, e * hid : (e + 1) * hid, :], part[1])

        ready = products(*units[0])
        held = []
        for now, (e, k) in enumerate(units):
            v, back = ready
            if now + 1 < len(units):
                ready = products(*units[now + 1])
            spot = pl.ds(pl.multiple_of(sl.start + k, 128), step)
            gate = 0.5 * gates[l, e : e + 1, spot]
            v2 = v * v
            inner = v * (C1 + C2 * v2)
            twice = 1.0 + jnp.tanh(inner)
            act = v * twice
            slope = twice * (1.0 + (2.0 - twice) * (v * (C1 + 3.0 * C2 * v2)))
            dgate_ref[e : e + 1, spot] = 0.5 * jnp.sum(act * back, axis=0, keepdims=True)
            held.append(split(act * gate) + split(slope * back * gate))
            if k + step < sl.size:
                continue
            joined = [cols(*parts) for parts in zip(*held)]
            gated, dpre = joined[:2], joined[2:]
            held = []
            if later:
                for k, x in enumerate(joined):
                    ref, slot = spare[4 * (e % 2) + k]
                    ref[slot, :, sl] = x
            else:
                weights_of(l, e, gated, dpre, y, ds2)
            dy = d3(
                up_n[l, :, e * hid : (e + 1) * hid],
                up_n[l, :, at + e * hid : at + (e + 1) * hid],
                dpre,
            )
            yield e, gated, dy

    def gates_back(l, ds, dy, sl):
        probs = [gates[l, e : e + 1, sl] for e in range(experts)]
        dgate = [dgate_ref[e : e + 1, sl] for e in range(experts)]
        centre = probs[0] * dgate[0]
        for e in range(1, experts):
            centre = centre + probs[e] * dgate[e]
        dlogit = rows(*[probs[e] * (dgate[e] - centre) for e in range(experts)])
        place = coords[0, :, sl]
        acc_r[l] += lanes(rows(dlogit * place[0:1], dlogit * place[1:2]))
        return ds + norm_out(l, 2, dy, sl)

    def experts_back(l, pair, sl, forward, later):
        ds2 = get(hold, 0, sl)
        y = get(y_ref, l * 3 + 2, sl)
        total, dy = None, None
        for e, gated, part in expert_back(l, pair, y, ds2, sl, later):
            dy = part if dy is None else dy + part
            if forward:
                part = down_of(l, e, gated)
                total = part if total is None else total + part
        dy_ref[:, sl] = dy if pair == 0 else dy_ref[:, sl] + dy
        if forward:
            stream[:, sl] += total

    def self_read_back(l, ds, sl):
        ds2 = split(ds)
        dmix = k3(w_outb[l, 1], ds2)
        back = k3(kv_n[l, funcs], split(dmix))
        q2 = get(qs, l, sl)
        q = whole(q2)
        rden = rden_ref[l, :, sl]
        u = rden * (rden * head_sum(q * back))
        dq = dmix + spread(rden) * back - wide(z_col[l, funcs], sl.size) * spread(u)
        put(*dzq[l], sl, split(softmax_back(q, dq)))
        da = split(dmix * spread(rden))
        u2 = split(u)
        r = nt(rows(*da, *u2), rows(*q2))
        acc_kv[:d, :] += r[:d, :d] + (r[:d, d:] + r[d : 2 * d, :d])
        low = r[2 * d :, :d] + r[2 * d :, d:]
        acc_kv[d:, :] += low[:8] + low[8:]

    def self_out_later(l, sl):
        acc_wo[l, 1] += outer(get(mixs, l, sl), split(stream[:, sl]))

    def back_row(x):
        return jnp.broadcast_to(-jnp.sum(x * head_mask, axis=0, keepdims=True), (HEADS, d))

    def send_self_back(l):
        at = layers + l
        src_s[at, :HEAD_DIM, :] = compact(acc_kv[:d, :])
        src_s[at, HEAD_DIM:, :] = back_row(acc_kv[d:, :])
        send_off(own, at)

    def self_total_back(l):
        unpack(own_parts(collect(own, layers + l)), dkv_t, dkv_n, dz_col, 0)

    def attention_back(l, ds, sl, later=False):
        k2, v2 = get(ks, l, sl), get(vs, l, sl)
        dk = k3(dkv_n[0], v2) + wide(dz_col[0], sl.size)
        dv = split(k3(dkv_t[0], k2))
        dzk = split(softmax_back(whole(k2), dk))
        q2 = get(*dzq[l], sl)
        dz = (rows(q2[0], dzk[0], dv[0]), rows(q2[1], dzk[1], dv[1]))
        if later:
            put(qs, 1, sl, dzk)
            put(ks, 1, sl, dv)
        else:
            acc_wi[l, 3 * d :, :] += outer(dz, get(y_ref, l * 3 + 1, sl))
        dy = d3(w_self[l, :, : 3 * d], w_self[l, :, 3 * d :], dz)
        return ds + norm_out(l, 1, dy, sl)

    def weights_later(sl):
        parts = (get(*dzq[0], sl), get(qs, 1, sl), get(ks, 1, sl))
        dz = (rows(*[part[0] for part in parts]), rows(*[part[1] for part in parts]))
        acc_wi[0, 3 * d :, :] += outer(dz, get(y_ref, 1, sl))
        acc_wo[0, 0] += outer(get(mixc, 0, sl), get(vs, 1, sl))

    def cross_read_back(l, ds, sl, later=False):
        ds2 = split(ds)
        dmix = k3(w_outb[l, 0], ds2)
        if later:
            put(vs, 1, sl, ds2)
        else:
            acc_wo[l, 0] += outer(get(mixc, l, sl), ds2)
        back = k3(kv_n[l, :funcs].reshape(funcs * d, 3 * d), split(dmix))
        q2 = get(qc, l, sl)
        q = whole(q2)
        dq = dmix
        da, us = [], []
        for f in range(funcs):
            rden = rdens_ref[l, f * 8 : (f + 1) * 8, sl]
            inv = rden * weight[f]
            back_f = back[f * d : (f + 1) * d]
            u = inv * (rden * head_sum(q * back_f))
            dq = dq + spread(inv) * back_f - wide(z_col[l, f], sl.size) * spread(u)
            da.append(dmix * spread(inv))
            us.append(u)
        if funcs % 2:
            us.append(jnp.zeros_like(us[0]))
        side = rows(*us)
        m = funcs * d
        r = nt(rows(*split(rows(*da)), *split(side)), rows(*q2))
        acc_dkvc[:m, :] += r[:m, :d] + (r[:m, d:] + r[m : 2 * m, :d])
        low = r[2 * m :, :d] + r[2 * m :, d:]
        high = side.shape[0]
        acc_dkvc[m:, :] += (low[:high] + low[high:])[: 8 * funcs]
        return softmax_back(q, dq)

    def cross_query_back(l, ds, dz, sl):
        dz2 = split(dz)
        acc_wi[l, :d, :] += outer(dz2, get(y_ref, l * 3, sl))
        return ds + norm_out(l, 0, k3(w_qc[l], dz2), sl)

    def send_cross_back(l):
        at = layers + l
        for f in range(funcs):
            src_c[at, cross_kv(f), :] = compact(acc_dkvc[f * d : (f + 1) * d, :])
            src_c[at, cross_key(f), :] = back_row(
                acc_dkvc[funcs * d + f * 8 : funcs * d + (f + 1) * 8, :]
            )[:1]
        send_off(cross, at)

    def cross_keys_back(l):
        total = collect(cross, layers + l)
        for f in range(funcs):
            unpack((total[cross_kv(f)], total[cross_key(f)]), dkv_t, dkv_n, dz_col, f)
        for f in range(funcs):
            k2 = get(kc, l * funcs + f, slice(None))
            v2 = get(vc, l * funcs + f, slice(None))
            dk = k3(dkv_n[f], v2) + wide(dz_col[f], points)
            dv = split(k3(dkv_t[f], k2))
            dzk = split(softmax_back(whole(k2), dk))
            both = fp[f]
            part = outer(
                (rows(dzk[0], dv[0]), rows(dzk[1], dv[1])), (both[:d], both[d:])
            )
            if f == 0:
                acc_wi[l, d : 3 * d, :] = part
            else:
                acc_wi[l, d : 3 * d, :] += part

    def each_tile(body, tile=TILE, then=(), in_line=False):
        tile = min(tile, count)
        move = take(then)
        if count // tile == 1 or (in_line and count // tile <= UNROLL):
            for at in range(0, count, tile):
                if at + tile == count:
                    move()
                body(pl.ds(at, tile))
            return

        def step(i, carry):
            if then:
                pl.when(i == count // tile - 1)(move)
            body(pl.ds(pl.multiple_of(i * tile, tile), tile))
            return carry

        lax.fori_loop(0, count // tile, step, 0)

    exact = functools.partial(
        lax.dot_general, precision=lax.Precision.HIGHEST, preferred_element_type=F32
    )

    def finish_in(l, at, ref, spot):
        ref[spot : spot + d, :] = exact(
            acc_wi[l, at * d : (at + 1) * d, :], perm, (((0,), (0,)), ((), ()))
        )

    def finish_out(l, a, ref, spot):
        ref[spot : spot + d, :] = exact(perm, acc_wo[l, a], (((0,), (0,)), ((), ())))

    in_load.wait()
    points_load.wait()
    for f in range(funcs):
        high, low = split(fgrad[0, f * points : (f + 1) * points, :].T)
        fp[f, :d, :] = high
        fp[f, d:, :] = low
    cot_load = load(cot_hbm, fgrad, first_load + 4)
    for ref in (src_c, src_s):
        ref[...] = jnp.zeros_like(ref)
    cut_attention(0, 0)
    pl.semaphore_wait(barrier, len(partners))
    cross_summary(0)

    out_load.wait()
    features_load.wait()
    cut_gains(0)

    def first(sl):
        s = out[0, sl, :].T
        stream[:, sl] = s
        cross_query(0, s, sl)

    each_tile(first)
    cut_attention(0, 1)
    cut_out(0, 0)
    cut_out(0, 1)
    acc_kv[...] = jnp.zeros_like(acc_kv)
    cross_total(0)
    each_tile(lambda sl: cross_read(0, stream[:, sl], sl))
    send_self(0)

    cut_attention(1, 0)
    cross_summary(1)
    for copy in up_loads + [down_load]:
        copy.wait()
    cut_experts(0)

    def route(sl):
        place = coords[0, :, sl]
        for l in range(layers):
            logit = [
                place[0:1] * router[l, 0, e] + place[1:2] * router[l, 1, e] for e in range(experts)
            ]
            top = functools.reduce(jnp.maximum, logit)
            grown = [jnp.exp(x - top) for x in logit]
            total = functools.reduce(jnp.add, grown)
            for e in range(experts):
                gates[l, e : e + 1, sl] = grown[e] / total

    route(pl.ds(0, count))
    acc_kv[...] = jnp.zeros_like(acc_kv)
    self_total(0)

    def second(sl):
        s, y = self_read(0, stream[:, sl], sl)
        stream[:, sl] = s + run_experts(0, y, sl)

    each_tile(second, WIDE_TILE, in_line=True)
    cut_gains(1)
    cut_attention(1, 1)
    cut_out(1, 0)
    cross_total(1)

    def second_cross(sl):
        s = stream[:, sl]
        cross_query(1, s, sl)
        cross_read(1, s, sl)

    each_tile(second_cross)
    send_self(1)

    cut_out(1, 1)
    cut_experts(1)
    cot_load.wait()

    def turn(sl):
        put(hold, 0, sl, split(fgrad[0, sl, :].T))

    each_tile(turn)
    for ref in (acc_wi, acc_wo, acc_g, acc_r, g_pair, acc_kv, acc_dkvc):
        ref[...] = jnp.zeros_like(ref)
    self_total(1)

    def third(sl):
        stream[:, sl] = self_read(1, stream[:, sl], sl)[0]

    each_tile(third)

    def pair_loop(l, pair, between=(), later=False):
        each_tile(
            lambda sl: experts_back(l, pair, sl, l == layers - 1, later), WIDE_TILE, between
        )

    pair_loop(1, 0)
    reduce_pair("a0", 1, 0)
    advance(["a0"])
    pair_loop(1, 1, ["a0"])
    reduce_pair("a1", 1, 1)
    advance(["a1"])

    def third_back(sl):
        ds = gates_back(1, whole(get(hold, 0, sl)), dy_ref[:, sl], sl)
        self_read_back(1, ds, sl)
        dy_ref[:, sl] = stream[:, sl]
        stream[:, sl] = ds

    each_tile(third_back)
    send_self_back(1)

    def third_later(sl):
        out[0, sl, :] = dy_ref[:, sl].T
        self_out_later(1, sl)

    each_tile(third_later)
    store(out, out_to)
    advance(["a0"])
    acc_kv[...] = jnp.zeros_like(acc_kv)
    self_total_back(1)
    advance(["a1"])

    def fourth(sl):
        ds = attention_back(1, stream[:, sl], sl)
        dz = cross_read_back(1, ds, sl)
        ds = cross_query_back(1, ds, dz, sl)
        stream[:, sl] = ds
        put(hold, 0, sl, split(ds))

    each_tile(fourth)
    send_cross_back(1)
    advance(["a0", "a1"])
    acc_dkvc[...] = jnp.zeros_like(acc_dkvc)
    pair_loop(0, 0, ["a0", "a1"])
    reduce_pair("b0", 0, 0)
    advance(["b0"])
    for at in range(3, 6):
        finish_in(1, at, g_att, at * d)
    for a in range(2):
        finish_out(1, a, g_att, (6 + a) * d)
    finish_in(1, 0, g_att, 0)
    cross_keys_back(1)
    finish_in(1, 1, g_att, d)
    finish_in(1, 2, g_att, 2 * d)
    att_stores = [
        storing(f_att.at[1, pl.ds(0, 6 * d)], in_to.at[1]),
        storing(f_att.at[1, pl.ds(6 * d, 2 * d)], out_proj_to.at[1]),
    ]
    reduce("c", 2 * layers, g_att, f_att.at[1], lambda: [move() for move in att_stores])
    advance(["c", "a1", "a0"])
    pair_loop(0, 1, ["a0", "b0", "c"], later=True)
    advance(["a1"])

    def fifth(sl):
        ds = gates_back(0, stream[:, sl], dy_ref[:, sl], sl)
        stream[:, sl] = ds
        self_read_back(0, ds, sl)

    each_tile(fifth)
    send_self_back(0)
    advance(["b0"])

    each_tile(lambda sl: self_out_later(0, sl))
    for e in range(2, experts):
        each_tile(lambda sl: expert_later(e, sl), WIDE_TILE)
    reduce_pair("b1", 0, 1)
    advance(["b1", "c"])
    self_total_back(0)
    advance(["b0", "b1", "a1"])

    def sixth(sl):
        stream[:, sl] = attention_back(0, stream[:, sl], sl, True)

    each_tile(sixth)
    advance(["c"])

    def sixth_cross(sl):
        dy_ref[:, sl] = cross_read_back(0, stream[:, sl], sl, True)

    each_tile(sixth_cross)
    send_cross_back(0)
    advance(["b0"])

    each_tile(weights_later, WIDE_TILE)
    for at in range(3, 6):
        finish_in(0, at, g_early, (at - 2) * d)
    for a in range(2):
        finish_out(0, a, g_early, (4 + a) * d)
    advance(["b1", "c"])

    def seventh(sl):
        fgrad[0, sl, :] = cross_query_back(0, stream[:, sl], dy_ref[:, sl], sl).T

    each_tile(seventh)
    store(fgrad, fgrad_to)
    finish_in(0, 0, g_early, 0)
    g_small[...] = jnp.zeros_like(g_small)
    for at in range(layers * 3):
        g_small[at : at + 1, :] = jnp.sum(acc_g[at].T, axis=0, keepdims=True)
    for l in range(layers):
        at = 8 * (l + 1)
        g_small[at : at + 8, :] = acc_r[l]

    early = f_early if summed else g_early
    early_stores = [
        storing(early.at[pl.ds(0, d)], in_to.at[0, pl.ds(0, d)]),
        storing(early.at[pl.ds(d, 3 * d)], in_to.at[0, pl.ds(3 * d, 3 * d)]),
        storing(early.at[pl.ds(4 * d, 2 * d)], out_proj_to.at[0]),
    ]
    reduce_quick("d", 1, g_early, f_early, lambda: [move() for move in early_stores])
    if summed:
        begin("s", exchange_small(g_small, f_small, *ring[-3:]))
    advance(["d", "s", "b0", "b1"])
    cross_keys_back(0)
    finish_in(0, 1, g_keys, 0)
    finish_in(0, 2, g_keys, d)
    keys = pl.ds(d, 2 * d)
    reduce_quick(
        "e", 0, g_keys, f_att.at[0, keys], storing(f_att.at[0, keys], in_to.at[0, keys])
    )
    while any(steps for group in sums.values() for steps in group):
        advance(["e", "s", "d", "b1", "c", "b0", "a1", "a0"])
    small = f_small if summed else g_small
    for l in range(layers):
        for j in range(3):
            f_gain[j, l : l + 1, :] = small[l * 3 + j : l * 3 + j + 1, :]
    routed = jnp.sum(small[...].T, axis=0, keepdims=True)
    for l in range(layers):
        for c in range(2):
            at = 8 * (l + 1) + c * experts
            f_router[l, c : c + 1, :] = routed[:, at : at + experts]
    store(f_gain, gain_to)
    store(f_router, router_to)
    if not summed:
        for store_of_sum in sums_stores:
            store_of_sum()
    for copy in stores:
        copy().wait()


def finish_kernel(n, *refs):
    sources, targets, held, sems = refs[:n], refs[n : 2 * n], refs[2 * n : 3 * n], refs[3 * n]
    inward = [pltpu.make_async_copy(sources[at], held[at], sems.at[0, at]) for at in range(n)]
    outward = [pltpu.make_async_copy(held[at], targets[at], sems.at[1, at]) for at in range(n)]
    for move in inward:
        move.start()
    for at in range(n):
        inward[at].wait()
        outward[at].start()
    for move in outward:
        move.wait()


def on_device(
    n_dp,
    n_blk,
    features,
    func_points,
    coords,
    presence,
    valid_rows,
    norm_gain,
    in_proj,
    out_proj,
    router,
    expert_up,
    expert_down,
    cotangent,
):
    layers, experts, d, hid = expert_up.shape
    pairs = layers * 2
    summed = n_dp % 2 == 0 and n_blk % 2 == 0 and (2 * d) % (8 * n_dp * n_blk) == 0
    count = features.shape[1]
    funcs, points = func_points.shape[1], func_points.shape[2]
    wide_hid = experts * hid
    shape = jax.ShapeDtypeStruct
    vmem = pl.BlockSpec(memory_space=pltpu.VMEM)
    smem = pl.BlockSpec(memory_space=pltpu.SMEM)
    far = pl.BlockSpec(memory_space=pl.ANY)
    pair = pltpu.VMEM((layers, 2 * d, count), BF16)
    up_shape, down_shape, pair_shape = (2 * d, hid), (2 * hid, d), (4 * hid, d)

    def local(dims):
        return pltpu.VMEM(dims if summed else (8, 128), F32)

    cross_rows = -(-funcs * (HEAD_DIM + 1) // 8) * 8
    scratch = [
        pltpu.SemaphoreType.DMA((7 + hid // 128,)),
        pltpu.SemaphoreType.DMA((10 + pairs * (1 + 2 * hid // 128),)),
        pltpu.VMEM(features.shape, F32),
        pltpu.VMEM(features.shape, F32),
        pltpu.VMEM((layers, 8 * d, d), F32),
        pltpu.VMEM((pairs,) + pair_shape, F32),
        pltpu.VMEM((3, layers, d), F32),
        pltpu.VMEM(router.shape, F32),
        local((8 * d, d)),
        local((pairs,) + pair_shape),
        pltpu.VMEM((6 * d, d), F32),
        local((6 * d, d)),
        local((2 * d, d)),
        pltpu.VMEM((32, 128), F32),
        local((32, 128)),
        pltpu.VMEM((layers, 6 * d, 3 * d), BF16),
        pltpu.VMEM((layers, d, 3 * d), BF16),
        pltpu.VMEM((layers, d, 6 * d), BF16),
        pltpu.VMEM((layers, 2, d, 3 * d), BF16),
        pltpu.VMEM((layers, 2, d, 3 * d), BF16),
        pltpu.VMEM((layers, wide_hid, 3 * d), BF16),
        pltpu.VMEM((layers, d, 2 * wide_hid), BF16),
        pltpu.VMEM((layers, d, 2 * wide_hid), BF16),
        pltpu.VMEM((layers, wide_hid, 3 * d), BF16),
        pltpu.VMEM((layers * 3, d, 128), F32),
        pltpu.VMEM((funcs, 2 * d, points), BF16),
        pltpu.VMEM((layers * funcs, 2 * d, points), BF16),
        pltpu.VMEM((layers * funcs, 2 * d, points), BF16),
        pltpu.VMEM((d, count), F32),
        pltpu.VMEM((layers * 3, 2 * d, count), BF16),
        pltpu.VMEM((layers * 3, 8, count), F32),
        pair,
        pair,
        pair,
        pair,
        pair,
        pair,
        pltpu.VMEM((1, 2 * d, count), BF16),
        pltpu.VMEM((layers, funcs * HEADS, count), F32),
        pltpu.VMEM((layers, HEADS, count), F32),
        pltpu.VMEM((layers, experts, count), F32),
        pltpu.VMEM((layers, funcs + 1, d, 3 * d), BF16),
        pltpu.VMEM((layers, funcs + 1, d, 3 * d), BF16),
        pltpu.VMEM((layers, funcs + 1, d, 128), F32),
        pltpu.VMEM((funcs, d, 3 * d), BF16),
        pltpu.VMEM((funcs, d, 3 * d), BF16),
        pltpu.VMEM((funcs, d, 128), F32),
        pltpu.VMEM((d + HEADS, d), F32),
        pltpu.VMEM((funcs * (d + HEADS), d), F32),
        pltpu.VMEM((layers, 6 * d, d), F32),
        pltpu.VMEM((layers, 2, d, d), F32),
        pltpu.VMEM((layers * 3, d, 128), F32),
        pltpu.VMEM((layers, 2 * experts, 128), F32),
        pltpu.VMEM((d, count), F32),
        pltpu.VMEM((experts, count), F32),
        pltpu.VMEM((2 * layers, cross_rows, d), F32),
        pltpu.VMEM((2 * layers, n_blk - 1, cross_rows, d), F32),
        pltpu.VMEM((2 * layers, MSG, d), F32),
        pltpu.VMEM((2 * layers, n_blk - 1, MSG, d), F32),
    ] + [pltpu.SemaphoreType.DMA((2 * layers, n_blk - 1))] * 4
    if summed:
        n_flat, n_line = n_dp, n_blk // 2
        moves = 2 + 2 * (n_flat - 1) + 2 * (n_line - 1)
        blocks = [pair_shape] * pairs + [(8 * d, d)]
        for high, width in blocks:
            scratch += [
                pltpu.VMEM((high // 2, width), F32),
                pltpu.VMEM((n_flat - 1, high // 2 // n_flat, width), F32),
                pltpu.VMEM((n_line - 1, high // 2 // n_flat // n_line, width), F32),
                pltpu.SemaphoreType.DMA((moves,)),
                pltpu.SemaphoreType.DMA((moves,)),
            ]
        group = 2 * n_flat
        some = 2 * (group - 1) + n_line - 1
        for high in (2 * d, 6 * d):
            scratch += [
                pltpu.VMEM((group - 1, high // group, d), F32),
                pltpu.VMEM((n_line, high // group, d), F32),
                pltpu.SemaphoreType.DMA((some,)),
                pltpu.SemaphoreType.DMA((some,)),
            ]
        few = n_flat + n_line - 1
        scratch += [
            pltpu.VMEM((2 + n_flat + n_line, 32, 128), F32),
            pltpu.SemaphoreType.DMA((few,)),
            pltpu.SemaphoreType.DMA((few,)),
        ]
    results = pl.pallas_call(
        functools.partial(device_kernel, n_dp, n_blk, summed),
        out_shape=[
            shape(features.shape, F32),
            shape(features.shape, F32),
            shape((layers, 6 * d, d), F32),
            shape((layers, 2 * d, d), F32),
            shape((pairs,) + up_shape, F32),
            shape((pairs,) + down_shape, F32),
            shape((3, layers, d), F32),
            shape(router.shape, F32),
        ],
        in_specs=[far, far, vmem, smem, smem, vmem, far, far, smem, far, far, far],
        out_specs=[far] * 8,
        scratch_shapes=scratch,
        compiler_params=pltpu.CompilerParams(
            collective_id=0, has_side_effects=True, vmem_limit_bytes=VMEM_BYTES
        ),
        name="gnot",
    )(
        features,
        func_points.reshape(funcs * points, d),
        coords,
        presence,
        valid_rows.transpose(1, 0, 2),
        norm_gain.transpose(1, 0, 2),
        in_proj.reshape(layers, 6 * d, d),
        out_proj.reshape(layers, 2 * d, d),
        router,
        expert_up.reshape((pairs,) + up_shape),
        expert_down.reshape((pairs,) + down_shape),
        cotangent,
    )
    if not summed:
        results = list(results[:2]) + list(lax.psum(list(results[2:]), ("dp", "blk")))
    results = pl.pallas_call(
        functools.partial(finish_kernel, len(results)),
        out_shape=[shape(x.shape, F32) for x in results],
        in_specs=[far] * len(results),
        out_specs=[far] * len(results),
        scratch_shapes=[pltpu.VMEM(x.shape, F32) for x in results]
        + [pltpu.SemaphoreType.DMA((2, len(results)))],
        compiler_params=pltpu.CompilerParams(vmem_limit_bytes=62 * 2**20),
        name="finish",
    )(*results)
    y, dx, in_g, out_g, up_g, down_g, gain_g, route_g = results
    return (
        y,
        dx,
        gain_g.transpose(1, 0, 2),
        in_g.reshape(in_proj.shape),
        out_g.reshape(out_proj.shape),
        route_g,
        up_g.reshape(expert_up.shape),
        down_g.reshape(expert_down.shape),
    )


def solution(mesh):
    placed = (
        P("dp", "blk", None),
        P("dp", None, "blk", None),
        P("dp", None, "blk"),
        P("dp", None),
        P("dp", None, None),
        P(),
        P(),
        P(),
        P(),
        P(),
        P(),
        P("dp", "blk", None),
    )
    return jax.shard_map(
        functools.partial(on_device, mesh.shape["dp"], mesh.shape["blk"]),
        mesh=mesh,
        in_specs=placed,
        out_specs=(P("dp", "blk", None), P("dp", "blk", None), P(), P(), P(), P(), P(), P()),
        check_vma=False,
    )
```
